32 devices in a mesh: seq: 16 (over z, y, x), dp: 2 (over core).
Axes of the slice: x: 2, y: 2, z: 4, core: 2. Of those that a mesh axis runs over, the one named last changes fastest.
Arguments:
- tokens: bfloat16 [2, 4096, 1472], P('dp', 'seq'), may hold values from -6 to 6
- cotangent: bfloat16 [2, 4096, 1472], P('dp', 'seq'), may hold values from -6 to 6
- item_lengths: int32 [2, 8], P('dp'), may hold values from 1 to 4, 16 in all within a row
- gain_attn: float32 [1472], replicated, may hold values from 0.1 to 1.9
- gain_ffn: float32 [1472], replicated, may hold values from 0.1 to 1.9
- rel_table: float32 [32, 6], replicated, may hold values from -4 to 4
- w_query: bfloat16 [1472, 384], replicated, may hold values from -0.0546875 to 0.0546875
- w_keyval: bfloat16 [1472, 768], replicated, may hold values from -0.15625 to 0.15625
- w_out: bfloat16 [384, 1472], replicated, may hold values from -1.25 to 1.25
- w_gateup: bfloat16 [1472, 7168], replicated, may hold values from -0.15625 to 0.15625
- w_down: bfloat16 [3584, 1472], replicated, may hold values from -0.09375 to 0.09375
Outputs:
- output: bfloat16 [2, 4096, 1472], P('dp', 'seq')
- input_grad: bfloat16 [2, 4096, 1472], P('dp', 'seq')
- gain_attn_grad: float32 [1472], replicated
- gain_ffn_grad: float32 [1472], replicated
- table_grad: float32 [32, 6], replicated
- query_grad: float32 [1472, 384], P('dp', 'seq')
- keyval_grad: float32 [1472, 768], P('dp', 'seq')
- out_grad: float32 [384, 1472], P('seq', 'dp')
- gateup_grad: float32 [1472, 7168], P('dp', 'seq')
- down_grad: float32 [3584, 1472], P('seq', 'dp')
The draws below stay inside these ranges and needn't reach their ends.
Inputs may be any that keep to these rules, and one draw needn't show every extreme that they name: `item_lengths`: each group's items fill its 16 blocks end to end; the longest has exactly 4 blocks.
All inputs are finite; a program needn't handle non-finite values.
Results may differ from the reference program's by a relative error of at most 0.015.
The reference program's roundings to bfloat16 on the way count: a program that leaves them out, or rounds other values in their place, can miss the bound.
Values may be sent and summed in bfloat16 or wider, within the bound.
No kernel may reach another device: no remote copies, remote signals or barrier semaphores. Data moves between devices by JAX's collectives and lax.ppermute only.
A program may use at most 256 MiB of HBM per device.

```python
import math
import jax
import jax.numpy as jnp
import numpy as np
from jax import lax

D = 1472
H = 6
DH = 64
FF = 3584
BUCKETS = 32
ITEM_MOST = 4
TOK_DEV = 256
INNER = 384
SEQ_TOK = 4096
ITEMS = 8
N_SEQ = 16
N_DP = 2


def levels(stream_key, dims, cuts, smallest, largest):
    loudness = 1.0
    for position, parts in cuts:
        draws = jax.random.uniform(jax.random.fold_in(jax.random.fold_in(stream_key, 6), position), (parts,), jnp.float32, smallest / len(cuts), largest / len(cuts))
        loudness = loudness * jnp.repeat(jnp.exp(draws), dims[position] // parts).reshape((-1,) + (1,) * (len(dims) - 1 - position))
    return loudness


def length_profile(number_of, total, limit, lean):
    portions = [(1 << 20) // math.isqrt(standing ** lean) + 1 for standing in range(2, number_of + 1)]
    surplus, holding = total - limit - (number_of - 1), [1] * (number_of - 1)
    while surplus > 0:
        candidates = [i for i in range(number_of - 1) if holding[i] < limit]
        whole, budget = sum([portions[i] for i in candidates]), surplus
        for i in candidates:
            extra = min(limit - holding[i], max(1, budget * portions[i] // whole), surplus)
            holding[i] = holding[i] + extra
            surplus = surplus - extra
    return np.array([limit] + holding)


def uneven(stream_key, count, total, limit, slope):
    if count == 2:
        one = jax.random.randint(stream_key, (), max(1, total - limit), min(limit, total - 1) + 1)
        return jnp.stack([one, total - one])
    sizes = jnp.asarray(length_profile(count, total, limit, slope), jnp.int32)
    couples = (count - 1) // 2
    giver, taker = sizes[1:1 + 2 * couples:2], sizes[2:2 + 2 * couples:2]
    room = jnp.minimum(giver - 1, limit - taker)
    shifted = jax.random.randint(jax.random.fold_in(stream_key, 1), (couples,), 0, 1 << 20) % (room + 1)
    sizes = sizes.at[1:1 + 2 * couples:2].set(giver - shifted).at[2:2 + 2 * couples:2].set(taker + shifted)
    return sizes[jax.random.permutation(jax.random.fold_in(stream_key, 2), count)]


def gaussian(rng, extent, deviation, bound, shards=(), kind=jnp.bfloat16):
    array = jax.random.normal(rng, extent, jnp.float32) * deviation
    if len(shards) > 0:
        array = levels(rng, extent, shards, -0.22, 0.18) * array
    return jnp.clip(array, min=-bound, max=bound).astype(kind)


def setup_inputs(seed: int = 0) -> dict:
    seeds = jax.random.split(jax.random.key(seed), 12)
    tokens = gaussian(seeds[0], (N_DP, SEQ_TOK, D), 1.0, 6.0, ((0, 2), (1, 16)))
    cotangent = gaussian(seeds[1], (N_DP, SEQ_TOK, D), 1.0, 6.0, ((0, 2), (1, 16)))
    item_lengths = jax.vmap(lambda own: uneven(own, ITEMS, N_SEQ, ITEM_MOST, 1))(jax.random.split(seeds[2], N_DP)).reshape((N_DP, ITEMS)).astype(jnp.int32)
    gain_attn = jnp.clip(1.0 + 0.18 * jax.random.normal(seeds[3], (D,), jnp.float32), 0.1, 1.9)
    gain_ffn = jnp.clip(1.0 + 0.18 * jax.random.normal(seeds[4], (D,), jnp.float32), 0.1, 1.9)
    rel_table = gaussian(seeds[5], (BUCKETS, H), 1.0, 4.0, (), jnp.float32)
    w_query = gaussian(seeds[6], (D, INNER), (8 * D) ** -0.5, 0.0546875)
    w_keyval = gaussian(seeds[7], (D, 2 * INNER), D ** -0.5, 0.15625)
    w_out = gaussian(seeds[8], (INNER, D), (INNER // 16) ** -0.5, 1.25)
    w_gateup = gaussian(seeds[9], (D, 2 * FF), D ** -0.5, 0.15625)
    w_down = gaussian(seeds[10], (FF, D), FF ** -0.5, 0.09375)
    return {"tokens": tokens, "cotangent": cotangent, "item_lengths": item_lengths, "gain_attn": gain_attn, "gain_ffn": gain_ffn, "rel_table": rel_table, "w_query": w_query, "w_keyval": w_keyval, "w_out": w_out, "w_gateup": w_gateup, "w_down": w_down}


bucket_edges = (12, 16, 23, 32, 46, 64, 91)
negative_fill = -1e+30
highest = lax.Precision.HIGHEST

@jax.custom_vjp
def low(v):
    return lax.optimization_barrier(v.astype(jnp.bfloat16)).astype(jnp.float32)

@jax.custom_vjp
def low_back(v):
    return v

def low_keep(v):
    return (low(v), None)

def low_pass(kept, grad):
    return (grad,)

def back_keep(v):
    return (v, None)

def back_low(kept, grad):
    return (low(grad),)
low.defvjp(low_keep, low_pass)
low_back.defvjp(back_keep, back_low)

def bucket_of(relative):
    ahead = jnp.where(relative > 0, 16, 0).astype(jnp.int32)
    distance = jnp.abs(relative).astype(jnp.int32)
    beyond = 8 + sum(((distance >= edge).astype(jnp.int32) for edge in bucket_edges))
    return ahead + jnp.where(distance < 8, distance, beyond).astype(jnp.int32)

def key_layout(lengths, block_index, block_count, row_count, reach_blocks):
    ends = jnp.cumsum(lengths).astype(jnp.int32)
    offsets = jnp.arange(-reach_blocks, reach_blocks + 1, dtype=jnp.int32)
    key_blocks = (block_index + offsets).astype(jnp.int32)
    own_item = jnp.sum((ends <= block_index).astype(jnp.int32))
    key_items = lax.optimization_barrier(jnp.sum((ends[None, :] <= key_blocks[:, None]).astype(jnp.int32), axis=1))
    usable = (key_blocks >= 0) & (key_blocks < block_count) & (key_items == own_item)
    key_usable = jnp.repeat(usable, row_count)
    key_count = (2 * reach_blocks + 1) * row_count
    key_place = jnp.arange(key_count, dtype=jnp.int32) - reach_blocks * row_count
    relative = key_place[None, :] - jnp.arange(row_count, dtype=jnp.int32)[:, None]
    return (key_usable, bucket_of(relative))

def rms_scale(values):
    return lax.rsqrt(lax.optimization_barrier(jnp.mean(values * values, axis=-1, keepdims=True)) + 1e-06)

def matmul(left, right):
    return jnp.dot(left, right, precision=highest)

def layer(inputs, weights, lengths):
    gain_attn, gain_ffn, rel_table, w_query, w_keyval, w_out, w_gateup, w_down = weights
    reach_blocks = ITEM_MOST - 1
    normed_one = low(inputs * rms_scale(inputs) * gain_attn)
    query = low_back(low(matmul(normed_one, w_query)))
    keyval = low_back(low(matmul(normed_one, w_keyval)))
    padded = jnp.pad(keyval, ((reach_blocks * TOK_DEV, reach_blocks * TOK_DEV), (0, 0)))

    def block_attention(block_index):
        query_block = lax.dynamic_slice_in_dim(query, block_index * TOK_DEV, TOK_DEV, 0).reshape(TOK_DEV, H, DH)
        keys_block = lax.dynamic_slice_in_dim(padded, block_index * TOK_DEV, (2 * reach_blocks + 1) * TOK_DEV, 0)
        key_heads = keys_block[:, :INNER].reshape(-1, H, DH)
        value_heads = keys_block[:, INNER:].reshape(-1, H, DH)
        key_usable, buckets = key_layout(lengths, block_index, N_SEQ, TOK_DEV, reach_blocks)
        bias = jnp.take(rel_table.T, buckets, axis=1)
        scores = low_back(jnp.einsum('qhd,khd->hqk', query_block, key_heads, precision=highest) + bias)
        scores = jnp.where(key_usable[None, None, :], scores, negative_fill)
        probability = low(jax.nn.softmax(scores, axis=-1))
        return jnp.einsum('hqk,khd->qhd', probability, value_heads, precision=highest).reshape(TOK_DEV, INNER)
    blocks = jnp.arange(N_SEQ, dtype=jnp.int32)
    attended = lax.map(jax.checkpoint(block_attention), blocks).reshape(SEQ_TOK, INNER)
    attended = low_back(low(attended))
    middle = inputs + low_back(matmul(attended, w_out))
    normed_two = low(middle * rms_scale(middle) * gain_ffn)
    gateup = low_back(matmul(normed_two, w_gateup))
    mixed = low(jax.nn.gelu(gateup[:, :FF], approximate=True) * gateup[:, FF:])
    return middle + matmul(mixed, w_down)

def reference(tokens, cotangent, item_lengths, gain_attn, gain_ffn, rel_table, w_query, w_keyval, w_out, w_gateup, w_down):
    params = tuple((value.astype(jnp.float32) for value in (gain_attn, gain_ffn, rel_table, w_query, w_keyval, w_out, w_gateup, w_down)))

    def per_group(totals, group):
        inputs, upstream, lengths = group

        def forward(values, *weights):
            return layer(values, weights, lengths)
        result, pull = jax.vjp(forward, inputs.astype(jnp.float32), *params)
        grads = pull(upstream.astype(jnp.float32))
        totals = tuple((before + grad for before, grad in zip(totals, grads[1:])))
        return (totals, (result.astype(jnp.bfloat16), grads[0].astype(jnp.bfloat16)))
    zeros = tuple((jnp.zeros_like(value) for value in params))
    totals, (results, input_grads) = lax.scan(per_group, zeros, (tokens, cotangent, item_lengths))
    return (results, input_grads, totals[0], totals[1], totals[2], totals[3], totals[4], totals[5], totals[6], totals[7])
```

```python
import functools

import jax
import jax.numpy as jnp
from jax import lax
from jax.experimental import pallas as pl
from jax.experimental.pallas import tpu as pltpu
from jax.sharding import PartitionSpec as P

H = 6
DH = 64
BUCKETS = 32
ITEM_MOST = 4
REACH = ITEM_MOST - 1
PAIR = 2 * DH
UNITS = 256

bucket_edges = (12, 16, 23, 32, 46, 64, 91)
negative_fill = -1e30
f32 = jnp.float32
bf16 = jnp.bfloat16
VMEM_MOST = 56 * 1024 * 1024


def bucket_of(relative):
    ahead = jnp.where(relative > 0, 16, 0).astype(jnp.int32)
    distance = jnp.abs(relative)
    beyond = 8 + sum(((distance >= edge).astype(jnp.int32) for edge in bucket_edges))
    return ahead + jnp.where(distance < 8, distance, beyond)


def dot_nn(left, right):
    return lax.dot_general(left, right, (((1,), (0,)), ((), ())), preferred_element_type=f32)


def dot_nt(left, right):
    return lax.dot_general(left, right, (((1,), (1,)), ((), ())), preferred_element_type=f32)


def dot_tn(left, right):
    return lax.dot_general(left, right, (((0,), (0,)), ((), ())), preferred_element_type=f32)


def rms_scale(values):
    return lax.rsqrt(jnp.mean(values * values, axis=-1, keepdims=True) + 1e-06)


def whole(shape):
    return pl.BlockSpec(shape, lambda *_: (0,) * len(shape))


def params():
    return pltpu.CompilerParams(vmem_limit_bytes=VMEM_MOST)


def bias_kernel(place_ref, by_shift_ref, out_ref):
    rows, keys = out_ref.shape[1:]
    wide = by_shift_ref.shape[-1]
    spread = jnp.broadcast_to(by_shift_ref[0], (rows, wide))
    turned = pltpu.roll(spread, 0, 1, stride=1, stride_axis=0)[:, :keys]
    key = lax.broadcasted_iota(jnp.int32, (rows, keys), 1)
    out_ref[0] = jnp.where(key < place_ref[1] * rows, turned, negative_fill)


def window_bias(place, by_shift, rows):
    keys = ITEM_MOST * rows
    wide = by_shift.shape[-1]
    return pl.pallas_call(
        bias_kernel,
        grid_spec=pltpu.PrefetchScalarGridSpec(
            num_scalar_prefetch=1,
            grid=(H,),
            in_specs=[pl.BlockSpec((1, 1, wide), lambda h, _: (h, 0, 0))],
            out_specs=pl.BlockSpec((1, rows, keys), lambda h, _: (h, 0, 0)),
        ),
        out_shape=jax.ShapeDtypeStruct((H, rows, keys), f32),
        compiler_params=params(),
        cost_estimate=pl.CostEstimate(
            flops=H * rows * keys * 40, bytes_accessed=H * rows * keys * 4, transcendentals=0
        ),
    )(place, by_shift.reshape(H, 1, wide))


def own_lanes(shape, which):
    lane = lax.broadcasted_iota(jnp.int32, shape, len(shape) - 1)
    return (lane >= which * DH) & (lane < (which + 1) * DH)


def attend_kernel(
    place_ref, query_ref, *refs
):
    pieces = refs[: 2 * REACH + 1]
    (bias_ref, inputs_ref, w_out_ref, gain_ref,
     attended_ref, prob_ref, window_ref, middle_ref, hidden_ref) = refs[2 * REACH + 1 :]
    rows = query_ref.shape[0]
    inner = w_out_ref.shape[0]
    pair = pl.program_id(0)
    place = place_ref[0]

    @pl.when(pair == 0)
    def _():
        for b in range(ITEM_MOST):
            for offset in range(-REACH, REACH + 1):
                if 0 <= b - offset < ITEM_MOST:

                    @pl.when(place == b - offset)
                    def _():
                        window_ref[b * rows : (b + 1) * rows, :] = pieces[offset + REACH][...]

    at = pl.multiple_of(pair * PAIR, PAIR)
    key = window_ref[:, pl.ds(at, PAIR)]
    value = window_ref[:, pl.ds(pl.multiple_of(inner + pair * PAIR, PAIR), PAIR)]
    query = query_ref[...]
    total = None
    for which in range(2):
        mine = own_lanes(query.shape, which)
        scores = dot_nt(jnp.where(mine, query, jnp.zeros_like(query)), key) + bias_ref[which]
        exponent = jnp.exp(scores - jnp.max(scores, axis=-1, keepdims=True))
        prob = exponent / jnp.sum(exponent, axis=-1, keepdims=True)
        prob_ref[which] = prob
        part = dot_nn(prob.astype(bf16), value)
        total = part if total is None else jnp.where(mine, part, total)
    attended_ref[:, pl.ds(at, PAIR)] = total.astype(bf16)

    @pl.when(pair == pl.num_programs(0) - 1)
    def _():
        middle = inputs_ref[...].astype(f32) + dot_nn(attended_ref[...], w_out_ref[...])
        middle_ref[...] = middle
        hidden_ref[...] = (middle * rms_scale(middle) * gain_ref[...]).astype(bf16)


def attend(place, query, pieces, bias, inputs, w_out, gain_ffn):
    rows, inner = query.shape
    width = inputs.shape[1]
    keys = ITEM_MOST * rows
    return pl.pallas_call(
        attend_kernel,
        grid_spec=pltpu.PrefetchScalarGridSpec(
            num_scalar_prefetch=1,
            grid=(H // 2,),
            in_specs=[pl.BlockSpec((rows, PAIR), lambda h, _: (0, h))]
            + [whole((rows, 2 * inner))] * (2 * REACH + 1)
            + [
                pl.BlockSpec((2, rows, keys), lambda h, _: (h, 0, 0)),
                whole((rows, width)),
                whole((inner, width)),
                whole((1, width)),
            ],
            out_specs=[
                whole((rows, inner)),
                pl.BlockSpec((2, rows, keys), lambda h, _: (h, 0, 0)),
                whole((keys, 2 * inner)),
                whole((rows, width)),
                whole((rows, width)),
            ],
        ),
        out_shape=[
            jax.ShapeDtypeStruct((rows, inner), bf16),
            jax.ShapeDtypeStruct((H, rows, keys), f32),
            jax.ShapeDtypeStruct((keys, 2 * inner), bf16),
            jax.ShapeDtypeStruct((rows, width), f32),
            jax.ShapeDtypeStruct((rows, width), bf16),
        ],
        compiler_params=params(),
        cost_estimate=pl.CostEstimate(
            flops=H * rows * keys * PAIR * 4 + 2 * rows * inner * width,
            bytes_accessed=H * rows * keys * 8 + 6 * 2**20,
            transcendentals=H * rows * keys,
        ),
    )(place, query, *pieces, bias, inputs, w_out, gain_ffn)


GELU_A = 0.7978845608028654
GELU_B = 0.044715


def ffn_kernel(last, half_ref, *refs):
    hidden_ref, upstream_ref, gate_w_ref, up_w_ref, down_w_ref = refs[:5]
    refs = refs[5:]
    if last:
        out_in, back_in, middle_ref, gain_ref, w_out_ref = refs[:5]
        (mixed_ref, gate_back_ref, up_back_ref, output_ref, gain_grad_ref, middle_back_ref,
         branch_ref, attended_back_ref, out_ref, back_ref) = refs[5:]
    else:
        mixed_ref, gate_back_ref, up_back_ref, out_ref, back_ref = refs
    step = pl.program_id(0)
    hidden = hidden_ref[...]
    upstream = upstream_ref[...]
    gate = dot_nn(hidden, gate_w_ref[...])
    up = dot_nn(hidden, up_w_ref[...])
    mixed_back = dot_nt(upstream, down_w_ref[...])
    squared = gate * gate
    bent = jnp.tanh(GELU_A * (gate + GELU_B * (squared * gate)))
    share = 0.5 * (1.0 + bent)
    gelu = gate * share
    slope = share + 0.5 * gate * (1.0 - bent * bent) * (GELU_A * (1.0 + 3.0 * GELU_B * squared))
    mixed = (gelu * up).astype(bf16)
    gate_back = (mixed_back * up * slope).astype(bf16)
    up_back = (mixed_back * gelu).astype(bf16)
    mixed_ref[...] = mixed
    gate_back_ref[...] = gate_back
    up_back_ref[...] = up_back
    forward = dot_nn(mixed, down_w_ref[...])
    backward = dot_nt(gate_back, gate_w_ref[...]) + dot_nt(up_back, up_w_ref[...])

    @pl.when(step == 0)
    def _():
        if last:
            out_ref[...] = out_in[...] + forward
            back_ref[...] = back_in[...] + backward
        else:
            out_ref[...] = forward
            back_ref[...] = backward

    @pl.when(step > 0)
    def _():
        out_ref[...] += forward
        back_ref[...] += backward

    if last:

        @pl.when(step == pl.num_programs(0) - 1)
        def _():
            middle = middle_ref[...]
            output_ref[...] = (middle + out_ref[...]).astype(bf16)
            scale = rms_scale(middle)
            normed = middle * scale
            back = back_ref[...]
            gain_grad_ref[...] = jnp.sum(back * normed, axis=0, keepdims=True)
            normed_back = back * gain_ref[...]
            mean = jnp.mean(normed_back * normed, axis=-1, keepdims=True)
            middle_back = upstream_ref[...].astype(f32) + scale * (normed_back - normed * mean)
            middle_back_ref[...] = middle_back
            branch = middle_back.astype(bf16)
            branch_ref[...] = branch
            attended_back_ref[...] = dot_nt(branch, w_out_ref[...]).astype(bf16)


def ffn_half(last, half, hidden, upstream, w_gateup, w_down, more):
    rows, width = hidden.shape
    units = w_down.shape[0]
    steps = units // 2 // UNITS
    both = units // UNITS
    column = lambda j, s: (0, j)
    in_specs = [
        whole((rows, width)),
        whole((rows, width)),
        pl.BlockSpec((width, UNITS), lambda j, s: (0, s[0] * steps + j)),
        pl.BlockSpec((width, UNITS), lambda j, s: (0, both + s[0] * steps + j)),
        pl.BlockSpec((UNITS, width), lambda j, s: (s[0] * steps + j, 0)),
    ]
    out_specs = [pl.BlockSpec((rows, UNITS), column)] * 3
    out_shape = [jax.ShapeDtypeStruct((rows, units // 2), bf16)] * 3
    sums = [jax.ShapeDtypeStruct((rows, width), f32)] * 2
    scratch = []
    if last:
        inner = more[-1].shape[0]
        in_specs += [whole((rows, width))] * 3 + [whole((1, width)), whole((inner, width))]
        out_specs += [
            whole((rows, width)),
            whole((1, width)),
            whole((rows, width)),
            whole((rows, width)),
            whole((rows, inner)),
        ]
        out_shape += [
            jax.ShapeDtypeStruct((rows, width), bf16),
            jax.ShapeDtypeStruct((1, width), f32),
            jax.ShapeDtypeStruct((rows, width), f32),
            jax.ShapeDtypeStruct((rows, width), bf16),
            jax.ShapeDtypeStruct((rows, inner), bf16),
        ]
        scratch = [pltpu.VMEM((rows, width), f32)] * 2
    else:
        out_specs += [whole((rows, width))] * 2
        out_shape += sums
    return pl.pallas_call(
        functools.partial(ffn_kernel, last),
        grid_spec=pltpu.PrefetchScalarGridSpec(
            num_scalar_prefetch=1,
            grid=(steps,),
            in_specs=in_specs,
            out_specs=out_specs,
            scratch_shapes=scratch,
        ),
        out_shape=out_shape,
        compiler_params=params(),
        cost_estimate=pl.CostEstimate(
            flops=6 * rows * width * units,
            bytes_accessed=3 * width * units + 12 * rows * width,
            transcendentals=rows * units // 2,
        ),
    )(half, hidden, upstream, w_gateup, w_gateup, w_down, *more)


def grad_kernel(
    mine_ref, left_own, left_far, right_own, right_far, kept_ref, sent_ref, halves
):
    rows = right_own.shape[0]
    part = right_own.shape[1] // 2

    @pl.when(pl.program_id(0) == 0)
    def _():
        for index, source in enumerate((right_own, right_far)):
            at = slice(index * rows, (index + 1) * rows)
            low, high = source[:, :part], source[:, part:]

            @pl.when(mine_ref[0] == 0)
            def _():
                halves[0, at, :] = low
                halves[1, at, :] = high

            @pl.when(mine_ref[0] != 0)
            def _():
                halves[0, at, :] = high
                halves[1, at, :] = low

    left = jnp.concatenate([left_own[...], left_far[...]], 0)
    kept_ref[...] = dot_tn(left, halves[0]).astype(bf16)
    sent_ref[...] = dot_tn(left, halves[1]).astype(bf16)


def weight_grad(mine, left_own, left_far, right_own, right_far):
    rows, units = left_own.shape
    width = right_own.shape[1]
    part = width // 2
    out = jax.ShapeDtypeStruct((units, part), bf16)
    return pl.pallas_call(
        grad_kernel,
        grid_spec=pltpu.PrefetchScalarGridSpec(
            num_scalar_prefetch=1,
            grid=(units // UNITS,),
            in_specs=[pl.BlockSpec((rows, UNITS), lambda j, _: (0, j))] * 2
            + [whole((rows, width))] * 2,
            out_specs=[pl.BlockSpec((UNITS, part), lambda j, _: (j, 0))] * 2,
            scratch_shapes=[pltpu.VMEM((2, 2 * rows, part), bf16)],
        ),
        out_shape=[out, out],
        compiler_params=params(),
        cost_estimate=pl.CostEstimate(
            flops=4 * rows * units * width,
            bytes_accessed=4 * rows * (units + width) + 2 * units * width,
            transcendentals=0,
        ),
    )(mine, left_own, left_far, right_own, right_far)


def attend_back_kernel(
    place_ref, query_ref, key_ref, value_ref, prob_ref, back_ref, *refs
):
    query_back_ref, by_shift_ref = refs[:2]
    outs = refs[2 : 3 + 2 * REACH]
    key_sum, value_sum = refs[3 + 2 * REACH :]
    rows = query_ref.shape[0]
    keys = key_ref.shape[0]
    pair = pl.program_id(0)
    inner = key_sum.shape[1]
    query, key, value, back = query_ref[...], key_ref[...], value_ref[...], back_ref[...]
    nothing = jnp.zeros_like(query)
    row = lax.broadcasted_iota(jnp.int32, (rows, rows), 0)
    column = lax.broadcasted_iota(jnp.int32, (rows, rows), 1)
    flip = jnp.where(row + column == rows - 1, 1.0, 0.0).astype(bf16)
    query_back = None
    key_back = None
    for which in range(2):
        mine = own_lanes(query.shape, which)
        own_query = jnp.where(mine, query, nothing)
        own_back = jnp.where(mine, back, nothing)
        prob = prob_ref[which]
        prob_back = dot_nt(own_back, value)
        delta = jnp.sum(prob * prob_back, axis=-1, keepdims=True)
        score_back = (prob * (prob_back - delta)).astype(bf16)
        part = dot_nn(score_back, key)
        query_back = part if query_back is None else jnp.where(mine, part, query_back)
        key_part = dot_tn(own_query, score_back)
        value_part = dot_tn(own_back, prob.astype(bf16))
        key_back = key_part if key_back is None else key_back + key_part
        value_back = value_part if which == 0 else value_back + value_part
        flipped = dot_nn(flip, score_back)
        wide = jnp.concatenate([flipped, jnp.zeros((rows, rows), f32)], 1)
        turned = pltpu.roll(wide, keys + 1, 1, stride=1, stride_axis=0)
        by_shift_ref[which] = jnp.sum(turned, axis=0, keepdims=True)
    query_back_ref[...] = query_back.astype(bf16)
    at = pl.multiple_of(pair * PAIR, PAIR)
    key_sum[:, pl.ds(at, PAIR)] = key_back.T
    value_sum[:, pl.ds(at, PAIR)] = value_back.T

    @pl.when(pair == pl.num_programs(0) - 1)
    def _():
        for offset in range(-REACH, REACH + 1):
            out = outs[offset + REACH]
            place = place_ref[0]

            @pl.when((place + offset < 0) | (place + offset >= ITEM_MOST))
            def _():
                out[...] = jnp.zeros_like(out)

            for b in range(ITEM_MOST):
                if 0 <= b - offset < ITEM_MOST:

                    @pl.when(place == b - offset)
                    def _():
                        at = slice(b * rows, (b + 1) * rows)
                        out[:, :inner] = key_sum[at, :].astype(out.dtype)
                        out[:, inner:] = value_sum[at, :].astype(out.dtype)


def attend_back(place, query, window, prob, back):
    rows, inner = query.shape
    keys = window.shape[0]
    pairs = H // 2
    out_dtypes = [f32 if o == 0 else bf16 for o in range(-REACH, REACH + 1)]
    return pl.pallas_call(
        attend_back_kernel,
        grid_spec=pltpu.PrefetchScalarGridSpec(
            num_scalar_prefetch=1,
            grid=(pairs,),
            in_specs=[
                pl.BlockSpec((rows, PAIR), lambda h, _: (0, h)),
                pl.BlockSpec((keys, PAIR), lambda h, _: (0, h)),
                pl.BlockSpec((keys, PAIR), lambda h, _: (0, pairs + h)),
                pl.BlockSpec((2, rows, keys), lambda h, _: (h, 0, 0)),
                pl.BlockSpec((rows, PAIR), lambda h, _: (0, h)),
            ],
            out_specs=[
                pl.BlockSpec((rows, PAIR), lambda h, _: (0, h)),
                pl.BlockSpec((2, 1, keys + rows), lambda h, _: (h, 0, 0)),
            ]
            + [whole((rows, 2 * inner))] * (2 * REACH + 1),
            scratch_shapes=[pltpu.VMEM((keys, inner), f32)] * 2,
        ),
        out_shape=[
            jax.ShapeDtypeStruct((rows, inner), bf16),
            jax.ShapeDtypeStruct((H, 1, keys + rows), f32),
        ]
        + [jax.ShapeDtypeStruct((rows, 2 * inner), dtype) for dtype in out_dtypes],
        compiler_params=params(),
        cost_estimate=pl.CostEstimate(
            flops=H * rows * keys * PAIR * 8 + 2 * H * rows * rows * keys,
            bytes_accessed=H * rows * keys * 4 + 8 * 2**20,
            transcendentals=0,
        ),
    )(place, query, window, window, prob, back)


def swapped(value, axis, bit):
    size = lax.axis_size(axis)
    return lax.ppermute(value, axis, [(i, i ^ bit) for i in range(size)])


def passed_along(value, axis, by):
    size = lax.axis_size(axis)
    pairs = [(i, i + by) for i in range(size) if 0 <= i + by < size]
    return lax.ppermute(value, axis, pairs)


def chosen(value, dim, index):
    return lax.dynamic_index_in_dim(value, index, dim, keepdims=False)


def added(left, right):
    return (left.astype(f32) + right.astype(f32)).astype(bf16)


def halved(state, dims, bit):
    left, right = state
    dim = dims.index(bit)
    mine = (lax.axis_index("seq") // bit) % 2
    other = added(chosen(left, dim, 1 - mine), chosen(right, dim, 1 - mine))
    kept = added(chosen(left, dim, mine), chosen(right, dim, mine))
    rest = dims[:dim] + dims[dim + 1 :]
    return (kept, swapped(other, "seq", bit)), rest


def scattered(state, dims, order):
    for bit in order:
        state, dims = halved(state, dims, bit)
    return state


def on_device(
    tokens,
    cotangent,
    item_lengths,
    gain_attn,
    gain_ffn,
    rel_table,
    w_query,
    w_keyval,
    w_out,
    w_gateup,
    w_down,
):
    rows = tokens.shape[1]
    width = tokens.shape[2]
    part = width // 2
    inner = w_query.shape[1]
    blocks = lax.axis_size("seq")
    me = lax.axis_index("seq")
    core = lax.axis_index("dp")
    top, pair = blocks // 2, blocks // 4
    low = [1 << i for i in range(blocks.bit_length() - 1)][:-2]

    x = tokens[0]
    inputs = x.astype(f32)
    upstream = cotangent[0]
    scale_one = rms_scale(inputs)
    hidden_one = (inputs * scale_one * gain_attn).astype(bf16)
    keyval = dot_nn(hidden_one, w_keyval).astype(bf16)
    pieces = [
        keyval if o == 0 else passed_along(keyval, "seq", -o) for o in range(-REACH, REACH + 1)
    ]
    query = dot_nn(hidden_one, w_query).astype(bf16)
    upstream_far = swapped(upstream, "seq", pair)

    ends = jnp.cumsum(item_lengths[0])
    own = jnp.sum((ends <= me).astype(jnp.int32))
    labels = jnp.arange(item_lengths.shape[1], dtype=jnp.int32)
    length = jnp.sum(jnp.where(labels == own, item_lengths[0], 0))
    end = jnp.sum(jnp.where(labels == own, ends, 0))
    place = jnp.stack([me - (end - length), length]).astype(jnp.int32)
    keys = ITEM_MOST * rows
    wide = keys + rows
    shift = jnp.arange(wide, dtype=jnp.int32)
    relative = jnp.where(shift < keys, shift, shift - wide) - place[0] * rows
    onehot = (
        bucket_of(relative)[:, None] == jnp.arange(BUCKETS, dtype=jnp.int32)[None, :]
    ).astype(f32)
    by_shift = jnp.sum(onehot[None] * rel_table.T[:, None, :], -1)
    bias = window_bias(place, by_shift, rows)

    attended, prob, window, middle, hidden_two = attend(
        place, query, pieces, bias, x, w_out, gain_ffn[None]
    )
    hidden_far = swapped(hidden_two, "seq", pair)

    half = ((me // pair) % 2).astype(jnp.int32)
    far = ffn_half(False, (1 - half)[None], hidden_two, upstream, w_gateup, w_down, ())
    arrived = [swapped(value, "seq", pair) for value in far[:3]]
    near = ffn_half(
        True,
        half[None],
        hidden_two,
        upstream,
        w_gateup,
        w_down,
        (far[3], far[4], middle, gain_ffn[None], w_out),
    )
    output, gain_ffn_grad, middle_back, branch, attended_back = near[3:]

    backs = attend_back(place, query, window, prob, attended_back)
    query_back, shift_sums = backs[:2]
    sends = backs[2:]
    keyval_back = sends[REACH]
    for o in range(-REACH, REACH + 1):
        if o != 0:
            keyval_back = keyval_back + passed_along(sends[o + REACH], "seq", o).astype(f32)
    keyval_back = keyval_back.astype(bf16)

    mine = core.astype(jnp.int32)[None]

    def summed_over_dp(kept, sent):
        return kept, swapped(sent, "dp", 1)

    def shaped(state, dims):
        return tuple(
            value.reshape((2,) * dims + (value.shape[0] >> dims, value.shape[1]))
            for value in state
        )

    down_state = summed_over_dp(*weight_grad(mine, near[0], arrived[0], upstream, upstream_far))
    gate_state = summed_over_dp(*weight_grad(mine, near[1], arrived[1], hidden_two, hidden_far))
    up_state = summed_over_dp(*weight_grad(mine, near[2], arrived[2], hidden_two, hidden_far))
    down_dims = [top] + low[::-1]
    gate_dims = low[::-1]
    down_state = scattered(shaped(down_state, len(down_dims)), down_dims, low + [top])
    gate_state = scattered(shaped(gate_state, len(gate_dims)), gate_dims, low[::-1])
    up_state = scattered(shaped(up_state, len(gate_dims)), gate_dims, low)
    gateup_state = tuple(jnp.stack(both) for both in zip(gate_state, up_state))
    gateup_state, _ = halved(gateup_state, [top], top)
    gateup_grad = (gateup_state[0].astype(f32) + gateup_state[1].astype(f32)).T
    turn = [
        (i, (i & ~(top | pair)) | (pair if i & top else 0) | (top if i & pair else 0))
        for i in range(blocks)
    ]
    down_grad = lax.ppermute(added(*down_state), "seq", turn).astype(f32)

    def halves(value):
        first, second = value[:, :part], value[:, part:]
        return jnp.where(core == 0, first, second), jnp.where(core == 0, second, first)

    hidden_kept, hidden_sent = halves(hidden_one)
    branch_kept, branch_sent = halves(branch)
    all_bits = [top, pair] + low[::-1]

    def blocked(value):
        return value.reshape((2,) * len(all_bits) + (value.shape[0] // blocks, value.shape[1]))

    def early(hidden_part, branch_part):
        return jnp.concatenate(
            [
                blocked(dot_tn(query_back, hidden_part).astype(bf16)),
                blocked(dot_tn(attended, branch_part).astype(bf16)),
            ],
            -2,
        )

    early_state = summed_over_dp(
        early(hidden_kept, branch_kept), early(hidden_sent, branch_sent)
    )
    early_kept, early_got = scattered(early_state, all_bits, low + [top, pair])
    late_state = summed_over_dp(
        blocked(dot_tn(keyval_back, hidden_kept).astype(bf16)),
        blocked(dot_tn(keyval_back, hidden_sent).astype(bf16)),
    )
    late_kept, late_got = scattered(late_state, all_bits, low[::-1] + [top, pair])
    early_grad = early_kept.astype(f32) + early_got.astype(f32)
    keyval_grad = (late_kept.astype(f32) + late_got.astype(f32)).T
    own_rows = inner // blocks
    query_grad = early_grad[:own_rows].T
    out_grad = early_grad[own_rows:]

    hidden_back = dot_nt(query_back, w_query) + dot_nt(keyval_back, w_keyval)
    normed_one = inputs * scale_one
    gain_attn_grad = jnp.sum(hidden_back * normed_one, axis=0)
    normed_back = hidden_back * gain_attn
    input_back = middle_back + scale_one * (
        normed_back - normed_one * jnp.mean(normed_back * normed_one, axis=-1, keepdims=True)
    )

    table_local = jnp.einsum(
        "mb,hm->bh", onehot, shift_sums[:, 0], precision=lax.Precision.HIGHEST
    )
    small = jnp.concatenate([gain_attn_grad, gain_ffn_grad[0], table_local.reshape(-1)])
    count = small.shape[0]
    small = jnp.pad(small, (0, -count % 128)).reshape(-1, 128)
    small = small + swapped(small, "dp", 1)
    for bit in low + [pair, top]:
        small = small + swapped(small, "seq", bit)
    small = small.reshape(-1)
    return (
        output[None],
        input_back[None].astype(bf16),
        small[:width],
        small[width : 2 * width],
        small[2 * width : count].reshape(BUCKETS, H),
        query_grad,
        keyval_grad,
        out_grad,
        gateup_grad,
        down_grad,
    )


def solution(mesh):
    placed = (
        P("dp", "seq", None),
        P("dp", "seq", None),
        P("dp", None),
        P(),
        P(),
        P(),
        P(),
        P(),
        P(),
        P(),
        P(),
    )
    return jax.shard_map(
        on_device,
        mesh=mesh,
        in_specs=placed,
        out_specs=(
            P("dp", "seq", None),
            P("dp", "seq", None),
            P(),
            P(),
            P(),
            P("dp", "seq"),
            P("dp", "seq"),
            P("seq", "dp"),
            P("dp", "seq"),
            P("seq", "dp"),
        ),
        check_vma=False,
    )
```

```python
import functools

import jax
import jax.numpy as jnp
from jax import lax
from jax.experimental import pallas as pl
from jax.experimental.pallas import tpu as pltpu
from jax.sharding import PartitionSpec as P

H = 6
DH = 64
BUCKETS = 32
ITEM_MOST = 4
REACH = ITEM_MOST - 1
PAIR = 2 * DH
UNITS = 896

bucket_edges = (12, 16, 23, 32, 46, 64, 91)
negative_fill = -1e30
f32 = jnp.float32
bf16 = jnp.bfloat16
VMEM_MOST = 56 * 1024 * 1024
FLOPS_PER_US = 5_000_000_000


def bucket_of(relative):
    ahead = jnp.where(relative > 0, 16, 0).astype(jnp.int32)
    distance = jnp.abs(relative)
    beyond = 8 + sum(((distance >= edge).astype(jnp.int32) for edge in bucket_edges))
    return ahead + jnp.where(distance < 8, distance, beyond)


def dot_nn(left, right):
    return lax.dot_general(left, right, (((1,), (0,)), ((), ())), preferred_element_type=f32)


def dot_nt(left, right):
    return lax.dot_general(left, right, (((1,), (1,)), ((), ())), preferred_element_type=f32)


def dot_tn(left, right):
    return lax.dot_general(left, right, (((0,), (0,)), ((), ())), preferred_element_type=f32)


def rms_scale(values):
    return lax.rsqrt(jnp.mean(values * values, axis=-1, keepdims=True) + 1e-06)


def lasting(microseconds):
    return pl.CostEstimate(
        flops=int(microseconds * FLOPS_PER_US), bytes_accessed=0, transcendentals=0
    )


def whole(shape):
    return pl.BlockSpec(shape, lambda *_: (0,) * len(shape))


def params():
    return pltpu.CompilerParams(vmem_limit_bytes=VMEM_MOST)


def up_to(count, step):
    return -(-count // step) * step


def shift_by_head(value):
    return pltpu.roll(value, DH, 1)


def columns(value, index):
    return value[:, index * PAIR : (index + 1) * PAIR]


def low_lanes(shape):
    return lax.broadcasted_iota(jnp.int32, shape, len(shape) - 1) % PAIR < DH


def packed_heads(query, keyval, half):
    low = low_lanes((query.shape[0], PAIR))
    key = [columns(keyval, i) for i in range(3)]
    value = [columns(keyval, i + 3) for i in range(3)]
    ask = [columns(query, i) for i in range(3)]
    if half == 0:
        parts = [
            key[0],
            jnp.where(low, key[1], shift_by_head(value[1])),
            value[0],
            ask[0],
            jnp.where(low, ask[1], 0.0),
        ]
    else:
        parts = [
            key[2],
            jnp.where(low, shift_by_head(key[1]), value[1]),
            value[2],
            ask[2],
            jnp.where(low, shift_by_head(ask[1]), 0.0),
        ]
    return jnp.concatenate(parts, 1).astype(bf16)


def open_kernel(
    spot_ref, inputs_ref, gain_ref, w_query_ref, w_keyval_ref, hidden_ref, mine_ref, other_ref
):
    width = inputs_ref.shape[0]
    inputs = inputs_ref[...].astype(f32)
    scale = lax.rsqrt(jnp.mean(inputs * inputs, axis=0, keepdims=True) + 1e-06)
    hidden = (inputs * scale * gain_ref[...]).astype(bf16).T
    hidden_ref[...] = jnp.zeros_like(hidden_ref)
    hidden_ref[:, :width] = hidden
    keyval = dot_nn(hidden, w_keyval_ref[...])
    query = dot_nn(hidden, w_query_ref[...])
    first = packed_heads(query, keyval, 0)
    second = packed_heads(query, keyval, 1)

    @pl.when(spot_ref[0] == 0)
    def _():
        mine_ref[...] = first
        other_ref[...] = second

    @pl.when(spot_ref[0] != 0)
    def _():
        mine_ref[...] = second
        other_ref[...] = first


def opened(spot, inputs, gain, w_query, w_keyval):
    width, rows = inputs.shape
    inner = w_query.shape[1]
    pack = jax.ShapeDtypeStruct((rows, 5 * PAIR), bf16)
    return pl.pallas_call(
        open_kernel,
        grid_spec=pltpu.PrefetchScalarGridSpec(
            num_scalar_prefetch=1,
            grid=(1,),
            in_specs=[
                whole((width, rows)),
                whole((width, 1)),
                whole((width, inner)),
                whole((width, 2 * inner)),
            ],
            out_specs=[
                whole((rows, up_to(width, 128))),
                whole(pack.shape),
                whole(pack.shape),
            ],
        ),
        out_shape=[jax.ShapeDtypeStruct((rows, up_to(width, 128)), bf16), pack, pack],
        compiler_params=params(),
        cost_estimate=lasting(5),
    )(spot, inputs, gain, w_query, w_keyval)


def turn_kernel(in_ref, out_ref):
    out_ref[...] = jnp.zeros_like(out_ref)
    out_ref[:, : in_ref.shape[0]] = in_ref[...].T


def turned_rows(value):
    width, rows = value.shape
    return pl.pallas_call(
        turn_kernel,
        out_shape=jax.ShapeDtypeStruct((rows, up_to(width, 128)), value.dtype),
        compiler_params=params(),
        cost_estimate=lasting(2),
    )(value)


def bias_kernel(place_ref, by_shift_ref, out_ref):
    rows, keys = out_ref.shape[2:]
    wide = by_shift_ref.shape[-1]
    spread = jnp.broadcast_to(by_shift_ref[0, 0], (rows, wide))
    turned = pltpu.roll(spread, 0, 1, stride=1, stride_axis=0)[:, :keys]
    key = lax.broadcasted_iota(jnp.int32, (rows, keys), 1)
    length = place_ref[2 + pl.program_id(0)]
    out_ref[0, 0] = jnp.where(key < length * rows, turned, negative_fill)


def window_bias(place, by_shift, rows):
    keys = ITEM_MOST * rows
    both, heads, wide = by_shift.shape
    return pl.pallas_call(
        bias_kernel,
        grid_spec=pltpu.PrefetchScalarGridSpec(
            num_scalar_prefetch=1,
            grid=(both, heads),
            in_specs=[pl.BlockSpec((1, 1, 1, wide), lambda b, h, _: (b, h, 0, 0))],
            out_specs=pl.BlockSpec((1, 1, rows, keys), lambda b, h, _: (b, h, 0, 0)),
        ),
        out_shape=jax.ShapeDtypeStruct((both, heads, rows, keys), f32),
        compiler_params=params(),
        cost_estimate=lasting(6),
    )(place, by_shift.reshape(both, heads, 1, wide))


SLOTS = 2 * REACH + 2


def attend_kernel(
    place_ref, query_ref, behind_far, behind, pair_ref, ahead, ahead_far, bias_ref,
    attended_ref, prob_ref, window_ref
):
    rows = query_ref.shape[1]
    block = pl.program_id(0)

    @pl.when(block == 0)
    def _():
        at = 0
        for piece in (behind_far, behind, pair_ref, ahead, ahead_far):
            window_ref[at : at + piece.shape[0], :] = piece[...]
            at += piece.shape[0]

    start = pl.multiple_of((REACH + block - place_ref[block]) * rows, rows)
    window = window_ref[pl.ds(start, ITEM_MOST * rows), :]
    query = query_ref[0]
    low = low_lanes((rows, PAIR))
    nothing = jnp.zeros((rows, PAIR), bf16)
    first = columns(query, 0)
    asks = (jnp.where(low, first, nothing), jnp.where(low, nothing, first), columns(query, 1))
    parts = []
    for head, (key, value) in enumerate(((0, 2), (0, 2), (1, 1))):
        scores = dot_nt(asks[head], columns(window, key)) + bias_ref[0, head]
        exponent = jnp.exp(scores - jnp.max(scores, axis=-1, keepdims=True))
        prob = exponent / jnp.sum(exponent, axis=-1, keepdims=True)
        prob_ref[0, head] = prob
        parts.append(dot_nn(prob.astype(bf16), columns(window, value)))
    attended_ref[0, :PAIR, :] = jnp.where(low, parts[0], parts[1]).T.astype(bf16)
    attended_ref[0, PAIR:, :] = parts[2].T[DH:].astype(bf16)


def attend(place, query, pieces, bias):
    _, rows, _ = query.shape
    keys = ITEM_MOST * rows
    wide = pieces[0].shape[1]
    heads = bias.shape[1]
    return pl.pallas_call(
        attend_kernel,
        grid_spec=pltpu.PrefetchScalarGridSpec(
            num_scalar_prefetch=1,
            grid=(2,),
            in_specs=[pl.BlockSpec((1, rows, 2 * PAIR), lambda b, _: (b, 0, 0))]
            + [whole(piece.shape) for piece in pieces]
            + [pl.BlockSpec((1, heads, rows, keys), lambda b, _: (b, 0, 0, 0))],
            out_specs=[
                pl.BlockSpec((1, heads * DH, rows), lambda b, _: (b, 0, 0)),
                pl.BlockSpec((1, heads, rows, keys), lambda b, _: (b, 0, 0, 0)),
                whole((SLOTS * rows, wide)),
            ],
        ),
        out_shape=[
            jax.ShapeDtypeStruct((2, heads * DH, rows), bf16),
            jax.ShapeDtypeStruct((2, heads, rows, keys), f32),
            jax.ShapeDtypeStruct((SLOTS * rows, wide), bf16),
        ],
        compiler_params=params(),
        cost_estimate=lasting(9),
    )(place, query, *pieces, bias)


def natural_heads(half, mine, other, out):
    each = mine.shape[0]

    def put(first, second):
        out[:each, :] = first[...]
        out[each : each + DH, :] = second[PAIR:, :]
        out[each + DH :, :] = second[:PAIR, :]

    @pl.when(half == 0)
    def _():
        put(mine, other)

    @pl.when(half != 0)
    def _():
        put(other, mine)


def middle_kernel(
    spot_ref, mine_ref, other_ref, inputs_ref, w_out_ref, gain_ref, middle_ref, hidden_ref, attended
):
    width = inputs_ref.shape[0]
    natural_heads(spot_ref[0], mine_ref, other_ref, attended)
    middle = inputs_ref[...].astype(f32) + dot_nn(w_out_ref[...], attended[...])
    middle_ref[...] = middle
    scale = lax.rsqrt(jnp.mean(middle * middle, axis=0, keepdims=True) + 1e-06)
    hidden_ref[...] = jnp.zeros_like(hidden_ref)
    hidden_ref[:, :width] = (middle * scale * gain_ref[...]).astype(bf16).T


def middle_part(spot, mine, other, inputs, w_out, gain):
    width, rows = inputs.shape
    inner = w_out.shape[1]
    return pl.pallas_call(
        middle_kernel,
        grid_spec=pltpu.PrefetchScalarGridSpec(
            num_scalar_prefetch=1,
            grid=(1,),
            in_specs=[
                whole(mine.shape),
                whole(other.shape),
                whole((width, rows)),
                whole((width, inner)),
                whole((width, 1)),
            ],
            out_specs=[whole((width, rows)), whole((rows, up_to(width, 128)))],
            scratch_shapes=[pltpu.VMEM((inner, rows), bf16)],
        ),
        out_shape=[
            jax.ShapeDtypeStruct((width, rows), f32),
            jax.ShapeDtypeStruct((rows, up_to(width, 128)), bf16),
        ],
        compiler_params=params(),
        cost_estimate=lasting(4),
    )(spot, mine, other, inputs, w_out, gain)


GELU_A = 0.7978845608028654
GELU_B = 0.044715


def filled(value, rows):
    return jnp.concatenate([value, jnp.zeros((rows - value.shape[0], value.shape[1]), value.dtype)], 0)


def packed_back(back, half):
    low = low_lanes((back.shape[0], PAIR))
    middle = columns(back, 1)
    if half == 0:
        parts = [columns(back, 0), jnp.where(low, 0.0, shift_by_head(middle))]
    else:
        parts = [columns(back, 2), jnp.where(low, 0.0, middle)]
    return jnp.concatenate(parts, 1).astype(bf16)


def ffn_kernel(last, spot_ref, hidden_ref, upstream_ref, gate_w_ref, up_w_ref, down_w_ref, *refs):
    if last:
        out_in, back_in, middle_ref, gain_ref, w_out_ref, cotangent_ref = refs[:6]
        (mixed_ref, both_ref, output_ref, gain_grad_ref, middle_back_ref,
         branch_ref, back_mine_ref, back_other_ref, out_ref, back_ref) = refs[6:]
    else:
        mixed_ref, both_ref, out_ref, back_ref = refs
    step = pl.program_id(0)
    width, units = gate_w_ref.shape
    hidden = hidden_ref[...]
    wide = hidden.shape[1]
    upstream = upstream_ref[...]
    gateup_w = jnp.concatenate([gate_w_ref[...], up_w_ref[...]], 1)
    gateup = dot_nn(hidden, filled(gateup_w, wide))
    gate, up = gateup[:, :units], gateup[:, units:]
    mixed_back = dot_nn(upstream, filled(down_w_ref[...], wide))
    squared = gate * gate
    bent = jnp.tanh(GELU_A * (gate + GELU_B * (squared * gate)))
    share = 0.5 * (1.0 + bent)
    gelu = gate * share
    slope = share + 0.5 * gate * (1.0 - bent * bent) * (GELU_A * (1.0 + 3.0 * GELU_B * squared))
    mixed = (gelu * up).astype(bf16).T
    gate_back = (mixed_back * up * slope).astype(bf16).T
    up_back = (mixed_back * gelu).astype(bf16).T
    mixed_ref[...] = mixed
    both_ref[0] = gate_back
    both_ref[1] = up_back
    forward = dot_nn(down_w_ref[...], mixed)
    backward = dot_nn(gateup_w, jnp.concatenate([gate_back, up_back], 0))

    @pl.when(step == 0)
    def _():
        if last:
            out_ref[...] = out_in[...] + forward
            back_ref[...] = back_in[...] + backward
        else:
            out_ref[...] = forward
            back_ref[...] = backward

    @pl.when(step > 0)
    def _():
        out_ref[...] += forward
        back_ref[...] += backward

    if not last:
        return

    @pl.when(step == pl.num_programs(0) - 1)
    def _():
        middle = middle_ref[...]
        output_ref[...] = (middle + out_ref[...]).astype(bf16)
        scale = lax.rsqrt(jnp.mean(middle * middle, axis=0, keepdims=True) + 1e-06)
        normed = middle * scale
        back = back_ref[...]
        gain_grad_ref[...] = jnp.sum(back * normed, axis=1, keepdims=True)
        normed_back = back * gain_ref[...]
        mean = jnp.mean(normed_back * normed, axis=0, keepdims=True)
        middle_back = cotangent_ref[...].astype(f32) + scale * (normed_back - normed * mean)
        middle_back_ref[...] = middle_back
        branch = middle_back.astype(bf16).T
        branch_ref[...] = jnp.zeros_like(branch_ref)
        branch_ref[:, :width] = branch
        attended_back = dot_nn(branch, w_out_ref[...])
        first = packed_back(attended_back, 0)
        second = packed_back(attended_back, 1)

        @pl.when(spot_ref[0] == 0)
        def _():
            back_mine_ref[...] = first
            back_other_ref[...] = second

        @pl.when(spot_ref[0] != 0)
        def _():
            back_mine_ref[...] = second
            back_other_ref[...] = first


def ffn_half(last, spot, hidden, upstream, w_gateup, w_down, more=()):
    rows, wide = hidden.shape
    width, units = w_down.shape
    steps = units // 2 // UNITS
    both = units // UNITS
    in_specs = [
        whole((rows, wide)),
        whole((rows, wide)),
        pl.BlockSpec((width, UNITS), lambda j, s: (0, s[1] * steps + j)),
        pl.BlockSpec((width, UNITS), lambda j, s: (0, both + s[1] * steps + j)),
        pl.BlockSpec((width, UNITS), lambda j, s: (0, s[1] * steps + j)),
    ] + [whole(value.shape) for value in more]
    sums = [jax.ShapeDtypeStruct((width, rows), f32)] * 2
    out_specs = [
        pl.BlockSpec((UNITS, rows), lambda j, s: (j, 0)),
        pl.BlockSpec((2, UNITS, rows), lambda j, s: (0, j, 0)),
    ]
    out_shape = [
        jax.ShapeDtypeStruct((units // 2, rows), bf16),
        jax.ShapeDtypeStruct((2, units // 2, rows), bf16),
    ]
    if last:
        rest = [
            jax.ShapeDtypeStruct((width, rows), bf16),
            jax.ShapeDtypeStruct((width, 1), f32),
            jax.ShapeDtypeStruct((width, rows), f32),
            jax.ShapeDtypeStruct((rows, wide), bf16),
            jax.ShapeDtypeStruct((rows, 2 * PAIR), bf16),
            jax.ShapeDtypeStruct((rows, 2 * PAIR), bf16),
        ]
    else:
        rest = sums
    return pl.pallas_call(
        functools.partial(ffn_kernel, last),
        grid_spec=pltpu.PrefetchScalarGridSpec(
            num_scalar_prefetch=1,
            grid=(steps,),
            in_specs=in_specs,
            out_specs=out_specs + [whole(value.shape) for value in rest],
            scratch_shapes=[pltpu.VMEM((width, rows), f32)] * 2 if last else [],
        ),
        out_shape=out_shape + rest,
        compiler_params=params(),
        cost_estimate=lasting(20),
    )(spot, hidden, upstream, w_gateup, w_gateup, w_down, *more)


def split_halves(mine, source, part, low_ref, high_ref):
    first, second = source[:, :part], source[:, part : 2 * part]

    @pl.when(mine == 0)
    def _():
        low_ref[:, :part] = first
        high_ref[:, :part] = second

    @pl.when(mine != 0)
    def _():
        low_ref[:, :part] = second
        high_ref[:, :part] = first


def pair_grad_kernel(
    part, spot_ref, left_own, left_far, right_own, right_far, kept_ref, sent_ref, halves
):
    rows = left_own.shape[-1]

    @pl.when(pl.program_id(0) == 0)
    def _():
        halves[...] = jnp.zeros_like(halves)
        for index, right in enumerate((right_own, right_far)):
            at = slice(index * rows, (index + 1) * rows)
            split_halves(spot_ref[0], right[...], part, halves.at[0, at], halves.at[1, at])

    left = jnp.concatenate([left_own[0], left_far[0]], 1)
    kept_ref[...] = dot_nn(left, halves[0]).astype(bf16)
    sent_ref[...] = dot_nn(left, halves[1]).astype(bf16)


def pair_grad(spot, tiles, tile, left_own, left_far, right_own, right_far, part):
    count, place = tiles
    rows = left_far.shape[-1]
    wide = up_to(part, 128)
    out = jax.ShapeDtypeStruct((count * tile, wide), bf16)
    left = pl.BlockSpec((1, tile, rows), lambda j, _: (*place(j), 0))
    return pl.pallas_call(
        functools.partial(pair_grad_kernel, part),
        grid_spec=pltpu.PrefetchScalarGridSpec(
            num_scalar_prefetch=1,
            grid=(count,),
            in_specs=[left, left, whole(right_own.shape), whole(right_far.shape)],
            out_specs=[pl.BlockSpec((tile, wide), lambda j, _: (j, 0))] * 2,
            scratch_shapes=[pltpu.VMEM((2, 2 * rows, wide), bf16)],
        ),
        out_shape=[out, out],
        compiler_params=params(),
        cost_estimate=lasting(8),
    )(spot, left_own, left_far, right_own, right_far)


def heads_grad_kernel(
    part, spot_ref, keyval_ref, query_ref, attended_ref, hidden_own, hidden_far, branch_own,
    branch_far, kept_ref, sent_ref, low, high, left
):
    rows = hidden_own.shape[0]
    half = spot_ref[1]
    each = query_ref.shape[1]
    kept = 0

    def ordered(source, at, first, second):
        @pl.when(half == 0)
        def _():
            for start, stop, to in first:
                left[at + to : at + to + stop - start, :] = source(start, stop)

        @pl.when(half != 0)
        def _():
            for start, stop, to in second:
                left[at + to : at + to + stop - start, :] = source(start, stop)

    same = ((0, 3 * DH, 0),)
    turned = ((PAIR, 3 * DH, 0), (0, PAIR, DH))
    value_first = ((4 * DH, 6 * DH, 0), (3 * DH, 4 * DH, PAIR))
    value_second = ((3 * DH, 6 * DH, 0),)

    def joined(ref):
        return lambda start, stop: jnp.concatenate(
            [ref[0, start:stop, :], ref[1, start:stop, :]], 1
        )

    def plain(start, stop):
        return keyval_ref[start:stop, :]

    ordered(joined(query_ref), 0, same, turned)
    ordered(plain, each, same, turned)
    ordered(plain, 2 * each, value_first, value_second)
    ordered(joined(attended_ref), 3 * each, same, turned)

    low[...] = jnp.zeros_like(low)
    high[...] = jnp.zeros_like(high)
    for own, far, at, stop in (
        (hidden_own, hidden_far, 0, 3 * each),
        (branch_own, branch_far, 3 * each, 4 * each),
    ):
        for index, source in ((0, own), (1, far)):

            @pl.when(half == index)
            def _():
                split_halves(spot_ref[0], source[...], part, low.at[:rows], high.at[:rows])

            @pl.when(half != index)
            def _():
                split_halves(spot_ref[0], source[...], part, low.at[rows:], high.at[rows:])

        kept_ref[at:stop, :] = dot_nn(left[at:stop, :], low[...]).astype(bf16)
        sent_ref[at:stop, :] = dot_nn(left[at:stop, :], high[...]).astype(bf16)


def heads_grad(spot, keyval, query, attended, hiddens, branches, part):
    wide = up_to(part, 128)
    rows = hiddens[0].shape[0]
    each = query.shape[1]
    out = jax.ShapeDtypeStruct((4 * each, wide), bf16)
    operands = (keyval, query, attended, *hiddens, *branches)
    return pl.pallas_call(
        functools.partial(heads_grad_kernel, part),
        grid_spec=pltpu.PrefetchScalarGridSpec(
            num_scalar_prefetch=1,
            grid=(1,),
            in_specs=[whole(value.shape) for value in operands],
            out_specs=[whole(out.shape)] * 2,
            scratch_shapes=[pltpu.VMEM((2 * rows, wide), bf16)] * 2
            + [pltpu.VMEM((4 * each, 2 * rows), bf16)],
        ),
        out_shape=[out, out],
        compiler_params=params(),
        cost_estimate=lasting(7),
    )(spot, *operands)


def attend_back_kernel(
    place_ref, query_ref, window_ref, prob_ref, back_ref, query_back_ref, by_shift_ref,
    behind_far, behind, pair_ref, ahead, ahead_far, total
):
    rows = query_ref.shape[1]
    keys = ITEM_MOST * rows
    block = pl.program_id(0)
    start = pl.multiple_of((REACH + block - place_ref[block]) * rows, rows)
    window = window_ref[pl.ds(start, keys), :]
    query, back = query_ref[0], back_ref[0]
    low = low_lanes((rows, PAIR))
    nothing = jnp.zeros((rows, PAIR), bf16)

    def spread(value):
        first = columns(value, 0)
        return jnp.where(low, first, nothing), jnp.where(low, nothing, first), columns(value, 1)

    asks, backs = spread(query), spread(back)
    row = lax.broadcasted_iota(jnp.int32, (rows, rows), 0)
    column = lax.broadcasted_iota(jnp.int32, (rows, rows), 1)
    flip = jnp.where(row + column == rows - 1, 1.0, 0.0).astype(bf16)
    query_parts, sums = [], [None] * 3
    for head, (key, value) in enumerate(((0, 2), (0, 2), (1, 1))):
        prob = prob_ref[0, head]
        prob_back = dot_nt(backs[head], columns(window, value))
        delta = jnp.sum(prob * prob_back, axis=-1, keepdims=True)
        score_back = (prob * (prob_back - delta)).astype(bf16)
        query_parts.append(dot_nn(score_back, columns(window, key)))
        key_part = dot_tn(asks[head], score_back)
        value_part = dot_tn(backs[head], prob.astype(bf16))
        for group, add in ((key, key_part), (value, value_part)):
            sums[group] = add if sums[group] is None else sums[group] + add
        flipped = dot_nn(flip, score_back)
        wide = jnp.concatenate([flipped, jnp.zeros((rows, rows), f32)], 1)
        turned = pltpu.roll(wide, keys + 1, 1, stride=1, stride_axis=0)
        by_shift_ref[0, head] = jnp.sum(turned, axis=0, keepdims=True)
    query_back_ref[0, :PAIR, :] = jnp.where(low, query_parts[0], query_parts[1]).T.astype(bf16)
    query_back_ref[0, PAIR:, :] = query_parts[2].T[:DH].astype(bf16)

    @pl.when(block == 0)
    def _():
        total[...] = jnp.zeros_like(total)

    for group in range(3):
        total[group * PAIR : (group + 1) * PAIR, pl.ds(start, keys)] += sums[group]

    @pl.when(block == 1)
    def _():
        at = 0
        for out in (behind_far, behind, pair_ref, ahead, ahead_far):
            out[...] = total[:, at : at + out.shape[1]].astype(out.dtype)
            at += out.shape[1]


def attend_back(place, query, window, prob, back):
    _, rows, _ = query.shape
    _, heads, _, keys = prob.shape
    wide = window.shape[1]
    pieces = [(rows, bf16), (2 * rows, bf16), (2 * rows, f32), (2 * rows, bf16), (rows, bf16)]
    each = pl.BlockSpec((1, rows, 2 * PAIR), lambda b, _: (b, 0, 0))
    return pl.pallas_call(
        attend_back_kernel,
        grid_spec=pltpu.PrefetchScalarGridSpec(
            num_scalar_prefetch=1,
            grid=(2,),
            in_specs=[
                each,
                whole(window.shape),
                pl.BlockSpec((1, heads, rows, keys), lambda b, _: (b, 0, 0, 0)),
                each,
            ],
            out_specs=[
                pl.BlockSpec((1, heads * DH, rows), lambda b, _: (b, 0, 0)),
                pl.BlockSpec((1, heads, 1, keys + rows), lambda b, _: (b, 0, 0, 0)),
            ]
            + [whole((wide, count)) for count, _ in pieces],
            scratch_shapes=[pltpu.VMEM((wide, SLOTS * rows), f32)],
        ),
        out_shape=[
            jax.ShapeDtypeStruct((2, heads * DH, rows), bf16),
            jax.ShapeDtypeStruct((2, heads, 1, keys + rows), f32),
        ]
        + [jax.ShapeDtypeStruct((wide, count), dtype) for count, dtype in pieces],
        compiler_params=params(),
        cost_estimate=lasting(12),
    )(place, query, window, prob, back)


def gather_kernel(
    spot_ref, pair_ref, behind, ahead, behind_far, ahead_far, query_ref, both_ref, mine_ref,
    other_ref
):
    rows = behind_far.shape[1]
    wide = pair_ref.shape[0]
    total = pair_ref[...] + behind[...].astype(f32) + ahead[...].astype(f32)
    first = (total[:, :rows] + behind_far[...].astype(f32)).astype(bf16)
    second = (total[:, rows:] + ahead_far[...].astype(f32)).astype(bf16)
    both_ref[:, :rows] = first
    both_ref[:, rows:] = second

    @pl.when(spot_ref[0] == 0)
    def _():
        mine_ref[:wide, :] = first
        other_ref[:wide, :] = second
        mine_ref[wide:, :] = query_ref[0]
        other_ref[wide:, :] = query_ref[1]

    @pl.when(spot_ref[0] != 0)
    def _():
        mine_ref[:wide, :] = second
        other_ref[:wide, :] = first
        mine_ref[wide:, :] = query_ref[1]
        other_ref[wide:, :] = query_ref[0]


def gathered(spot, pair, behind, ahead, behind_far, ahead_far, query):
    wide, rows = behind_far.shape
    operands = (pair, behind, ahead, behind_far, ahead_far, query)
    pack = jax.ShapeDtypeStruct((wide + query.shape[1], rows), bf16)
    both = jax.ShapeDtypeStruct((wide, 2 * rows), bf16)
    return pl.pallas_call(
        gather_kernel,
        grid_spec=pltpu.PrefetchScalarGridSpec(
            num_scalar_prefetch=1,
            grid=(1,),
            in_specs=[whole(value.shape) for value in operands],
            out_specs=[whole(both.shape), whole(pack.shape), whole(pack.shape)],
        ),
        out_shape=[both, pack, pack],
        compiler_params=params(),
        cost_estimate=lasting(3),
    )(spot, *operands)


def close_kernel(
    spot_ref, mine_ref, other_ref, inputs_ref, middle_back_ref, w_query_ref, w_keyval_ref,
    gain_ref, input_back_ref, gain_grad_ref, query_back, keyval_back
):
    inner = query_back.shape[0]
    each = inner // 2

    def put(first, second):
        keyval_back[:each, :] = first[:each, :]
        keyval_back[each : each + DH, :] = second[PAIR : PAIR + DH, :]
        keyval_back[each + DH : inner, :] = second[:PAIR, :]
        keyval_back[inner : inner + PAIR, :] = first[4 * DH : 6 * DH, :]
        keyval_back[inner + PAIR : inner + each, :] = first[3 * DH : 4 * DH, :]
        keyval_back[inner + each :, :] = second[3 * DH : 6 * DH, :]
        query_back[:each, :] = first[inner:, :]
        query_back[each : each + DH, :] = second[inner + PAIR :, :]
        query_back[each + DH :, :] = second[inner : inner + PAIR, :]

    @pl.when(spot_ref[0] == 0)
    def _():
        put(mine_ref, other_ref)

    @pl.when(spot_ref[0] != 0)
    def _():
        put(other_ref, mine_ref)

    inputs = inputs_ref[...].astype(f32)
    scale = lax.rsqrt(jnp.mean(inputs * inputs, axis=0, keepdims=True) + 1e-06)
    normed = inputs * scale
    back = dot_nn(w_query_ref[...], query_back[...]) + dot_nn(w_keyval_ref[...], keyval_back[...])
    gain_grad_ref[...] = jnp.sum(back * normed, axis=1, keepdims=True)
    normed_back = back * gain_ref[...]
    mean = jnp.mean(normed_back * normed, axis=0, keepdims=True)
    input_back_ref[...] = (
        middle_back_ref[...] + scale * (normed_back - normed * mean)
    ).astype(bf16)


def closed(spot, mine, other, inputs, middle_back, w_query, w_keyval, gain):
    width, rows = inputs.shape
    inner = w_query.shape[1]
    operands = (mine, other, inputs, middle_back, w_query, w_keyval, gain)
    return pl.pallas_call(
        close_kernel,
        grid_spec=pltpu.PrefetchScalarGridSpec(
            num_scalar_prefetch=1,
            grid=(1,),
            in_specs=[whole(value.shape) for value in operands],
            out_specs=[whole((width, rows)), whole((width, 1))],
            scratch_shapes=[
                pltpu.VMEM((inner, rows), bf16),
                pltpu.VMEM((2 * inner, rows), bf16),
            ],
        ),
        out_shape=[
            jax.ShapeDtypeStruct((width, rows), bf16),
            jax.ShapeDtypeStruct((width, 1), f32),
        ],
        compiler_params=params(),
        cost_estimate=lasting(6),
    )(spot, *operands)


def swapped(value, axis, bit):
    size = lax.axis_size(axis)
    return lax.ppermute(value, axis, [(i, i ^ bit) for i in range(size)])


def passed_along(value, axis, by):
    size = lax.axis_size(axis)
    pairs = [(i, i + by) for i in range(size) if 0 <= i + by < size]
    return lax.ppermute(value, axis, pairs)


def of_both(value, bit):
    size = lax.axis_size("seq")
    groups = [[i, i | bit] for i in range(size) if not i & bit]
    return lax.all_gather(value, "seq", axis=0, tiled=True, axis_index_groups=groups)


def chosen(value, dim, index):
    return lax.dynamic_index_in_dim(value, index, dim, keepdims=False)


def added(left, right):
    return (left.astype(f32) + right.astype(f32)).astype(bf16)


def parted(state, dims, bit):
    left, right = state
    dim = dims.index(bit)
    mine = (lax.axis_index("seq") // bit) % 2
    kept = added(chosen(left, dim, mine), chosen(right, dim, mine))
    sent = added(chosen(left, dim, 1 - mine), chosen(right, dim, 1 - mine))
    return kept, sent, dims[:dim] + dims[dim + 1 :]


def after(value, *others):
    return lax.optimization_barrier((value, *others))[0]


class Halving:
    def __init__(self, state, dims, order):
        self.kept, self.got = state
        self.dims, self.order = dims, list(order)

    def step(self, earlier):
        bit = self.order.pop(0)
        got = after(self.got, earlier)
        self.kept, sent, self.dims = parted((self.kept, got), self.dims, bit)
        self.got = swapped(sent, "seq", bit)
        return sent

    def total(self, dtype=bf16):
        return (self.kept.astype(f32) + self.got.astype(f32)).astype(dtype)


def on_device(
    tokens,
    cotangent,
    item_lengths,
    gain_attn,
    gain_ffn,
    rel_table,
    w_query,
    w_keyval,
    w_out,
    w_gateup,
    w_down,
):
    rows = tokens.shape[1]
    width = tokens.shape[2]
    part = width // 2
    inner = w_query.shape[1]
    blocks = lax.axis_size("seq")
    me = lax.axis_index("seq")
    core = lax.axis_index("dp").astype(jnp.int32)
    top, pair, third = blocks // 2, blocks // 4, blocks // 8
    low = [1 << i for i in range(blocks.bit_length() - 1)][:-2]

    inputs = tokens[0].T
    cotangent = cotangent[0].T
    w_out = w_out.T
    w_down = w_down.T
    gain_attn = gain_attn[:, None]
    gain_ffn = gain_ffn[:, None]

    def bit_of(bit):
        return ((me // bit) % 2).astype(jnp.int32)

    side = bit_of(1)
    half = bit_of(pair)
    down_half = bit_of(third)

    def by_side(mine, other):
        return jnp.where(side == 0, mine, other), jnp.where(side == 0, other, mine)

    hidden_one, mine, other = opened(side[None], inputs, gain_attn, w_query, w_keyval)
    got = swapped(other, "seq", 1)
    blocks_here = me - side + jnp.arange(2, dtype=jnp.int32)
    ends = jnp.cumsum(item_lengths[0])
    own = jnp.sum((ends[None, :] <= blocks_here[:, None]).astype(jnp.int32), 1)
    labels = jnp.arange(item_lengths.shape[1], dtype=jnp.int32)
    mark = labels[None, :] == own[:, None]
    length = jnp.sum(jnp.where(mark, item_lengths[0][None, :], 0), 1)
    end = jnp.sum(jnp.where(mark, ends[None, :], 0), 1)
    place = jnp.concatenate([blocks_here - (end - length), length]).astype(jnp.int32)
    keys = ITEM_MOST * rows
    turns = keys + rows
    shift = jnp.arange(turns, dtype=jnp.int32)
    relative = jnp.where(shift < keys, shift, shift - turns)[None, :] - place[:2, None] * rows
    onehot = (
        bucket_of(relative)[:, :, None] == jnp.arange(BUCKETS, dtype=jnp.int32)[None, None, :]
    ).astype(f32)
    table = jnp.where(
        side == 0,
        rel_table[:, :3],
        jnp.concatenate([rel_table[:, 4:6], rel_table[:, 3:4]], 1),
    )
    by_shift = jnp.sum(onehot[:, None] * table.T[None, :, None, :], -1)
    bias = window_bias(place, by_shift, rows)

    got = after(got, bias)
    first, second = by_side(mine, got)
    wide = 3 * PAIR
    queries = jnp.stack([first[:, wide:], second[:, wide:]])
    keyvals = jnp.concatenate([first[:, :wide], second[:, :wide]], 0)
    pieces = [
        passed_along(second[:, :wide], "seq", 4),
        passed_along(keyvals, "seq", 2),
        keyvals,
        passed_along(keyvals, "seq", -2),
        passed_along(first[:, :wide], "seq", -4),
    ]

    upstream = turned_rows(cotangent)
    attended, prob, window = attend(place, queries, pieces, bias)
    attended_got = swapped(chosen(attended, 0, 1 - side), "seq", 1)
    middle, hidden_two = middle_part(
        side[None], chosen(attended, 0, side), attended_got, inputs, w_out, gain_ffn
    )
    hidden_far = swapped(hidden_two, "seq", pair)
    upstream_far = swapped(upstream, "seq", third)
    hidden_one_far = swapped(hidden_one, "seq", 1)

    mixed_first, back_first, *sums = ffn_half(
        False, jnp.stack([side, 1 - half]), hidden_two, upstream, w_gateup, w_down
    )
    back_far = swapped(back_first, "seq", pair)
    sums = after(tuple(sums), hidden_far, upstream_far)
    mixed_second, back, output, gain_ffn_grad, middle_back, branch, back_mine, back_other = ffn_half(
        True,
        jnp.stack([side, half]),
        hidden_two,
        upstream,
        w_gateup,
        w_down,
        (*sums, middle, gain_ffn, w_out, cotangent),
    )
    same = half == down_half
    mixed = jnp.where(same, mixed_second, mixed_first)
    mixed_far = swapped(jnp.where(same, mixed_first, mixed_second), "seq", third)
    back_got = swapped(back_other, "seq", 1)
    branch_far = swapped(after(branch, back_got), "seq", 1)
    attended_back = jnp.stack(by_side(back_mine, back_got))
    attended_back = after(attended_back, hidden_one_far)

    backs = attend_back(place, queries, window, prob, attended_back)
    query_back, shift_sums = backs[:2]
    sends = backs[2:]

    def over_dp(kept, sent, dims):
        got = swapped(sent, "dp", 1)
        return tuple(
            value.reshape((2,) * dims + (value.shape[0] >> dims, value.shape[1]))
            for value in (kept, got)
        )

    spot = jnp.stack([core, half])
    units = mixed.shape[0]
    owned = units * 4 // blocks
    split = owned // 2
    owners = units // owned

    parts = 2 if split % 16 == 0 else 1
    tile = split if parts == 2 else units // 4
    tiles = 2 * owners if parts == 2 else 8

    def part_of(index):
        if parts == 1:
            return (tiles, lambda j: (j // 4, j % 4))
        return (tiles, lambda j: (j // owners, 2 * (j % owners) + index))

    near_kept, near_sent = pair_grad(
        spot,
        part_of(0),
        tile,
        after(back, query_back),
        back_far,
        hidden_two,
        hidden_far,
        part,
    )
    near = Halving(
        over_dp(near_kept, near_sent, len(low) + 1), [top] + low[::-1], low[::-1] + [top]
    )
    down_kept, down_sent = pair_grad(
        spot,
        (4, lambda j: (0, j)),
        units // 4,
        after(mixed, near_kept)[None],
        mixed_far[None],
        upstream,
        upstream_far,
        part,
    )
    sent = near.step(down_kept)
    down = Halving(
        over_dp(down_kept, after(down_sent, sent), len(low) + 1),
        [pair, top] + low[-2::-1],
        [pair] + low[-2::-1] + [top],
    )
    keyval_back, to_close, to_swap = gathered(
        side[None],
        after(sends[2], sent),
        passed_along(sends[3], "seq", 2),
        passed_along(sends[1], "seq", -2),
        passed_along(sends[4], "seq", 4),
        passed_along(sends[0], "seq", -4),
        query_back,
    )
    closed_with = swapped(to_swap, "seq", 1)
    far = None
    done = keyval_back
    if parts == 2:
        done, far_sent = pair_grad(
            spot, part_of(1), tile, after(back, keyval_back), back_far, hidden_two, hidden_far, part
        )
    sent = down.step(done)
    if parts == 2:
        far = Halving(
            over_dp(done, after(far_sent, sent), len(low) + 1),
            [top] + low[::-1],
            low[::-1] + [top],
        )
    input_back, gain_attn_grad = closed(
        side[None],
        after(to_close, sent),
        closed_with,
        inputs,
        middle_back,
        w_query,
        w_keyval,
        gain_attn,
    )

    sent = far.step(gain_attn_grad) if far else gain_attn_grad

    head_kept, head_sent = heads_grad(
        jnp.stack([core, side]),
        after(keyval_back, sent),
        query_back,
        attended,
        (hidden_one, hidden_one_far),
        (branch, branch_far),
        part,
    )
    others = [top, pair] + low[:0:-1]
    count = len(others)
    each = inner // 2

    def by_owner(value):
        def cut(array, bits):
            array = array.reshape((2,) * count + (-1, array.shape[-1]))
            return array.transpose([bits.index(bit) for bit in others] + [count, count + 1])

        asks = [pair] + low[:0:-1] + [top]
        keyvals = [top] + low[:0:-1] + [pair]
        return jnp.concatenate(
            [
                cut(value[:each], asks),
                cut(value[3 * each :], asks),
                cut(value[each : 3 * each], keyvals),
            ],
            -2,
        )

    sums = jnp.einsum(
        "pmb,phm->bh", onehot, shift_sums[:, :, 0], precision=lax.Precision.HIGHEST
    )
    nothing = jnp.zeros_like(sums)
    table_local = jnp.where(
        side == 0,
        jnp.concatenate([sums, nothing], 1),
        jnp.concatenate([nothing, sums[:, 2:], sums[:, :2]], 1),
    )
    small = jnp.concatenate(
        [gain_attn_grad.reshape(-1), gain_ffn_grad.reshape(-1), table_local.reshape(-1)]
    )
    taken = small.shape[0]
    small = jnp.pad(small, (0, -taken % 128)).reshape(-1, 128)
    small_got = swapped(small, "dp", 1)
    head = Halving(
        (by_owner(head_kept), by_owner(swapped(head_sent, "dp", 1))),
        others,
        [pair] + low[1:] + [top],
    )
    small_order = low + [pair, top]
    sent = near.step(head_kept)
    chains = [chain for chain in (head, down, near, far) if chain]
    while any(chain.order for chain in chains) or small_order:
        for chain in chains:
            if chain.order:
                sent = chain.step(sent)
            if small_order and chain in (head, near):
                small = small + after(small_got, sent)
                small_got = swapped(small, "seq", small_order.pop(0))
    small = small + after(small_got, sent)

    turn = [
        (i, (i & ~(top | third)) | (third if i & top else 0) | (top if i & third else 0))
        for i in range(blocks)
    ]
    down_grad = lax.ppermute(down.total(), "seq", turn).astype(f32)[:, :part]
    def exchanged(i, bit):
        return (i & ~(1 | bit)) | (1 if i & bit else 0) | (bit if i & 1 else 0)

    own_rows = inner // blocks
    head_sum = head.total()
    asks = lax.ppermute(
        head_sum[: 2 * own_rows], "seq", [(i, exchanged(i, top)) for i in range(blocks)]
    ).astype(f32)
    query_grad = asks[:own_rows, :part].T
    out_grad = asks[own_rows:, :part]
    keyval_grad = (
        lax.ppermute(
            head_sum[2 * own_rows :], "seq", [(i, exchanged(i, pair)) for i in range(blocks)]
        )
        .astype(f32)[:, :part]
        .T
    )
    gateup_grad = jnp.concatenate([one.total(f32)[:, :part].T for one in (near, far) if one], 1)
    small = small.reshape(-1)
    return (
        output.T[None],
        input_back.T[None],
        small[:width],
        small[width : 2 * width],
        small[2 * width : taken].reshape(BUCKETS, H),
        query_grad,
        keyval_grad,
        out_grad,
        gateup_grad,
        down_grad,
    )


def solution(mesh):
    placed = (
        P("dp", "seq", None),
        P("dp", "seq", None),
        P("dp", None),
        P(),
        P(),
        P(),
        P(),
        P(),
        P(),
        P(),
        P(),
    )
    return jax.shard_map(
        on_device,
        mesh=mesh,
        in_specs=placed,
        out_specs=(
            P("dp", "seq", None),
            P("dp", "seq", None),
            P(),
            P(),
            P(),
            P("dp", "seq"),
            P("dp", "seq"),
            P("seq", "dp"),
            P("dp", "seq"),
            P("seq", "dp"),
        ),
        check_vma=False,
    )
```

```python
import functools

import jax
import jax.numpy as jnp
from jax import lax
from jax.experimental import pallas as pl
from jax.experimental.pallas import tpu as pltpu
from jax.sharding import PartitionSpec as P

H = 6
DH = 64
BUCKETS = 32
ITEM_MOST = 4
REACH = ITEM_MOST - 1
PAIR = 2 * DH
UNITS = 896

bucket_edges = (12, 16, 23, 32, 46, 64, 91)
negative_fill = -1e30
f32 = jnp.float32
bf16 = jnp.bfloat16
VMEM_MOST = 56 * 1024 * 1024
FLOPS_PER_US = 5_000_000_000


def bucket_of(relative):
    ahead = jnp.where(relative > 0, 16, 0).astype(jnp.int32)
    distance = jnp.abs(relative)
    beyond = 8 + sum(((distance >= edge).astype(jnp.int32) for edge in bucket_edges))
    return ahead + jnp.where(distance < 8, distance, beyond)


def dot_nn(left, right):
    return lax.dot_general(left, right, (((1,), (0,)), ((), ())), preferred_element_type=f32)


def dot_nt(left, right):
    return lax.dot_general(left, right, (((1,), (1,)), ((), ())), preferred_element_type=f32)


def dot_tn(left, right):
    return lax.dot_general(left, right, (((0,), (0,)), ((), ())), preferred_element_type=f32)


def rms_scale(values):
    return lax.rsqrt(jnp.mean(values * values, axis=-1, keepdims=True) + 1e-06)


def lasting(microseconds):
    return pl.CostEstimate(
        flops=int(microseconds * FLOPS_PER_US), bytes_accessed=0, transcendentals=0
    )


def whole(shape):
    return pl.BlockSpec(shape, lambda *_: (0,) * len(shape))


def params():
    return pltpu.CompilerParams(vmem_limit_bytes=VMEM_MOST)


def up_to(count, step):
    return -(-count // step) * step


def spread_width(width):
    return 2 * up_to(width // 2, 128)


def spread_rows(out, value, gain=None):
    half = value.shape[0] // 2
    each = out.shape[1] // 2
    nothing = jnp.zeros((out.shape[0], each - half), out.dtype)
    for index in range(2):
        part = value[index * half : (index + 1) * half].T
        if gain is not None:
            part = part * gain[:, index * half : (index + 1) * half]
        out[:, index * each : index * each + half] = part.astype(out.dtype)
        out[:, index * each + half : (index + 1) * each] = nothing


def spread_depth(value, wide):
    half = value.shape[0] // 2
    nothing = jnp.zeros((wide // 2 - half, value.shape[1]), value.dtype)
    return jnp.concatenate([value[:half], nothing, value[half:], nothing], 0)


def as_column(row):
    return jnp.broadcast_to(row, (128, row.shape[1])).T[:, :1]


def as_row(column):
    return jnp.broadcast_to(column, (column.shape[0], 128)).T[:1]


def shift_by_head(value):
    return pltpu.roll(value, DH, 1)


def columns(value, index):
    return value[:, index * PAIR : (index + 1) * PAIR]


def low_lanes(shape):
    return lax.broadcasted_iota(jnp.int32, shape, len(shape) - 1) % PAIR < DH


def packed_heads(query, keyval, half):
    low = low_lanes((query.shape[0], PAIR))
    key = [columns(keyval, i) for i in range(3)]
    value = [columns(keyval, i + 3) for i in range(3)]
    ask = [columns(query, i) for i in range(3)]
    if half == 0:
        parts = [
            key[0],
            jnp.where(low, key[1], shift_by_head(value[1])),
            value[0],
            ask[0],
            jnp.where(low, ask[1], 0.0),
        ]
    else:
        parts = [
            key[2],
            jnp.where(low, shift_by_head(key[1]), value[1]),
            value[2],
            ask[2],
            jnp.where(low, shift_by_head(ask[1]), 0.0),
        ]
    return jnp.concatenate(parts, 1).astype(bf16)


def open_kernel(
    spot_ref, inputs_ref, gain_ref, w_query_ref, w_keyval_ref, hidden_ref, mine_ref, other_ref
):
    inputs = inputs_ref[...].astype(f32)
    scale = lax.rsqrt(jnp.mean(inputs * inputs, axis=0, keepdims=True) + 1e-06)
    spread_rows(hidden_ref, inputs * scale, gain_ref[...])
    hidden = hidden_ref[...]
    wide = hidden.shape[1]
    keyval = dot_nn(hidden, spread_depth(w_keyval_ref[...], wide))
    query = dot_nn(hidden, spread_depth(w_query_ref[...], wide))
    first = packed_heads(query, keyval, 0)
    second = packed_heads(query, keyval, 1)

    @pl.when(spot_ref[0] == 0)
    def _():
        mine_ref[...] = first
        other_ref[...] = second

    @pl.when(spot_ref[0] != 0)
    def _():
        mine_ref[...] = second
        other_ref[...] = first


def opened(spot, inputs, gain, w_query, w_keyval):
    width, rows = inputs.shape
    inner = w_query.shape[1]
    pack = jax.ShapeDtypeStruct((rows, 5 * PAIR), bf16)
    return pl.pallas_call(
        open_kernel,
        grid_spec=pltpu.PrefetchScalarGridSpec(
            num_scalar_prefetch=1,
            grid=(1,),
            in_specs=[
                whole((width, rows)),
                whole((1, width)),
                whole((width, inner)),
                whole((width, 2 * inner)),
            ],
            out_specs=[
                whole((rows, spread_width(width))),
                whole(pack.shape),
                whole(pack.shape),
            ],
        ),
        out_shape=[jax.ShapeDtypeStruct((rows, spread_width(width)), bf16), pack, pack],
        compiler_params=params(),
        cost_estimate=lasting(5),
    )(spot, inputs, gain, w_query, w_keyval)


def turn_kernel(in_ref, out_ref):
    spread_rows(out_ref, in_ref[...])


def turned_rows(value):
    width, rows = value.shape
    return pl.pallas_call(
        turn_kernel,
        out_shape=jax.ShapeDtypeStruct((rows, spread_width(width)), value.dtype),
        compiler_params=params(),
        cost_estimate=lasting(2),
    )(value)


def bias_kernel(place_ref, by_shift_ref, out_ref):
    rows, keys = out_ref.shape[2:]
    wide = by_shift_ref.shape[-1]
    spread = jnp.broadcast_to(by_shift_ref[0, 0], (rows, wide))
    turned = pltpu.roll(spread, 0, 1, stride=1, stride_axis=0)[:, :keys]
    key = lax.broadcasted_iota(jnp.int32, (rows, keys), 1)
    length = place_ref[2 + pl.program_id(0)]
    out_ref[0, 0] = jnp.where(key < length * rows, turned, negative_fill)


def window_bias(place, by_shift, rows):
    keys = ITEM_MOST * rows
    both, heads, wide = by_shift.shape
    return pl.pallas_call(
        bias_kernel,
        grid_spec=pltpu.PrefetchScalarGridSpec(
            num_scalar_prefetch=1,
            grid=(both, heads),
            in_specs=[pl.BlockSpec((1, 1, 1, wide), lambda b, h, _: (b, h, 0, 0))],
            out_specs=pl.BlockSpec((1, 1, rows, keys), lambda b, h, _: (b, h, 0, 0)),
        ),
        out_shape=jax.ShapeDtypeStruct((both, heads, rows, keys), f32),
        compiler_params=params(),
        cost_estimate=lasting(6),
    )(place, by_shift.reshape(both, heads, 1, wide))


SLOTS = 2 * REACH + 2


def pair_kernel(spot_ref, mine_ref, got_ref, both_ref, first_ref, second_ref):
    rows = mine_ref.shape[0]
    wide = first_ref.shape[1]
    mine, got = mine_ref[:, :wide], got_ref[:, :wide]

    def put(first, second):
        first_ref[...] = first
        second_ref[...] = second
        both_ref[:rows, :] = first
        both_ref[rows:, :] = second

    @pl.when(spot_ref[0] == 0)
    def _():
        put(mine, got)

    @pl.when(spot_ref[0] != 0)
    def _():
        put(got, mine)


def paired(spot, mine, got):
    rows = mine.shape[0]
    shapes = [(2 * rows, 3 * PAIR), (rows, 3 * PAIR), (rows, 3 * PAIR)]
    return pl.pallas_call(
        pair_kernel,
        grid_spec=pltpu.PrefetchScalarGridSpec(
            num_scalar_prefetch=1,
            grid=(1,),
            in_specs=[whole(mine.shape)] * 2,
            out_specs=[whole(shape) for shape in shapes],
        ),
        out_shape=[jax.ShapeDtypeStruct(shape, bf16) for shape in shapes],
        compiler_params=params(),
        cost_estimate=lasting(1),
    )(spot, mine, got)


GROUPS = ((0, 2), (0, 2), (1, 1))


def spread_heads(own, mine, got):
    value = jnp.where(own, mine, got)
    first = columns(value, 0)
    low = low_lanes(first.shape)
    nothing = jnp.zeros_like(first)
    return jnp.where(low, first, nothing), jnp.where(low, nothing, first), columns(value, 1)


def attend_kernel(
    place_ref, mine_ref, got_ref, behind_far, behind, pair_ref, ahead, ahead_far, bias_ref,
    attended_mine, attended_other, prob_ref, window_ref
):
    rows = mine_ref.shape[0]
    wide = window_ref.shape[1]
    block = pl.program_id(0)
    own = block == place_ref[4]

    @pl.when(block == 0)
    def _():
        at = 0
        for piece in (behind_far, behind, pair_ref, ahead, ahead_far):
            window_ref[at : at + piece.shape[0], :] = piece[...]
            at += piece.shape[0]

    asks = spread_heads(own, mine_ref[:, wide:], got_ref[:, wide:])
    start = pl.multiple_of((REACH + block - place_ref[block]) * rows, rows)
    window = window_ref[pl.ds(start, ITEM_MOST * rows), :]
    parts = []
    for head, (key, value) in enumerate(GROUPS):
        scores = dot_nt(asks[head], columns(window, key)) + bias_ref[0, head]
        exponent = jnp.exp(scores - jnp.max(scores, axis=-1, keepdims=True))
        prob = exponent / jnp.sum(exponent, axis=-1, keepdims=True)
        prob_ref[0, head] = prob
        parts.append(dot_nn(prob.astype(bf16), columns(window, value)))

    def put(out):
        low = low_lanes((rows, PAIR))
        out[:PAIR, :] = jnp.where(low, parts[0], parts[1]).T.astype(bf16)
        out[PAIR:, :] = parts[2].T[DH:].astype(bf16)

    @pl.when(own)
    def _():
        put(attended_mine)

    @pl.when(jnp.logical_not(own))
    def _():
        put(attended_other)


def attend(place, mine, got, pieces, bias):
    rows = mine.shape[0]
    keys = ITEM_MOST * rows
    wide = pieces[0].shape[1]
    heads = bias.shape[1]
    tall = pl.BlockSpec((1, heads, rows, keys), lambda b, _: (b, 0, 0, 0))
    return pl.pallas_call(
        attend_kernel,
        grid_spec=pltpu.PrefetchScalarGridSpec(
            num_scalar_prefetch=1,
            grid=(2,),
            in_specs=[whole(mine.shape)] * 2 + [whole(piece.shape) for piece in pieces] + [tall],
            out_specs=[
                whole((heads * DH, rows)),
                whole((heads * DH, rows)),
                tall,
                whole((SLOTS * rows, wide)),
            ],
        ),
        out_shape=[
            jax.ShapeDtypeStruct((heads * DH, rows), bf16),
            jax.ShapeDtypeStruct((heads * DH, rows), bf16),
            jax.ShapeDtypeStruct((2, heads, rows, keys), f32),
            jax.ShapeDtypeStruct((SLOTS * rows, wide), bf16),
        ],
        compiler_params=params(),
        cost_estimate=lasting(9),
    )(place, mine, got, *pieces, bias)


def natural_heads(half, mine, other, out):
    each = mine.shape[0]

    def put(first, second):
        out[:each, :] = first[...]
        out[each : each + DH, :] = second[PAIR:, :]
        out[each + DH :, :] = second[:PAIR, :]

    @pl.when(half == 0)
    def _():
        put(mine, other)

    @pl.when(half != 0)
    def _():
        put(other, mine)


def middle_kernel(
    spot_ref, mine_ref, other_ref, inputs_ref, w_out_ref, gain_ref, middle_ref, hidden_ref, attended
):
    natural_heads(spot_ref[0], mine_ref, other_ref, attended)
    middle = inputs_ref[...].astype(f32) + dot_nn(w_out_ref[...], attended[...])
    middle_ref[...] = middle
    scale = lax.rsqrt(jnp.mean(middle * middle, axis=0, keepdims=True) + 1e-06)
    spread_rows(hidden_ref, middle * scale, gain_ref[...])


def middle_part(spot, mine, other, inputs, w_out, gain):
    width, rows = inputs.shape
    inner = w_out.shape[1]
    return pl.pallas_call(
        middle_kernel,
        grid_spec=pltpu.PrefetchScalarGridSpec(
            num_scalar_prefetch=1,
            grid=(1,),
            in_specs=[
                whole(mine.shape),
                whole(other.shape),
                whole((width, rows)),
                whole((width, inner)),
                whole((1, width)),
            ],
            out_specs=[whole((width, rows)), whole((rows, spread_width(width)))],
            scratch_shapes=[pltpu.VMEM((inner, rows), bf16)],
        ),
        out_shape=[
            jax.ShapeDtypeStruct((width, rows), f32),
            jax.ShapeDtypeStruct((rows, spread_width(width)), bf16),
        ],
        compiler_params=params(),
        cost_estimate=lasting(4),
    )(spot, mine, other, inputs, w_out, gain)


GELU_A = 0.7978845608028654
GELU_B = 0.044715


def packed_back(back, half):
    low = low_lanes((back.shape[0], PAIR))
    middle = columns(back, 1)
    if half == 0:
        parts = [columns(back, 0), jnp.where(low, 0.0, shift_by_head(middle))]
    else:
        parts = [columns(back, 2), jnp.where(low, 0.0, middle)]
    return jnp.concatenate(parts, 1).astype(bf16)


def ffn_kernel(last, spot_ref, hidden_ref, upstream_ref, gate_w_ref, up_w_ref, down_w_ref, *refs):
    if last:
        out_in, back_in, middle_ref, gain_ref, w_out_ref, cotangent_ref = refs[:6]
        (mixed_ref, both_ref, output_ref, gain_grad_ref, middle_back_ref,
         branch_ref, back_mine_ref, back_other_ref, out_ref, back_ref) = refs[6:]
    else:
        mixed_ref, both_ref, out_ref, back_ref = refs
    step = pl.program_id(0)
    units = gate_w_ref.shape[1]
    hidden = hidden_ref[...]
    wide = hidden.shape[1]
    upstream = upstream_ref[...]
    gateup_w = jnp.concatenate([gate_w_ref[...], up_w_ref[...]], 1)
    gateup = dot_nn(hidden, spread_depth(gateup_w, wide))
    gate, up = gateup[:, :units], gateup[:, units:]
    mixed_back = dot_nn(upstream, spread_depth(down_w_ref[...], wide))
    squared = gate * gate
    bent = jnp.tanh(GELU_A * (gate + GELU_B * (squared * gate)))
    share = 0.5 * (1.0 + bent)
    gelu = gate * share
    slope = share + 0.5 * gate * (1.0 - bent * bent) * (GELU_A * (1.0 + 3.0 * GELU_B * squared))
    mixed = (gelu * up).astype(bf16).T
    gate_back = (mixed_back * up * slope).astype(bf16).T
    up_back = (mixed_back * gelu).astype(bf16).T
    mixed_ref[...] = mixed
    both_ref[0] = gate_back
    both_ref[1] = up_back
    forward = dot_nn(down_w_ref[...], mixed)
    backward = dot_nn(gateup_w, jnp.concatenate([gate_back, up_back], 0))

    @pl.when(step == 0)
    def _():
        if last:
            out_ref[...] = out_in[...] + forward
            back_ref[...] = back_in[...] + backward
        else:
            out_ref[...] = forward
            back_ref[...] = backward

    @pl.when(step > 0)
    def _():
        out_ref[...] += forward
        back_ref[...] += backward

    if not last:
        return

    @pl.when(step == pl.num_programs(0) - 1)
    def _():
        middle = middle_ref[...]
        output_ref[...] = (middle + out_ref[...]).astype(bf16)
        scale = lax.rsqrt(jnp.mean(middle * middle, axis=0, keepdims=True) + 1e-06)
        normed = middle * scale
        back = back_ref[...]
        gain_grad_ref[...] = as_row(jnp.sum(back * normed, axis=1, keepdims=True))
        normed_back = back * as_column(gain_ref[...])
        mean = jnp.mean(normed_back * normed, axis=0, keepdims=True)
        middle_back = cotangent_ref[...].astype(f32) + scale * (normed_back - normed * mean)
        middle_back_ref[...] = middle_back
        spread_rows(branch_ref, middle_back)
        attended_back = dot_nn(branch_ref[...], spread_depth(w_out_ref[...], wide))
        first = packed_back(attended_back, 0)
        second = packed_back(attended_back, 1)

        @pl.when(spot_ref[0] == 0)
        def _():
            back_mine_ref[...] = first
            back_other_ref[...] = second

        @pl.when(spot_ref[0] != 0)
        def _():
            back_mine_ref[...] = second
            back_other_ref[...] = first


def ffn_half(last, spot, hidden, upstream, w_gateup, w_down, more=()):
    rows, wide = hidden.shape
    width, units = w_down.shape
    steps = units // 2 // UNITS
    both = units // UNITS
    in_specs = [
        whole((rows, wide)),
        whole((rows, wide)),
        pl.BlockSpec((width, UNITS), lambda j, s: (0, s[1] * steps + j)),
        pl.BlockSpec((width, UNITS), lambda j, s: (0, both + s[1] * steps + j)),
        pl.BlockSpec((width, UNITS), lambda j, s: (0, s[1] * steps + j)),
    ] + [whole(value.shape) for value in more]
    sums = [jax.ShapeDtypeStruct((width, rows), f32)] * 2
    out_specs = [
        pl.BlockSpec((UNITS, rows), lambda j, s: (j, 0)),
        pl.BlockSpec((2, UNITS, rows), lambda j, s: (0, j, 0)),
    ]
    out_shape = [
        jax.ShapeDtypeStruct((units // 2, rows), bf16),
        jax.ShapeDtypeStruct((2, units // 2, rows), bf16),
    ]
    if last:
        rest = [
            jax.ShapeDtypeStruct((width, rows), bf16),
            jax.ShapeDtypeStruct((1, width), f32),
            jax.ShapeDtypeStruct((width, rows), f32),
            jax.ShapeDtypeStruct((rows, wide), bf16),
            jax.ShapeDtypeStruct((rows, 2 * PAIR), bf16),
            jax.ShapeDtypeStruct((rows, 2 * PAIR), bf16),
        ]
    else:
        rest = sums
    return pl.pallas_call(
        functools.partial(ffn_kernel, last),
        grid_spec=pltpu.PrefetchScalarGridSpec(
            num_scalar_prefetch=1,
            grid=(steps,),
            in_specs=in_specs,
            out_specs=out_specs + [whole(value.shape) for value in rest],
            scratch_shapes=[pltpu.VMEM((width, rows), f32)] * 2 if last else [],
        ),
        out_shape=out_shape + rest,
        compiler_params=params(),
        cost_estimate=lasting(20),
    )(spot, hidden, upstream, w_gateup, w_gateup, w_down, *more)


def half_of(ref, index):
    each = ref.shape[1] // 2
    return ref[:, pl.ds(pl.multiple_of(index * each, 128), each)]


def pair_grad_kernel(
    parts, spot_ref, left_own, left_other, left_far, right_own, right_far, *refs
):
    outs, halves = refs[:-1], refs[-1]
    rows = left_far.shape[-1]
    mine = spot_ref[0]

    @pl.when(pl.program_id(0) == 0)
    def _():
        for index, right in enumerate((right_own, right_far)):
            at = slice(index * rows, (index + 1) * rows)
            halves[0, at, :] = half_of(right, mine)
            halves[1, at, :] = half_of(right, 1 - mine)

    own = left_own[0] if left_other is None else jnp.where(spot_ref[1] != 0, left_own[0], left_other[0])
    left = jnp.concatenate([own, left_far[0]], 1)
    each = left.shape[0] // parts
    for half in range(2):
        product = dot_nn(left, halves[half]).astype(bf16)
        for part in range(parts):
            outs[2 * part + half][...] = product[part * each : (part + 1) * each]


def pair_grad(spot, tiles, tile, parts, left_own, left_far, right_own, right_far):
    count, place = tiles
    rows = left_far.shape[-1]
    wide = right_own.shape[1] // 2
    each = tile // parts
    out = jax.ShapeDtypeStruct((count * each, wide), bf16)
    left = pl.BlockSpec((1, tile, rows), lambda j, _: (*place(j), 0))

    def kernel(spot_ref, *refs):
        if len(left_own) == 1:
            pair_grad_kernel(parts, spot_ref, refs[0], None, *refs[1:])
        else:
            pair_grad_kernel(parts, spot_ref, *refs)

    return pl.pallas_call(
        kernel,
        grid_spec=pltpu.PrefetchScalarGridSpec(
            num_scalar_prefetch=1,
            grid=(count,),
            in_specs=[left] * (len(left_own) + 1) + [whole(right_own.shape), whole(right_far.shape)],
            out_specs=[pl.BlockSpec((each, wide), lambda j, _: (j, 0))] * (2 * parts),
            scratch_shapes=[pltpu.VMEM((2, 2 * rows, wide), bf16)],
        ),
        out_shape=[out] * (2 * parts),
        compiler_params=params(),
        cost_estimate=lasting(8),
    )(spot, *left_own, left_far, right_own, right_far)


def quad_grad_kernel(
    parts, spot_ref, left_own, left_far, left_own_got, left_far_got, *refs
):
    rights, outs, halves = refs[:4], refs[4:-1], refs[-1]
    rows = left_own.shape[-1]
    mine = spot_ref[0]

    @pl.when((pl.program_id(0) == 0) & (pl.program_id(1) == 0))
    def _():
        for index, right in enumerate(rights):
            at = slice(index * rows, (index + 1) * rows)
            halves[0, at, :] = half_of(right, mine)
            halves[1, at, :] = half_of(right, 1 - mine)

    left = jnp.concatenate([left_own[0], left_far[0], left_own_got[0], left_far_got[0]], 1)
    each = left.shape[0] // parts
    for half in range(2):
        product = dot_nn(left, halves[half]).astype(bf16)
        for part in range(parts):
            outs[2 * part + half][...] = product[part * each : (part + 1) * each]


def quad_grad(spot, owned, parts, lefts, lefts_got, rights):
    groups, units, rows = lefts_got[0].shape
    wide = rights[0].shape[1] // 2
    runs = units // owned
    each = owned // parts
    out = jax.ShapeDtypeStruct((groups * runs * each, wide), bf16)
    return pl.pallas_call(
        functools.partial(quad_grad_kernel, parts),
        grid_spec=pltpu.PrefetchScalarGridSpec(
            num_scalar_prefetch=1,
            grid=(groups, runs),
            in_specs=[pl.BlockSpec((1, owned, rows), lambda g, j, s: (g, 2 * j + s[1], 0))] * 2
            + [pl.BlockSpec((1, owned, rows), lambda g, j, s: (g, j, 0))] * 2
            + [whole(right.shape) for right in rights],
            out_specs=[pl.BlockSpec((each, wide), lambda g, j, s: (g * runs + j, 0))] * (2 * parts),
            scratch_shapes=[pltpu.VMEM((2, 4 * rows, wide), bf16)],
        ),
        out_shape=[out] * (2 * parts),
        compiler_params=params(),
        cost_estimate=lasting(12),
    )(spot, *lefts, *lefts_got, *rights)


def heads_grad_kernel(
    spot_ref, keyval_ref, query_ref, attended_own, attended_far, hidden_own, hidden_far, branch_own,
    branch_far, kept_ref, sent_ref, low, high, left
):
    rows = hidden_own.shape[0]
    mine, half = spot_ref[0], spot_ref[1]
    each = query_ref.shape[1]

    def ordered(source, at, first, second):
        @pl.when(half == 0)
        def _():
            for start, stop, to in first:
                left[at + to : at + to + stop - start, :] = source(start, stop)

        @pl.when(half != 0)
        def _():
            for start, stop, to in second:
                left[at + to : at + to + stop - start, :] = source(start, stop)

    same = ((0, 3 * DH, 0),)
    turned = ((PAIR, 3 * DH, 0), (0, PAIR, DH))
    value_first = ((4 * DH, 6 * DH, 0), (3 * DH, 4 * DH, PAIR))
    value_second = ((3 * DH, 6 * DH, 0),)

    def joined(ref):
        return lambda start, stop: jnp.concatenate(
            [ref[0, start:stop, :], ref[1, start:stop, :]], 1
        )

    def plain(start, stop):
        return keyval_ref[start:stop, :]

    ordered(joined(query_ref), 0, same, turned)
    ordered(plain, each, same, turned)
    ordered(plain, 2 * each, value_first, value_second)

    def by_side(start, stop):
        own, far = attended_own[start:stop, :], attended_far[start:stop, :]
        first = jnp.where(half == 0, own, far)
        second = jnp.where(half == 0, far, own)
        return jnp.concatenate([first, second], 1)

    ordered(by_side, 3 * each, same, turned)
    for own, far, at, stop in (
        (hidden_own, hidden_far, 0, 3 * each),
        (branch_own, branch_far, 3 * each, 4 * each),
    ):
        for index, source in ((0, own), (1, far)):

            @pl.when(half == index)
            def _():
                low[:rows, :] = half_of(source, mine)
                high[:rows, :] = half_of(source, 1 - mine)

            @pl.when(half != index)
            def _():
                low[rows:, :] = half_of(source, mine)
                high[rows:, :] = half_of(source, 1 - mine)

        kept_ref[at:stop, :] = dot_nn(left[at:stop, :], low[...]).astype(bf16)
        sent_ref[at:stop, :] = dot_nn(left[at:stop, :], high[...]).astype(bf16)


def heads_grad(spot, keyval, query, attended, hiddens, branches):
    wide = hiddens[0].shape[1] // 2
    rows = hiddens[0].shape[0]
    each = query.shape[1]
    out = jax.ShapeDtypeStruct((4 * each, wide), bf16)
    operands = (keyval, query, *attended, *hiddens, *branches)
    return pl.pallas_call(
        heads_grad_kernel,
        grid_spec=pltpu.PrefetchScalarGridSpec(
            num_scalar_prefetch=1,
            grid=(1,),
            in_specs=[whole(value.shape) for value in operands],
            out_specs=[whole(out.shape)] * 2,
            scratch_shapes=[pltpu.VMEM((2 * rows, wide), bf16)] * 2
            + [pltpu.VMEM((4 * each, 2 * rows), bf16)],
        ),
        out_shape=[out, out],
        compiler_params=params(),
        cost_estimate=lasting(7),
    )(spot, *operands)


def attend_back_kernel(
    place_ref, mine_ref, got_ref, window_ref, prob_ref, back_mine, back_got, query_back_ref,
    by_shift_ref, behind_far, behind, pair_ref, ahead, ahead_far, total
):
    rows = mine_ref.shape[0]
    wide = window_ref.shape[1]
    keys = ITEM_MOST * rows
    block = pl.program_id(0)
    own = block == place_ref[4]
    asks = spread_heads(own, mine_ref[:, wide:], got_ref[:, wide:])
    backs = spread_heads(own, back_mine[...], back_got[...])

    @pl.when(block == 0)
    def _():
        total[...] = jnp.zeros_like(total)

    start = pl.multiple_of((REACH + block - place_ref[block]) * rows, rows)
    window = window_ref[pl.ds(start, keys), :]
    row = lax.broadcasted_iota(jnp.int32, (rows, rows), 0)
    column = lax.broadcasted_iota(jnp.int32, (rows, rows), 1)
    flip = jnp.where(row + column == rows - 1, 1.0, 0.0).astype(bf16)
    parts, sums = [], [None] * 3
    for head, (key, value) in enumerate(GROUPS):
        prob = prob_ref[0, head]
        prob_back = dot_nt(backs[head], columns(window, value))
        delta = jnp.sum(prob * prob_back, axis=-1, keepdims=True)
        score_back = (prob * (prob_back - delta)).astype(bf16)
        parts.append(dot_nn(score_back, columns(window, key)))
        key_part = dot_tn(asks[head], score_back)
        value_part = dot_tn(backs[head], prob.astype(bf16))
        for group, add in ((key, key_part), (value, value_part)):
            sums[group] = add if sums[group] is None else sums[group] + add
        flipped = jnp.concatenate([dot_nn(flip, score_back), jnp.zeros((rows, rows), f32)], 1)
        turned = pltpu.roll(flipped, keys + 1, 1, stride=1, stride_axis=0)
        by_shift_ref[0, head] = jnp.sum(turned, axis=0, keepdims=True)
    low = low_lanes((rows, PAIR))
    query_back_ref[0, :PAIR, :] = jnp.where(low, parts[0], parts[1]).T.astype(bf16)
    query_back_ref[0, PAIR:, :] = parts[2].T[:DH].astype(bf16)
    for group in range(3):
        total[group * PAIR : (group + 1) * PAIR, pl.ds(start, keys)] += sums[group]

    @pl.when(block == 1)
    def _():
        at = 0
        for out in (behind_far, behind, pair_ref, ahead, ahead_far):
            out[...] = total[:, at : at + out.shape[1]].astype(out.dtype)
            at += out.shape[1]


def attend_back(place, mine, got, window, prob, back_mine, back_got):
    rows = mine.shape[0]
    _, heads, _, keys = prob.shape
    wide = window.shape[1]
    pieces = [(rows, bf16), (2 * rows, bf16), (2 * rows, f32), (2 * rows, bf16), (rows, bf16)]
    return pl.pallas_call(
        attend_back_kernel,
        grid_spec=pltpu.PrefetchScalarGridSpec(
            num_scalar_prefetch=1,
            grid=(2,),
            in_specs=[
                whole(mine.shape),
                whole(got.shape),
                whole(window.shape),
                pl.BlockSpec((1, heads, rows, keys), lambda b, _: (b, 0, 0, 0)),
                whole(back_mine.shape),
                whole(back_got.shape),
            ],
            out_specs=[
                pl.BlockSpec((1, heads * DH, rows), lambda b, _: (b, 0, 0)),
                pl.BlockSpec((1, heads, 1, keys + rows), lambda b, _: (b, 0, 0, 0)),
            ]
            + [whole((wide, count)) for count, _ in pieces],
            scratch_shapes=[
                pltpu.VMEM((wide, SLOTS * rows), f32),
            ],
        ),
        out_shape=[
            jax.ShapeDtypeStruct((2, heads * DH, rows), bf16),
            jax.ShapeDtypeStruct((2, heads, 1, keys + rows), f32),
        ]
        + [jax.ShapeDtypeStruct((wide, count), dtype) for count, dtype in pieces],
        compiler_params=params(),
        cost_estimate=lasting(12),
    )(place, mine, got, window, prob, back_mine, back_got)


def gather_kernel(
    spot_ref, pair_ref, behind, ahead, behind_far, ahead_far, query_ref, both_ref, mine_ref,
    other_ref
):
    rows = behind_far.shape[1]
    wide = pair_ref.shape[0]
    total = pair_ref[...] + behind[...].astype(f32) + ahead[...].astype(f32)
    first = (total[:, :rows] + behind_far[...].astype(f32)).astype(bf16)
    second = (total[:, rows:] + ahead_far[...].astype(f32)).astype(bf16)
    both_ref[:, :rows] = first
    both_ref[:, rows:] = second

    @pl.when(spot_ref[0] == 0)
    def _():
        mine_ref[:wide, :] = first
        other_ref[:wide, :] = second
        mine_ref[wide:, :] = query_ref[0]
        other_ref[wide:, :] = query_ref[1]

    @pl.when(spot_ref[0] != 0)
    def _():
        mine_ref[:wide, :] = second
        other_ref[:wide, :] = first
        mine_ref[wide:, :] = query_ref[1]
        other_ref[wide:, :] = query_ref[0]


def gathered(spot, pair, behind, ahead, behind_far, ahead_far, query):
    wide, rows = behind_far.shape
    operands = (pair, behind, ahead, behind_far, ahead_far, query)
    pack = jax.ShapeDtypeStruct((wide + query.shape[1], rows), bf16)
    both = jax.ShapeDtypeStruct((wide, 2 * rows), bf16)
    return pl.pallas_call(
        gather_kernel,
        grid_spec=pltpu.PrefetchScalarGridSpec(
            num_scalar_prefetch=1,
            grid=(1,),
            in_specs=[whole(value.shape) for value in operands],
            out_specs=[whole(both.shape), whole(pack.shape), whole(pack.shape)],
        ),
        out_shape=[both, pack, pack],
        compiler_params=params(),
        cost_estimate=lasting(3),
    )(spot, *operands)


def close_kernel(
    spot_ref, mine_ref, other_ref, inputs_ref, middle_back_ref, w_query_ref, w_keyval_ref,
    gain_ref, input_back_ref, gain_grad_ref, query_back, keyval_back
):
    inner = query_back.shape[0]
    each = inner // 2

    def put(first, second):
        keyval_back[:each, :] = first[:each, :]
        keyval_back[each : each + DH, :] = second[PAIR : PAIR + DH, :]
        keyval_back[each + DH : inner, :] = second[:PAIR, :]
        keyval_back[inner : inner + PAIR, :] = first[4 * DH : 6 * DH, :]
        keyval_back[inner + PAIR : inner + each, :] = first[3 * DH : 4 * DH, :]
        keyval_back[inner + each :, :] = second[3 * DH : 6 * DH, :]
        query_back[:each, :] = first[inner:, :]
        query_back[each : each + DH, :] = second[inner + PAIR :, :]
        query_back[each + DH :, :] = second[inner : inner + PAIR, :]

    @pl.when(spot_ref[0] == 0)
    def _():
        put(mine_ref, other_ref)

    @pl.when(spot_ref[0] != 0)
    def _():
        put(other_ref, mine_ref)

    inputs = inputs_ref[...].astype(f32)
    scale = lax.rsqrt(jnp.mean(inputs * inputs, axis=0, keepdims=True) + 1e-06)
    normed = inputs * scale
    back = dot_nn(w_query_ref[...], query_back[...]) + dot_nn(w_keyval_ref[...], keyval_back[...])
    gain_grad_ref[...] = as_row(jnp.sum(back * normed, axis=1, keepdims=True))
    normed_back = back * as_column(gain_ref[...])
    mean = jnp.mean(normed_back * normed, axis=0, keepdims=True)
    input_back_ref[...] = (
        middle_back_ref[...] + scale * (normed_back - normed * mean)
    ).astype(bf16)


def closed(spot, mine, other, inputs, middle_back, w_query, w_keyval, gain):
    width, rows = inputs.shape
    inner = w_query.shape[1]
    operands = (mine, other, inputs, middle_back, w_query, w_keyval, gain)
    return pl.pallas_call(
        close_kernel,
        grid_spec=pltpu.PrefetchScalarGridSpec(
            num_scalar_prefetch=1,
            grid=(1,),
            in_specs=[whole(value.shape) for value in operands],
            out_specs=[whole((width, rows)), whole((1, width))],
            scratch_shapes=[
                pltpu.VMEM((inner, rows), bf16),
                pltpu.VMEM((2 * inner, rows), bf16),
            ],
        ),
        out_shape=[
            jax.ShapeDtypeStruct((width, rows), bf16),
            jax.ShapeDtypeStruct((1, width), f32),
        ],
        compiler_params=params(),
        cost_estimate=lasting(6),
    )(spot, *operands)


def swapped(value, axis, bit):
    size = lax.axis_size(axis)
    return lax.ppermute(value, axis, [(i, i ^ bit) for i in range(size)])


def passed_along(value, axis, by):
    size = lax.axis_size(axis)
    pairs = [(i, i + by) for i in range(size) if 0 <= i + by < size]
    return lax.ppermute(value, axis, pairs)


def of_both(value, bit):
    size = lax.axis_size("seq")
    groups = [[i, i | bit] for i in range(size) if not i & bit]
    return lax.all_gather(value, "seq", axis=0, tiled=True, axis_index_groups=groups)


def chosen(value, dim, index):
    return lax.dynamic_index_in_dim(value, index, dim, keepdims=False)


def added(left, right):
    return (left.astype(f32) + right.astype(f32)).astype(bf16)


def parted(state, dims, bit):
    left, right = state
    dim = dims.index(bit)
    mine = (lax.axis_index("seq") // bit) % 2
    kept = added(chosen(left, dim, mine), chosen(right, dim, mine))
    sent = added(chosen(left, dim, 1 - mine), chosen(right, dim, 1 - mine))
    return kept, sent, dims[:dim] + dims[dim + 1 :]


def after(value, *others):
    return lax.optimization_barrier((value, *others))[0]


class Halving:
    def __init__(self, state, dims, order):
        self.kept, self.got = state
        self.dims, self.order = dims, list(order)

    def step(self, earlier):
        bit = self.order.pop(0)
        got = after(self.got, earlier)
        self.kept, sent, self.dims = parted((self.kept, got), self.dims, bit)
        self.got = swapped(sent, "seq", bit)
        return sent

    def total(self, dtype=bf16):
        return (self.kept.astype(f32) + self.got.astype(f32)).astype(dtype)


def on_device(
    tokens,
    cotangent,
    item_lengths,
    gain_attn,
    gain_ffn,
    rel_table,
    w_query,
    w_keyval,
    w_out,
    w_gateup,
    w_down,
):
    rows = tokens.shape[1]
    width = tokens.shape[2]
    part = width // 2
    inner = w_query.shape[1]
    blocks = lax.axis_size("seq")
    me = lax.axis_index("seq")
    core = lax.axis_index("dp").astype(jnp.int32)
    top, pair, third = blocks // 2, blocks // 4, blocks // 8
    low = [1 << i for i in range(blocks.bit_length() - 1)][:-2]

    inputs = tokens[0].T
    cotangent = cotangent[0].T
    w_out = w_out.T
    w_down = w_down.T
    gain_attn = gain_attn[None]
    gain_ffn = gain_ffn[None]

    def bit_of(bit):
        return ((me // bit) % 2).astype(jnp.int32)

    side = bit_of(1)
    half = bit_of(pair)
    down_half = bit_of(third)

    hidden_one, mine, other = opened(side[None], inputs, gain_attn, w_query, w_keyval)
    got = swapped(other, "seq", 1)
    blocks_here = me - side + jnp.arange(2, dtype=jnp.int32)
    ends = jnp.cumsum(item_lengths[0])
    own = jnp.sum((ends[None, :] <= blocks_here[:, None]).astype(jnp.int32), 1)
    labels = jnp.arange(item_lengths.shape[1], dtype=jnp.int32)
    mark = labels[None, :] == own[:, None]
    length = jnp.sum(jnp.where(mark, item_lengths[0][None, :], 0), 1)
    end = jnp.sum(jnp.where(mark, ends[None, :], 0), 1)
    place = jnp.concatenate([blocks_here - (end - length), length, side[None]]).astype(jnp.int32)
    keys = ITEM_MOST * rows
    turns = keys + rows
    shift = jnp.arange(turns, dtype=jnp.int32)
    relative = jnp.where(shift < keys, shift, shift - turns)[None, :] - place[:2, None] * rows
    onehot = (
        bucket_of(relative)[:, :, None] == jnp.arange(BUCKETS, dtype=jnp.int32)[None, None, :]
    ).astype(f32)
    table = jnp.where(
        side == 0,
        rel_table[:, :3],
        jnp.concatenate([rel_table[:, 4:6], rel_table[:, 3:4]], 1),
    )
    by_shift = jnp.sum(onehot[:, None] * table.T[None, :, None, :], -1)
    bias = window_bias(place, by_shift, rows)

    got = after(got, bias)
    keyvals, first, second = paired(side[None], mine, got)
    pieces = [
        passed_along(second, "seq", 4),
        passed_along(keyvals, "seq", 2),
        keyvals,
        passed_along(keyvals, "seq", -2),
        passed_along(first, "seq", -4),
    ]

    attended, attended_other, prob, window = attend(place, mine, got, pieces, bias)
    attended_got = swapped(attended_other, "seq", 1)
    upstream = turned_rows(after(cotangent, attended))
    middle, hidden_two = middle_part(
        side[None], attended, attended_got, inputs, w_out, gain_ffn
    )
    hidden_far = swapped(hidden_two, "seq", pair)
    hidden_got = swapped(hidden_two, "seq", 1)
    hidden_far_got = swapped(hidden_far, "seq", 1)
    upstream_far = swapped(upstream, "seq", third)
    hidden_one_far = swapped(hidden_one, "seq", 1)

    mixed_first, back_first, *sums = ffn_half(
        False, jnp.stack([side, 1 - half]), hidden_two, upstream, w_gateup, w_down
    )
    back_far = swapped(back_first, "seq", pair)
    sums = after(tuple(sums), hidden_far, upstream_far, hidden_got)
    mixed_second, back, output, gain_ffn_grad, middle_back, branch, back_mine, back_other = ffn_half(
        True,
        jnp.stack([side, half]),
        hidden_two,
        upstream,
        w_gateup,
        w_down,
        (*sums, middle, gain_ffn, w_out, cotangent),
    )
    same = half == down_half
    mixed_far = swapped(jnp.where(same, mixed_first, mixed_second), "seq", third)
    back_got = swapped(back_other, "seq", 1)
    branch_far = swapped(after(branch, back_got), "seq", 1)
    back_mine = after(back_mine, hidden_one_far, hidden_far_got)

    backs = attend_back(place, mine, got, window, prob, back_mine, back_got)
    query_back, shift_sums = backs[:2]
    sends = backs[2:]

    def over_dp(kept, sent, dims):
        got = swapped(sent, "dp", 1)
        return tuple(
            value.reshape((2,) * dims + (value.shape[0] >> dims, value.shape[1]))
            for value in (kept, got)
        )

    spot = jnp.stack([core, side])
    units = mixed_first.shape[0]
    owned = units * 4 // blocks
    parts = 2 if owned % 32 == 0 else 1

    def other_owners(value):
        value = value.reshape(2, units // owned // 2, 2, owned, rows)
        return chosen(value, 2, 1 - side).reshape(2, units // 2, rows)

    back_got = swapped(other_owners(back), "seq", 1)
    back_far_sent = other_owners(back_far)
    back_far_got = swapped(back_far_sent, "seq", 1)
    down_kept, down_sent = pair_grad(
        jnp.stack([core, same.astype(jnp.int32)]),
        (2, lambda j: (0, j)),
        units // 2,
        1,
        (after(mixed_second, query_back, back_got, back_far_sent)[None], mixed_first[None]),
        mixed_far[None],
        upstream,
        upstream_far,
    )
    down = Halving(
        over_dp(down_kept, down_sent, len(low) + 1),
        [pair, top] + low[-2::-1],
        [pair] + low[-2::-1] + [top],
    )
    sent = down.step(down_kept)
    near_kept, near_sent, *far_grads = quad_grad(
        spot,
        owned,
        parts,
        (after(back, sent), back_far),
        (back_got, back_far_got),
        (hidden_two, hidden_far, hidden_got, hidden_far_got),
    )
    keyval_back, to_close, to_swap = gathered(
        side[None],
        after(sends[2], near_kept),
        passed_along(sends[3], "seq", 2),
        passed_along(sends[1], "seq", -2),
        passed_along(sends[4], "seq", 4),
        passed_along(sends[0], "seq", -4),
        query_back,
    )
    closed_with = swapped(to_swap, "seq", 1)
    gate_dims = [top] + low[:0:-1]
    gate_order = low[:0:-1] + [top]
    near = Halving(over_dp(near_kept, near_sent, len(low)), gate_dims, gate_order)
    far = None
    if parts == 2:
        far = Halving(over_dp(*far_grads, len(low)), gate_dims, gate_order)
    sent = keyval_back
    sent = near.step(sent)
    head_kept, head_sent = heads_grad(
        jnp.stack([core, side]),
        after(keyval_back, sent),
        query_back,
        (attended, attended_other),
        (hidden_one, hidden_one_far),
        (branch, branch_far),
    )
    others = [top, pair] + low[:0:-1]
    count = len(others)
    each = inner // 2

    def by_owner(value):
        def cut(array, bits):
            array = array.reshape((2,) * count + (-1, array.shape[-1]))
            return array.transpose([bits.index(bit) for bit in others] + [count, count + 1])

        asks = [pair] + low[:0:-1] + [top]
        keyvals = [top] + low[:0:-1] + [pair]
        return jnp.concatenate(
            [
                cut(value[:each], asks),
                cut(value[3 * each :], asks),
                cut(value[each : 3 * each], keyvals),
            ],
            -2,
        )

    head = Halving(
        (by_owner(head_kept), by_owner(swapped(head_sent, "dp", 1))),
        others,
        [pair] + low[1:] + [top],
    )
    sent = head_kept
    sent = far.step(sent) if far else sent
    input_back, gain_attn_grad = closed(
        side[None],
        after(to_close, sent),
        closed_with,
        inputs,
        middle_back,
        w_query,
        w_keyval,
        gain_attn,
    )

    sums = jnp.einsum(
        "pmb,phm->bh", onehot, shift_sums[:, :, 0], precision=lax.Precision.HIGHEST
    )
    nothing = jnp.zeros_like(sums)
    table_local = jnp.where(
        side == 0,
        jnp.concatenate([sums, nothing], 1),
        jnp.concatenate([nothing, sums[:, 2:], sums[:, :2]], 1),
    )
    small = jnp.concatenate(
        [gain_attn_grad.reshape(-1), gain_ffn_grad.reshape(-1), table_local.reshape(-1)]
    )
    taken = small.shape[0]
    small = jnp.pad(small, (0, -taken % 128)).reshape(-1, 128)
    small_got = swapped(small, "dp", 1)
    sent = gain_attn_grad
    small_order = low + [pair, top]
    chains = [chain for chain in (head, down, near, far) if chain]
    while any(chain.order for chain in chains) or small_order:
        for chain in chains:
            if chain.order:
                sent = chain.step(sent)
            if small_order and chain in (head, near):
                small = small + after(small_got, sent)
                small_got = swapped(small, "seq", small_order.pop(0))
    small = small + after(small_got, sent)

    turn = [
        (i, (i & ~(top | third)) | (third if i & top else 0) | (top if i & third else 0))
        for i in range(blocks)
    ]
    down_grad = lax.ppermute(down.total(), "seq", turn).astype(f32)[:, :part]
    def exchanged(i, bit):
        return (i & ~(1 | bit)) | (1 if i & bit else 0) | (bit if i & 1 else 0)

    own_rows = inner // blocks
    head_sum = head.total()
    asks = lax.ppermute(
        head_sum[: 2 * own_rows], "seq", [(i, exchanged(i, top)) for i in range(blocks)]
    ).astype(f32)
    query_grad = asks[:own_rows, :part].T
    out_grad = asks[own_rows:, :part]
    keyval_grad = (
        lax.ppermute(
            head_sum[2 * own_rows :], "seq", [(i, exchanged(i, pair)) for i in range(blocks)]
        )
        .astype(f32)[:, :part]
        .T
    )
    gateup_grad = jnp.concatenate([one.total(f32)[:, :part].T for one in (near, far) if one], 1)
    small = small.reshape(-1)
    return (
        output.T[None],
        input_back.T[None],
        small[:width],
        small[width : 2 * width],
        small[2 * width : taken].reshape(BUCKETS, H),
        query_grad,
        keyval_grad,
        out_grad,
        gateup_grad,
        down_grad,
    )


def solution(mesh):
    placed = (
        P("dp", "seq", None),
        P("dp", "seq", None),
        P("dp", None),
        P(),
        P(),
        P(),
        P(),
        P(),
        P(),
        P(),
        P(),
    )
    return jax.shard_map(
        on_device,
        mesh=mesh,
        in_specs=placed,
        out_specs=(
            P("dp", "seq", None),
            P("dp", "seq", None),
            P(),
            P(),
            P(),
            P("dp", "seq"),
            P("dp", "seq"),
            P("seq", "dp"),
            P("dp", "seq"),
            P("seq", "dp"),
        ),
        check_vma=False,
    )
```

```python
import functools

import jax
import jax.numpy as jnp
from jax import lax
from jax.experimental import pallas as pl
from jax.experimental.pallas import tpu as pltpu
from jax.sharding import PartitionSpec as P

H = 6
DH = 64
BUCKETS = 32
ITEM_MOST = 4
REACH = ITEM_MOST - 1
PAIR = 2 * DH
UNITS = 896

bucket_edges = (12, 16, 23, 32, 46, 64, 91)
negative_fill = -1e30
f32 = jnp.float32
bf16 = jnp.bfloat16
VMEM_MOST = 56 * 1024 * 1024
FLOPS_PER_US = 5_000_000_000


def bucket_of(relative):
    ahead = jnp.where(relative > 0, 16, 0).astype(jnp.int32)
    distance = jnp.abs(relative)
    beyond = 8 + sum(((distance >= edge).astype(jnp.int32) for edge in bucket_edges))
    return ahead + jnp.where(distance < 8, distance, beyond)


def dot_nn(left, right):
    return lax.dot_general(left, right, (((1,), (0,)), ((), ())), preferred_element_type=f32)


def dot_nt(left, right):
    return lax.dot_general(left, right, (((1,), (1,)), ((), ())), preferred_element_type=f32)


def dot_tn(left, right):
    return lax.dot_general(left, right, (((0,), (0,)), ((), ())), preferred_element_type=f32)


def rms_scale(values):
    return lax.rsqrt(jnp.mean(values * values, axis=-1, keepdims=True) + 1e-06)


def lasting(microseconds):
    return pl.CostEstimate(
        flops=int(microseconds * FLOPS_PER_US), bytes_accessed=0, transcendentals=0
    )


def whole(shape):
    return pl.BlockSpec(shape, lambda *_: (0,) * len(shape))


def params():
    return pltpu.CompilerParams(vmem_limit_bytes=VMEM_MOST)


def up_to(count, step):
    return -(-count // step) * step


def spread_width(width):
    return 2 * up_to(width // 2, 128)


def spread_rows(out, value, gain=None):
    half = value.shape[0] // 2
    each = out.shape[1] // 2
    nothing = jnp.zeros((out.shape[0], each - half), out.dtype)
    for index in range(2):
        part = value[index * half : (index + 1) * half].T
        if gain is not None:
            part = part * gain[:, index * half : (index + 1) * half]
        out[:, index * each : index * each + half] = part.astype(out.dtype)
        out[:, index * each + half : (index + 1) * each] = nothing


def spread_depth(value, wide):
    half = value.shape[0] // 2
    nothing = jnp.zeros((wide // 2 - half, value.shape[1]), value.dtype)
    return jnp.concatenate([value[:half], nothing, value[half:], nothing], 0)


def as_column(row):
    return jnp.broadcast_to(row, (128, row.shape[1])).T[:, :1]


def as_row(column):
    return jnp.broadcast_to(column, (column.shape[0], 128)).T[:1]


def shift_by_head(value):
    return pltpu.roll(value, DH, 1)


def columns(value, index):
    return value[:, index * PAIR : (index + 1) * PAIR]


def low_lanes(shape):
    return lax.broadcasted_iota(jnp.int32, shape, len(shape) - 1) % PAIR < DH


def packed_heads(query, keyval, half):
    low = low_lanes((query.shape[0], PAIR))
    key = [columns(keyval, i) for i in range(3)]
    value = [columns(keyval, i + 3) for i in range(3)]
    ask = [columns(query, i) for i in range(3)]
    if half == 0:
        parts = [
            key[0],
            jnp.where(low, key[1], shift_by_head(value[1])),
            value[0],
            ask[0],
            jnp.where(low, ask[1], 0.0),
        ]
    else:
        parts = [
            key[2],
            jnp.where(low, shift_by_head(key[1]), value[1]),
            value[2],
            ask[2],
            jnp.where(low, shift_by_head(ask[1]), 0.0),
        ]
    return jnp.concatenate(parts, 1).astype(bf16)


def open_kernel(
    spot_ref, inputs_ref, gain_ref, w_query_ref, w_keyval_ref, hidden_ref, mine_ref, other_ref
):
    inputs = inputs_ref[...].astype(f32)
    scale = lax.rsqrt(jnp.mean(inputs * inputs, axis=0, keepdims=True) + 1e-06)
    spread_rows(hidden_ref, inputs * scale, gain_ref[...])
    hidden = hidden_ref[...]
    wide = hidden.shape[1]
    keyval = dot_nn(hidden, spread_depth(w_keyval_ref[...], wide))
    query = dot_nn(hidden, spread_depth(w_query_ref[...], wide))
    first = packed_heads(query, keyval, 0)
    second = packed_heads(query, keyval, 1)

    @pl.when(spot_ref[0] == 0)
    def _():
        mine_ref[...] = first
        other_ref[...] = second

    @pl.when(spot_ref[0] != 0)
    def _():
        mine_ref[...] = second
        other_ref[...] = first


def opened(spot, inputs, gain, w_query, w_keyval):
    width, rows = inputs.shape
    inner = w_query.shape[1]
    pack = jax.ShapeDtypeStruct((rows, 5 * PAIR), bf16)
    return pl.pallas_call(
        open_kernel,
        grid_spec=pltpu.PrefetchScalarGridSpec(
            num_scalar_prefetch=1,
            grid=(1,),
            in_specs=[
                whole((width, rows)),
                whole((1, width)),
                whole((width, inner)),
                whole((width, 2 * inner)),
            ],
            out_specs=[
                whole((rows, spread_width(width))),
                whole(pack.shape),
                whole(pack.shape),
            ],
        ),
        out_shape=[jax.ShapeDtypeStruct((rows, spread_width(width)), bf16), pack, pack],
        compiler_params=params(),
        cost_estimate=lasting(5),
    )(spot, inputs, gain, w_query, w_keyval)


def turn_kernel(in_ref, out_ref):
    spread_rows(out_ref, in_ref[...])


def turned_rows(value):
    width, rows = value.shape
    return pl.pallas_call(
        turn_kernel,
        out_shape=jax.ShapeDtypeStruct((rows, spread_width(width)), value.dtype),
        compiler_params=params(),
        cost_estimate=lasting(2),
    )(value)


def bias_kernel(place_ref, by_shift_ref, out_ref):
    rows, keys = out_ref.shape[2:]
    wide = by_shift_ref.shape[-1]
    spread = jnp.broadcast_to(by_shift_ref[0, 0], (rows, wide))
    turned = pltpu.roll(spread, 0, 1, stride=1, stride_axis=0)[:, :keys]
    key = lax.broadcasted_iota(jnp.int32, (rows, keys), 1)
    length = place_ref[2 + pl.program_id(0)]
    out_ref[0, 0] = jnp.where(key < length * rows, turned, negative_fill)


def window_bias(place, by_shift, rows):
    keys = ITEM_MOST * rows
    both, heads, wide = by_shift.shape
    return pl.pallas_call(
        bias_kernel,
        grid_spec=pltpu.PrefetchScalarGridSpec(
            num_scalar_prefetch=1,
            grid=(both, heads),
            in_specs=[pl.BlockSpec((1, 1, 1, wide), lambda b, h, _: (b, h, 0, 0))],
            out_specs=pl.BlockSpec((1, 1, rows, keys), lambda b, h, _: (b, h, 0, 0)),
        ),
        out_shape=jax.ShapeDtypeStruct((both, heads, rows, keys), f32),
        compiler_params=params(),
        cost_estimate=lasting(6),
    )(place, by_shift.reshape(both, heads, 1, wide))


SLOTS = 2 * REACH + 2


def pair_kernel(spot_ref, mine_ref, got_ref, both_ref, first_ref, second_ref):
    rows = mine_ref.shape[0]
    wide = first_ref.shape[1]
    mine, got = mine_ref[:, :wide], got_ref[:, :wide]

    def put(first, second):
        first_ref[...] = first
        second_ref[...] = second
        both_ref[:rows, :] = first
        both_ref[rows:, :] = second

    @pl.when(spot_ref[0] == 0)
    def _():
        put(mine, got)

    @pl.when(spot_ref[0] != 0)
    def _():
        put(got, mine)


def paired(spot, mine, got):
    rows = mine.shape[0]
    shapes = [(2 * rows, 3 * PAIR), (rows, 3 * PAIR), (rows, 3 * PAIR)]
    return pl.pallas_call(
        pair_kernel,
        grid_spec=pltpu.PrefetchScalarGridSpec(
            num_scalar_prefetch=1,
            grid=(1,),
            in_specs=[whole(mine.shape)] * 2,
            out_specs=[whole(shape) for shape in shapes],
        ),
        out_shape=[jax.ShapeDtypeStruct(shape, bf16) for shape in shapes],
        compiler_params=params(),
        cost_estimate=lasting(1),
    )(spot, mine, got)


GROUPS = ((0, 2), (0, 2), (1, 1))


def spread_heads(own, mine, got):
    value = jnp.where(own, mine, got)
    first = columns(value, 0)
    low = low_lanes(first.shape)
    nothing = jnp.zeros_like(first)
    return jnp.where(low, first, nothing), jnp.where(low, nothing, first), columns(value, 1)


def attend_kernel(
    place_ref, mine_ref, got_ref, behind_far, behind, pair_ref, ahead, ahead_far, bias_ref,
    attended_mine, attended_other, prob_ref, window_ref
):
    rows = mine_ref.shape[0]
    wide = window_ref.shape[1]
    block = pl.program_id(0)
    own = block == place_ref[4]

    @pl.when(block == 0)
    def _():
        at = 0
        for piece in (behind_far, behind, pair_ref, ahead, ahead_far):
            window_ref[at : at + piece.shape[0], :] = piece[...]
            at += piece.shape[0]

    asks = spread_heads(own, mine_ref[:, wide:], got_ref[:, wide:])
    start = pl.multiple_of((REACH + block - place_ref[block]) * rows, rows)
    window = window_ref[pl.ds(start, ITEM_MOST * rows), :]
    parts = []
    for head, (key, value) in enumerate(GROUPS):
        scores = dot_nt(asks[head], columns(window, key)) + bias_ref[0, head]
        exponent = jnp.exp(scores - jnp.max(scores, axis=-1, keepdims=True))
        prob = exponent / jnp.sum(exponent, axis=-1, keepdims=True)
        prob_ref[0, head] = prob
        parts.append(dot_nn(prob.astype(bf16), columns(window, value)))

    def put(out):
        low = low_lanes((rows, PAIR))
        out[:PAIR, :] = jnp.where(low, parts[0], parts[1]).T.astype(bf16)
        out[PAIR:, :] = parts[2].T[DH:].astype(bf16)

    @pl.when(own)
    def _():
        put(attended_mine)

    @pl.when(jnp.logical_not(own))
    def _():
        put(attended_other)


def attend(place, mine, got, pieces, bias):
    rows = mine.shape[0]
    keys = ITEM_MOST * rows
    wide = pieces[0].shape[1]
    heads = bias.shape[1]
    tall = pl.BlockSpec((1, heads, rows, keys), lambda b, _: (b, 0, 0, 0))
    return pl.pallas_call(
        attend_kernel,
        grid_spec=pltpu.PrefetchScalarGridSpec(
            num_scalar_prefetch=1,
            grid=(2,),
            in_specs=[whole(mine.shape)] * 2 + [whole(piece.shape) for piece in pieces] + [tall],
            out_specs=[
                whole((heads * DH, rows)),
                whole((heads * DH, rows)),
                tall,
                whole((SLOTS * rows, wide)),
            ],
        ),
        out_shape=[
            jax.ShapeDtypeStruct((heads * DH, rows), bf16),
            jax.ShapeDtypeStruct((heads * DH, rows), bf16),
            jax.ShapeDtypeStruct((2, heads, rows, keys), f32),
            jax.ShapeDtypeStruct((SLOTS * rows, wide), bf16),
        ],
        compiler_params=params(),
        cost_estimate=lasting(9),
    )(place, mine, got, *pieces, bias)


def natural_heads(half, mine, other, out):
    each = mine.shape[0]

    def put(first, second):
        out[:each, :] = first[...]
        out[each : each + DH, :] = second[PAIR:, :]
        out[each + DH :, :] = second[:PAIR, :]

    @pl.when(half == 0)
    def _():
        put(mine, other)

    @pl.when(half != 0)
    def _():
        put(other, mine)


def middle_kernel(
    spot_ref, mine_ref, other_ref, inputs_ref, w_out_ref, gain_ref, middle_ref, hidden_ref, attended
):
    natural_heads(spot_ref[0], mine_ref, other_ref, attended)
    middle = inputs_ref[...].astype(f32) + dot_nn(w_out_ref[...], attended[...])
    middle_ref[...] = middle
    scale = lax.rsqrt(jnp.mean(middle * middle, axis=0, keepdims=True) + 1e-06)
    spread_rows(hidden_ref, middle * scale, gain_ref[...])


def middle_part(spot, mine, other, inputs, w_out, gain):
    width, rows = inputs.shape
    inner = w_out.shape[1]
    return pl.pallas_call(
        middle_kernel,
        grid_spec=pltpu.PrefetchScalarGridSpec(
            num_scalar_prefetch=1,
            grid=(1,),
            in_specs=[
                whole(mine.shape),
                whole(other.shape),
                whole((width, rows)),
                whole((width, inner)),
                whole((1, width)),
            ],
            out_specs=[whole((width, rows)), whole((rows, spread_width(width)))],
            scratch_shapes=[pltpu.VMEM((inner, rows), bf16)],
        ),
        out_shape=[
            jax.ShapeDtypeStruct((width, rows), f32),
            jax.ShapeDtypeStruct((rows, spread_width(width)), bf16),
        ],
        compiler_params=params(),
        cost_estimate=lasting(4),
    )(spot, mine, other, inputs, w_out, gain)


GELU_A = 0.7978845608028654
GELU_B = 0.044715


def packed_back(back, half):
    low = low_lanes((back.shape[0], PAIR))
    middle = columns(back, 1)
    if half == 0:
        parts = [columns(back, 0), jnp.where(low, 0.0, shift_by_head(middle))]
    else:
        parts = [columns(back, 2), jnp.where(low, 0.0, middle)]
    return jnp.concatenate(parts, 1).astype(bf16)


def ffn_kernel(last, spot_ref, hidden_ref, upstream_ref, gate_w_ref, up_w_ref, down_w_ref, *refs):
    if last:
        out_in, back_in, middle_ref, gain_ref, w_out_ref, cotangent_ref = refs[:6]
        (mixed_ref, both_ref, output_ref, gain_grad_ref, middle_back_ref,
         branch_ref, back_mine_ref, back_other_ref, out_ref, back_ref) = refs[6:]
    else:
        mixed_ref, both_ref, out_ref, back_ref = refs
    step = pl.program_id(0)
    units = gate_w_ref.shape[1]
    hidden = hidden_ref[...]
    wide = hidden.shape[1]
    upstream = upstream_ref[...]
    gateup_w = jnp.concatenate([gate_w_ref[...], up_w_ref[...]], 1)
    gateup = dot_nn(hidden, spread_depth(gateup_w, wide))
    gate, up = gateup[:, :units], gateup[:, units:]
    mixed_back = dot_nn(upstream, spread_depth(down_w_ref[...], wide))
    squared = gate * gate
    bent = jnp.tanh(GELU_A * (gate + GELU_B * (squared * gate)))
    share = 0.5 * (1.0 + bent)
    gelu = gate * share
    slope = share + 0.5 * gate * (1.0 - bent * bent) * (GELU_A * (1.0 + 3.0 * GELU_B * squared))
    mixed = (gelu * up).astype(bf16).T
    gate_back = (mixed_back * up * slope).astype(bf16).T
    up_back = (mixed_back * gelu).astype(bf16).T
    mixed_ref[...] = mixed
    both_ref[0] = gate_back
    both_ref[1] = up_back
    forward = dot_nn(down_w_ref[...], mixed)
    backward = dot_nn(gateup_w, jnp.concatenate([gate_back, up_back], 0))

    @pl.when(step == 0)
    def _():
        if last:
            out_ref[...] = out_in[...] + forward
            back_ref[...] = back_in[...] + backward
        else:
            out_ref[...] = forward
            back_ref[...] = backward

    @pl.when(step > 0)
    def _():
        out_ref[...] += forward
        back_ref[...] += backward

    if not last:
        return

    @pl.when(step == pl.num_programs(0) - 1)
    def _():
        middle = middle_ref[...]
        output_ref[...] = (middle + out_ref[...]).astype(bf16)
        scale = lax.rsqrt(jnp.mean(middle * middle, axis=0, keepdims=True) + 1e-06)
        normed = middle * scale
        back = back_ref[...]
        gain_grad_ref[...] = as_row(jnp.sum(back * normed, axis=1, keepdims=True))
        normed_back = back * as_column(gain_ref[...])
        mean = jnp.mean(normed_back * normed, axis=0, keepdims=True)
        middle_back = cotangent_ref[...].astype(f32) + scale * (normed_back - normed * mean)
        middle_back_ref[...] = middle_back
        spread_rows(branch_ref, middle_back)
        attended_back = dot_nn(branch_ref[...], spread_depth(w_out_ref[...], wide))
        first = packed_back(attended_back, 0)
        second = packed_back(attended_back, 1)

        @pl.when(spot_ref[0] == 0)
        def _():
            back_mine_ref[...] = first
            back_other_ref[...] = second

        @pl.when(spot_ref[0] != 0)
        def _():
            back_mine_ref[...] = second
            back_other_ref[...] = first


def ffn_half(last, spot, hidden, upstream, w_gateup, w_down, more=()):
    rows, wide = hidden.shape
    width, units = w_down.shape
    steps = units // 2 // UNITS
    both = units // UNITS
    in_specs = [
        whole((rows, wide)),
        whole((rows, wide)),
        pl.BlockSpec((width, UNITS), lambda j, s: (0, s[1] * steps + j)),
        pl.BlockSpec((width, UNITS), lambda j, s: (0, both + s[1] * steps + j)),
        pl.BlockSpec((width, UNITS), lambda j, s: (0, s[1] * steps + j)),
    ] + [whole(value.shape) for value in more]
    sums = [jax.ShapeDtypeStruct((width, rows), f32)] * 2
    out_specs = [
        pl.BlockSpec((UNITS, rows), lambda j, s: (j, 0)),
        pl.BlockSpec((2, UNITS, rows), lambda j, s: (0, j, 0)),
    ]
    out_shape = [
        jax.ShapeDtypeStruct((units // 2, rows), bf16),
        jax.ShapeDtypeStruct((2, units // 2, rows), bf16),
    ]
    if last:
        rest = [
            jax.ShapeDtypeStruct((width, rows), bf16),
            jax.ShapeDtypeStruct((1, width), f32),
            jax.ShapeDtypeStruct((width, rows), f32),
            jax.ShapeDtypeStruct((rows, wide), bf16),
            jax.ShapeDtypeStruct((rows, 2 * PAIR), bf16),
            jax.ShapeDtypeStruct((rows, 2 * PAIR), bf16),
        ]
    else:
        rest = sums
    return pl.pallas_call(
        functools.partial(ffn_kernel, last),
        grid_spec=pltpu.PrefetchScalarGridSpec(
            num_scalar_prefetch=1,
            grid=(steps,),
            in_specs=in_specs,
            out_specs=out_specs + [whole(value.shape) for value in rest],
            scratch_shapes=[pltpu.VMEM((width, rows), f32)] * 2 if last else [],
        ),
        out_shape=out_shape + rest,
        compiler_params=params(),
        cost_estimate=lasting(20),
    )(spot, hidden, upstream, w_gateup, w_gateup, w_down, *more)


def half_of(ref, index):
    each = ref.shape[1] // 2
    return ref[:, pl.ds(pl.multiple_of(index * each, 128), each)]


def pair_grad_kernel(
    parts, spot_ref, left_own, left_other, left_far, right_own, right_far, *refs
):
    outs, halves = refs[:-1], refs[-1]
    rows = left_far.shape[-1]
    mine = spot_ref[0]

    @pl.when(pl.program_id(0) == 0)
    def _():
        for index, right in enumerate((right_own, right_far)):
            at = slice(index * rows, (index + 1) * rows)
            halves[0, at, :] = half_of(right, mine)
            halves[1, at, :] = half_of(right, 1 - mine)

    own = left_own[0] if left_other is None else jnp.where(spot_ref[1] != 0, left_own[0], left_other[0])
    left = jnp.concatenate([own, left_far[0]], 1)
    each = left.shape[0] // parts
    for half in range(2):
        product = dot_nn(left, halves[half]).astype(bf16)
        for part in range(parts):
            outs[2 * part + half][...] = product[part * each : (part + 1) * each]


def pair_grad(spot, tiles, tile, parts, left_own, left_far, right_own, right_far):
    count, place = tiles
    rows = left_far.shape[-1]
    wide = right_own.shape[1] // 2
    each = tile // parts
    out = jax.ShapeDtypeStruct((count * each, wide), bf16)
    left = pl.BlockSpec((1, tile, rows), lambda j, _: (*place(j), 0))

    def kernel(spot_ref, *refs):
        if len(left_own) == 1:
            pair_grad_kernel(parts, spot_ref, refs[0], None, *refs[1:])
        else:
            pair_grad_kernel(parts, spot_ref, *refs)

    return pl.pallas_call(
        kernel,
        grid_spec=pltpu.PrefetchScalarGridSpec(
            num_scalar_prefetch=1,
            grid=(count,),
            in_specs=[left] * (len(left_own) + 1) + [whole(right_own.shape), whole(right_far.shape)],
            out_specs=[pl.BlockSpec((each, wide), lambda j, _: (j, 0))] * (2 * parts),
            scratch_shapes=[pltpu.VMEM((2, 2 * rows, wide), bf16)],
        ),
        out_shape=[out] * (2 * parts),
        compiler_params=params(),
        cost_estimate=lasting(24),
    )(spot, *left_own, left_far, right_own, right_far)


def quad_grad_kernel(
    parts, spot_ref, left_own, left_far, left_own_got, left_far_got, *refs
):
    rights, outs, halves = refs[:4], refs[4:-1], refs[-1]
    rows = left_own.shape[-1]
    mine = spot_ref[0]

    @pl.when((pl.program_id(0) == 0) & (pl.program_id(1) == 0))
    def _():
        for index, right in enumerate(rights):
            at = slice(index * rows, (index + 1) * rows)
            halves[0, at, :] = half_of(right, mine)
            halves[1, at, :] = half_of(right, 1 - mine)

    left = jnp.concatenate([left_own[0], left_far[0], left_own_got[0], left_far_got[0]], 1)
    each = left.shape[0] // parts
    for half in range(2):
        product = dot_nn(left, halves[half]).astype(bf16)
        for part in range(parts):
            outs[2 * part + half][...] = product[part * each : (part + 1) * each]


def quad_grad(spot, owned, parts, lefts, lefts_got, rights):
    groups, units, rows = lefts_got[0].shape
    wide = rights[0].shape[1] // 2
    runs = units // owned
    each = owned // parts
    out = jax.ShapeDtypeStruct((groups * runs * each, wide), bf16)
    return pl.pallas_call(
        functools.partial(quad_grad_kernel, parts),
        grid_spec=pltpu.PrefetchScalarGridSpec(
            num_scalar_prefetch=1,
            grid=(groups, runs),
            in_specs=[pl.BlockSpec((1, owned, rows), lambda g, j, s: (g, 2 * j + s[1], 0))] * 2
            + [pl.BlockSpec((1, owned, rows), lambda g, j, s: (g, j, 0))] * 2
            + [whole(right.shape) for right in rights],
            out_specs=[pl.BlockSpec((each, wide), lambda g, j, s: (g * runs + j, 0))] * (2 * parts),
            scratch_shapes=[pltpu.VMEM((2, 4 * rows, wide), bf16)],
        ),
        out_shape=[out] * (2 * parts),
        compiler_params=params(),
        cost_estimate=lasting(12),
    )(spot, *lefts, *lefts_got, *rights)


def heads_grad_kernel(
    spot_ref, keyval_ref, query_ref, attended_own, attended_far, hidden_own, hidden_far, branch_own,
    branch_far, kept_ref, sent_ref, low, high, left
):
    rows = hidden_own.shape[0]
    mine, half = spot_ref[0], spot_ref[1]
    each = query_ref.shape[1]

    def ordered(source, at, first, second):
        @pl.when(half == 0)
        def _():
            for start, stop, to in first:
                left[at + to : at + to + stop - start, :] = source(start, stop)

        @pl.when(half != 0)
        def _():
            for start, stop, to in second:
                left[at + to : at + to + stop - start, :] = source(start, stop)

    same = ((0, 3 * DH, 0),)
    turned = ((PAIR, 3 * DH, 0), (0, PAIR, DH))
    value_first = ((4 * DH, 6 * DH, 0), (3 * DH, 4 * DH, PAIR))
    value_second = ((3 * DH, 6 * DH, 0),)

    def joined(ref):
        return lambda start, stop: jnp.concatenate(
            [ref[0, start:stop, :], ref[1, start:stop, :]], 1
        )

    def plain(start, stop):
        return keyval_ref[start:stop, :]

    ordered(joined(query_ref), 0, same, turned)
    ordered(plain, each, same, turned)
    ordered(plain, 2 * each, value_first, value_second)

    def by_side(start, stop):
        own, far = attended_own[start:stop, :], attended_far[start:stop, :]
        first = jnp.where(half == 0, own, far)
        second = jnp.where(half == 0, far, own)
        return jnp.concatenate([first, second], 1)

    ordered(by_side, 3 * each, same, turned)
    for own, far, at, stop in (
        (hidden_own, hidden_far, 0, 3 * each),
        (branch_own, branch_far, 3 * each, 4 * each),
    ):
        for index, source in ((0, own), (1, far)):

            @pl.when(half == index)
            def _():
                low[:rows, :] = half_of(source, mine)
                high[:rows, :] = half_of(source, 1 - mine)

            @pl.when(half != index)
            def _():
                low[rows:, :] = half_of(source, mine)
                high[rows:, :] = half_of(source, 1 - mine)

        kept_ref[at:stop, :] = dot_nn(left[at:stop, :], low[...]).astype(bf16)
        sent_ref[at:stop, :] = dot_nn(left[at:stop, :], high[...]).astype(bf16)


def heads_grad(spot, keyval, query, attended, hiddens, branches):
    wide = hiddens[0].shape[1] // 2
    rows = hiddens[0].shape[0]
    each = query.shape[1]
    out = jax.ShapeDtypeStruct((4 * each, wide), bf16)
    operands = (keyval, query, *attended, *hiddens, *branches)
    return pl.pallas_call(
        heads_grad_kernel,
        grid_spec=pltpu.PrefetchScalarGridSpec(
            num_scalar_prefetch=1,
            grid=(1,),
            in_specs=[whole(value.shape) for value in operands],
            out_specs=[whole(out.shape)] * 2,
            scratch_shapes=[pltpu.VMEM((2 * rows, wide), bf16)] * 2
            + [pltpu.VMEM((4 * each, 2 * rows), bf16)],
        ),
        out_shape=[out, out],
        compiler_params=params(),
        cost_estimate=lasting(2.1),
    )(spot, *operands)


def attend_back_kernel(
    place_ref, mine_ref, got_ref, window_ref, prob_ref, back_mine, back_got, query_back_ref,
    by_shift_ref, behind_far, behind, pair_ref, ahead, ahead_far, total
):
    rows = mine_ref.shape[0]
    wide = window_ref.shape[1]
    keys = ITEM_MOST * rows
    block = pl.program_id(0)
    own = block == place_ref[4]
    asks = spread_heads(own, mine_ref[:, wide:], got_ref[:, wide:])
    backs = spread_heads(own, back_mine[...], back_got[...])

    @pl.when(block == 0)
    def _():
        total[...] = jnp.zeros_like(total)

    start = pl.multiple_of((REACH + block - place_ref[block]) * rows, rows)
    window = window_ref[pl.ds(start, keys), :]
    row = lax.broadcasted_iota(jnp.int32, (rows, rows), 0)
    column = lax.broadcasted_iota(jnp.int32, (rows, rows), 1)
    flip = jnp.where(row + column == rows - 1, 1.0, 0.0).astype(bf16)
    parts, sums = [], [None] * 3
    for head, (key, value) in enumerate(GROUPS):
        prob = prob_ref[0, head]
        prob_back = dot_nt(backs[head], columns(window, value))
        delta = jnp.sum(prob * prob_back, axis=-1, keepdims=True)
        score_back = (prob * (prob_back - delta)).astype(bf16)
        parts.append(dot_nn(score_back, columns(window, key)))
        key_part = dot_tn(asks[head], score_back)
        value_part = dot_tn(backs[head], prob.astype(bf16))
        for group, add in ((key, key_part), (value, value_part)):
            sums[group] = add if sums[group] is None else sums[group] + add
        flipped = jnp.concatenate([dot_nn(flip, score_back), jnp.zeros((rows, rows), f32)], 1)
        turned = pltpu.roll(flipped, keys + 1, 1, stride=1, stride_axis=0)
        by_shift_ref[0, head] = jnp.sum(turned, axis=0, keepdims=True)
    low = low_lanes((rows, PAIR))
    query_back_ref[0, :PAIR, :] = jnp.where(low, parts[0], parts[1]).T.astype(bf16)
    query_back_ref[0, PAIR:, :] = parts[2].T[:DH].astype(bf16)
    for group in range(3):
        total[group * PAIR : (group + 1) * PAIR, pl.ds(start, keys)] += sums[group]

    @pl.when(block == 1)
    def _():
        at = 0
        for out in (behind_far, behind, pair_ref, ahead, ahead_far):
            out[...] = total[:, at : at + out.shape[1]].astype(out.dtype)
            at += out.shape[1]


def attend_back(place, mine, got, window, prob, back_mine, back_got):
    rows = mine.shape[0]
    _, heads, _, keys = prob.shape
    wide = window.shape[1]
    pieces = [(rows, bf16), (2 * rows, bf16), (2 * rows, f32), (2 * rows, bf16), (rows, bf16)]
    return pl.pallas_call(
        attend_back_kernel,
        grid_spec=pltpu.PrefetchScalarGridSpec(
            num_scalar_prefetch=1,
            grid=(2,),
            in_specs=[
                whole(mine.shape),
                whole(got.shape),
                whole(window.shape),
                pl.BlockSpec((1, heads, rows, keys), lambda b, _: (b, 0, 0, 0)),
                whole(back_mine.shape),
                whole(back_got.shape),
            ],
            out_specs=[
                pl.BlockSpec((1, heads * DH, rows), lambda b, _: (b, 0, 0)),
                pl.BlockSpec((1, heads, 1, keys + rows), lambda b, _: (b, 0, 0, 0)),
            ]
            + [whole((wide, count)) for count, _ in pieces],
            scratch_shapes=[
                pltpu.VMEM((wide, SLOTS * rows), f32),
            ],
        ),
        out_shape=[
            jax.ShapeDtypeStruct((2, heads * DH, rows), bf16),
            jax.ShapeDtypeStruct((2, heads, 1, keys + rows), f32),
        ]
        + [jax.ShapeDtypeStruct((wide, count), dtype) for count, dtype in pieces],
        compiler_params=params(),
        cost_estimate=lasting(3.6),
    )(place, mine, got, window, prob, back_mine, back_got)


def gather_kernel(
    spot_ref, pair_ref, behind, ahead, behind_far, ahead_far, query_ref, both_ref, mine_ref,
    other_ref
):
    rows = behind_far.shape[1]
    wide = pair_ref.shape[0]
    total = pair_ref[...] + behind[...].astype(f32) + ahead[...].astype(f32)
    first = (total[:, :rows] + behind_far[...].astype(f32)).astype(bf16)
    second = (total[:, rows:] + ahead_far[...].astype(f32)).astype(bf16)
    both_ref[:, :rows] = first
    both_ref[:, rows:] = second

    @pl.when(spot_ref[0] == 0)
    def _():
        mine_ref[:wide, :] = first
        other_ref[:wide, :] = second
        mine_ref[wide:, :] = query_ref[0]
        other_ref[wide:, :] = query_ref[1]

    @pl.when(spot_ref[0] != 0)
    def _():
        mine_ref[:wide, :] = second
        other_ref[:wide, :] = first
        mine_ref[wide:, :] = query_ref[1]
        other_ref[wide:, :] = query_ref[0]


def gathered(spot, pair, behind, ahead, behind_far, ahead_far, query):
    wide, rows = behind_far.shape
    operands = (pair, behind, ahead, behind_far, ahead_far, query)
    pack = jax.ShapeDtypeStruct((wide + query.shape[1], rows), bf16)
    both = jax.ShapeDtypeStruct((wide, 2 * rows), bf16)
    return pl.pallas_call(
        gather_kernel,
        grid_spec=pltpu.PrefetchScalarGridSpec(
            num_scalar_prefetch=1,
            grid=(1,),
            in_specs=[whole(value.shape) for value in operands],
            out_specs=[whole(both.shape), whole(pack.shape), whole(pack.shape)],
        ),
        out_shape=[both, pack, pack],
        compiler_params=params(),
        cost_estimate=lasting(3),
    )(spot, *operands)


def close_kernel(
    spot_ref, mine_ref, other_ref, inputs_ref, middle_back_ref, w_query_ref, w_keyval_ref,
    gain_ref, input_back_ref, gain_grad_ref, query_back, keyval_back
):
    inner = query_back.shape[0]
    each = inner // 2

    def put(first, second):
        keyval_back[:each, :] = first[:each, :]
        keyval_back[each : each + DH, :] = second[PAIR : PAIR + DH, :]
        keyval_back[each + DH : inner, :] = second[:PAIR, :]
        keyval_back[inner : inner + PAIR, :] = first[4 * DH : 6 * DH, :]
        keyval_back[inner + PAIR : inner + each, :] = first[3 * DH : 4 * DH, :]
        keyval_back[inner + each :, :] = second[3 * DH : 6 * DH, :]
        query_back[:each, :] = first[inner:, :]
        query_back[each : each + DH, :] = second[inner + PAIR :, :]
        query_back[each + DH :, :] = second[inner : inner + PAIR, :]

    @pl.when(spot_ref[0] == 0)
    def _():
        put(mine_ref, other_ref)

    @pl.when(spot_ref[0] != 0)
    def _():
        put(other_ref, mine_ref)

    inputs = inputs_ref[...].astype(f32)
    scale = lax.rsqrt(jnp.mean(inputs * inputs, axis=0, keepdims=True) + 1e-06)
    normed = inputs * scale
    back = dot_nn(w_query_ref[...], query_back[...]) + dot_nn(w_keyval_ref[...], keyval_back[...])
    gain_grad_ref[...] = as_row(jnp.sum(back * normed, axis=1, keepdims=True))
    normed_back = back * as_column(gain_ref[...])
    mean = jnp.mean(normed_back * normed, axis=0, keepdims=True)
    input_back_ref[...] = (
        middle_back_ref[...] + scale * (normed_back - normed * mean)
    ).astype(bf16)


def closed(spot, mine, other, inputs, middle_back, w_query, w_keyval, gain):
    width, rows = inputs.shape
    inner = w_query.shape[1]
    operands = (mine, other, inputs, middle_back, w_query, w_keyval, gain)
    return pl.pallas_call(
        close_kernel,
        grid_spec=pltpu.PrefetchScalarGridSpec(
            num_scalar_prefetch=1,
            grid=(1,),
            in_specs=[whole(value.shape) for value in operands],
            out_specs=[whole((width, rows)), whole((1, width))],
            scratch_shapes=[
                pltpu.VMEM((inner, rows), bf16),
                pltpu.VMEM((2 * inner, rows), bf16),
            ],
        ),
        out_shape=[
            jax.ShapeDtypeStruct((width, rows), bf16),
            jax.ShapeDtypeStruct((1, width), f32),
        ],
        compiler_params=params(),
        cost_estimate=lasting(18),
    )(spot, *operands)


def swapped(value, axis, bit):
    size = lax.axis_size(axis)
    return lax.ppermute(value, axis, [(i, i ^ bit) for i in range(size)])


def passed_along(value, axis, by):
    size = lax.axis_size(axis)
    pairs = [(i, i + by) for i in range(size) if 0 <= i + by < size]
    return lax.ppermute(value, axis, pairs)


def of_both(value, bit):
    size = lax.axis_size("seq")
    groups = [[i, i | bit] for i in range(size) if not i & bit]
    return lax.all_gather(value, "seq", axis=0, tiled=True, axis_index_groups=groups)


def chosen(value, dim, index):
    return lax.dynamic_index_in_dim(value, index, dim, keepdims=False)


def added(left, right):
    return (left.astype(f32) + right.astype(f32)).astype(bf16)


def parted(state, dims, bit):
    left, right = state
    dim = dims.index(bit)
    mine = (lax.axis_index("seq") // bit) % 2
    kept = added(chosen(left, dim, mine), chosen(right, dim, mine))
    sent = added(chosen(left, dim, 1 - mine), chosen(right, dim, 1 - mine))
    return kept, sent, dims[:dim] + dims[dim + 1 :]


def after(value, *others):
    return lax.optimization_barrier((value, *others))[0]


class Halving:
    def __init__(self, state, dims, order):
        self.kept, self.got = state
        self.dims, self.order = dims, list(order)

    def step(self, earlier):
        bit = self.order.pop(0)
        got = after(self.got, earlier)
        self.kept, sent, self.dims = parted((self.kept, got), self.dims, bit)
        self.got = swapped(sent, "seq", bit)
        return sent

    def total(self, dtype=bf16):
        return (self.kept.astype(f32) + self.got.astype(f32)).astype(dtype)


def on_device(
    tokens,
    cotangent,
    item_lengths,
    gain_attn,
    gain_ffn,
    rel_table,
    w_query,
    w_keyval,
    w_out,
    w_gateup,
    w_down,
):
    rows = tokens.shape[1]
    width = tokens.shape[2]
    part = width // 2
    inner = w_query.shape[1]
    blocks = lax.axis_size("seq")
    me = lax.axis_index("seq")
    core = lax.axis_index("dp").astype(jnp.int32)
    top, pair, third = blocks // 2, blocks // 4, blocks // 8
    low = [1 << i for i in range(blocks.bit_length() - 1)][:-2]

    inputs = tokens[0].T
    cotangent = cotangent[0].T
    w_out = w_out.T
    w_down = w_down.T
    gain_attn = gain_attn[None]
    gain_ffn = gain_ffn[None]

    def bit_of(bit):
        return ((me // bit) % 2).astype(jnp.int32)

    side = bit_of(1)
    half = bit_of(pair)
    down_half = bit_of(third)

    hidden_one, mine, other = opened(side[None], inputs, gain_attn, w_query, w_keyval)
    got = swapped(other, "seq", 1)
    blocks_here = me - side + jnp.arange(2, dtype=jnp.int32)
    ends = jnp.cumsum(item_lengths[0])
    own = jnp.sum((ends[None, :] <= blocks_here[:, None]).astype(jnp.int32), 1)
    labels = jnp.arange(item_lengths.shape[1], dtype=jnp.int32)
    mark = labels[None, :] == own[:, None]
    length = jnp.sum(jnp.where(mark, item_lengths[0][None, :], 0), 1)
    end = jnp.sum(jnp.where(mark, ends[None, :], 0), 1)
    place = jnp.concatenate([blocks_here - (end - length), length, side[None]]).astype(jnp.int32)
    keys = ITEM_MOST * rows
    turns = keys + rows
    shift = jnp.arange(turns, dtype=jnp.int32)
    relative = jnp.where(shift < keys, shift, shift - turns)[None, :] - place[:2, None] * rows
    onehot = (
        bucket_of(relative)[:, :, None] == jnp.arange(BUCKETS, dtype=jnp.int32)[None, None, :]
    ).astype(f32)
    table = jnp.where(
        side == 0,
        rel_table[:, :3],
        jnp.concatenate([rel_table[:, 4:6], rel_table[:, 3:4]], 1),
    )
    by_shift = jnp.sum(onehot[:, None] * table.T[None, :, None, :], -1)
    bias = window_bias(place, by_shift, rows)

    got = after(got, bias)
    keyvals, first, second = paired(side[None], mine, got)
    pieces = [
        passed_along(second, "seq", 4),
        passed_along(keyvals, "seq", 2),
        keyvals,
        passed_along(keyvals, "seq", -2),
        passed_along(first, "seq", -4),
    ]

    attended, attended_other, prob, window = attend(place, mine, got, pieces, bias)
    attended_got = swapped(attended_other, "seq", 1)
    upstream = turned_rows(after(cotangent, attended))
    middle, hidden_two = middle_part(
        side[None], attended, attended_got, inputs, w_out, gain_ffn
    )
    hidden_far = swapped(hidden_two, "seq", pair)
    hidden_got = swapped(hidden_two, "seq", 1)
    hidden_far_got = swapped(hidden_far, "seq", 1)
    upstream_far = swapped(upstream, "seq", third)
    hidden_one_far = swapped(hidden_one, "seq", 1)

    mixed_first, back_first, *sums = ffn_half(
        False, jnp.stack([side, 1 - half]), hidden_two, upstream, w_gateup, w_down
    )
    back_far = swapped(back_first, "seq", pair)
    sums = after(tuple(sums), hidden_far, upstream_far, hidden_got)
    mixed_second, back, output, gain_ffn_grad, middle_back, branch, back_mine, back_other = ffn_half(
        True,
        jnp.stack([side, half]),
        hidden_two,
        upstream,
        w_gateup,
        w_down,
        (*sums, middle, gain_ffn, w_out, cotangent),
    )
    same = half == down_half
    mixed_far = swapped(jnp.where(same, mixed_first, mixed_second), "seq", third)
    back_got = swapped(back_other, "seq", 1)
    branch_far = swapped(after(branch, back_got), "seq", 1)
    back_mine = after(back_mine, hidden_one_far, hidden_far_got)

    backs = attend_back(place, mine, got, window, prob, back_mine, back_got)
    query_back, shift_sums = backs[:2]
    sends = backs[2:]

    def over_dp(kept, sent, dims):
        got = swapped(sent, "dp", 1)
        return tuple(
            value.reshape((2,) * dims + (value.shape[0] >> dims, value.shape[1]))
            for value in (kept, got)
        )

    spot = jnp.stack([core, side])
    units = mixed_first.shape[0]
    owned = units * 4 // blocks
    parts = 2 if owned % 32 == 0 else 1

    def other_owners(value):
        value = value.reshape(2, units // owned // 2, 2, owned, rows)
        return chosen(value, 2, 1 - side).reshape(2, units // 2, rows)

    back_got = swapped(other_owners(back), "seq", 1)
    back_far_sent = other_owners(back_far)
    back_far_got = swapped(back_far_sent, "seq", 1)
    down_kept, down_sent = pair_grad(
        jnp.stack([core, same.astype(jnp.int32)]),
        (2, lambda j: (0, j)),
        units // 2,
        1,
        (after(mixed_second, query_back, back_got, back_far_sent)[None], mixed_first[None]),
        mixed_far[None],
        upstream,
        upstream_far,
    )
    down = Halving(
        over_dp(down_kept, down_sent, len(low) + 1),
        [pair, top] + low[-2::-1],
        [pair] + low[-2::-1] + [top],
    )
    sent = down.step(down_kept)
    near_kept, near_sent, *far_grads = quad_grad(
        spot,
        owned,
        parts,
        (after(back, sent), back_far),
        (back_got, back_far_got),
        (hidden_two, hidden_far, hidden_got, hidden_far_got),
    )
    keyval_back, to_close, to_swap = gathered(
        side[None],
        after(sends[2], near_kept),
        passed_along(sends[3], "seq", 2),
        passed_along(sends[1], "seq", -2),
        passed_along(sends[4], "seq", 4),
        passed_along(sends[0], "seq", -4),
        query_back,
    )
    closed_with = swapped(to_swap, "seq", 1)
    gate_dims = [top] + low[:0:-1]
    gate_order = low[:0:-1] + [top]
    near = Halving(over_dp(near_kept, near_sent, len(low)), gate_dims, gate_order)
    far = None
    if parts == 2:
        far = Halving(over_dp(*far_grads, len(low)), gate_dims, gate_order)
    sent = keyval_back
    sent = near.step(sent)
    head_kept, head_sent = heads_grad(
        jnp.stack([core, side]),
        after(keyval_back, sent),
        query_back,
        (attended, attended_other),
        (hidden_one, hidden_one_far),
        (branch, branch_far),
    )
    others = [top, pair] + low[:0:-1]
    count = len(others)
    each = inner // 2

    def by_owner(value):
        def cut(array, bits):
            array = array.reshape((2,) * count + (-1, array.shape[-1]))
            return array.transpose([bits.index(bit) for bit in others] + [count, count + 1])

        asks = [pair] + low[:0:-1] + [top]
        keyvals = [top] + low[:0:-1] + [pair]
        return jnp.concatenate(
            [
                cut(value[:each], asks),
                cut(value[3 * each :], asks),
                cut(value[each : 3 * each], keyvals),
            ],
            -2,
        )

    head = Halving(
        (by_owner(head_kept), by_owner(swapped(head_sent, "dp", 1))),
        others,
        [pair] + low[1:] + [top],
    )
    sent = head_kept
    sent = far.step(sent) if far else sent
    input_back, gain_attn_grad = closed(
        side[None],
        after(to_close, sent),
        closed_with,
        inputs,
        middle_back,
        w_query,
        w_keyval,
        gain_attn,
    )

    sums = jnp.einsum(
        "pmb,phm->bh", onehot, shift_sums[:, :, 0], precision=lax.Precision.HIGHEST
    )
    nothing = jnp.zeros_like(sums)
    table_local = jnp.where(
        side == 0,
        jnp.concatenate([sums, nothing], 1),
        jnp.concatenate([nothing, sums[:, 2:], sums[:, :2]], 1),
    )
    small = jnp.concatenate(
        [gain_attn_grad.reshape(-1), gain_ffn_grad.reshape(-1), table_local.reshape(-1)]
    )
    taken = small.shape[0]
    small = jnp.pad(small, (0, -taken % 128)).reshape(-1, 128)
    small_got = swapped(small, "dp", 1)
    sent = gain_attn_grad
    small_order = low[::-1] + [pair, top]
    chains = [chain for chain in (near, far, down, head) if chain]
    while any(chain.order for chain in chains) or small_order:
        for chain in chains:
            if chain.order:
                sent = chain.step(sent)
            if small_order and chain in (head, near):
                small = small + after(small_got, sent)
                small_got = swapped(small, "seq", small_order.pop(0))
    small = small + after(small_got, sent)

    turn = [
        (i, (i & ~(top | third)) | (third if i & top else 0) | (top if i & third else 0))
        for i in range(blocks)
    ]
    down_grad = lax.ppermute(down.total(), "seq", turn).astype(f32)[:, :part]
    def exchanged(i, bit):
        return (i & ~(1 | bit)) | (1 if i & bit else 0) | (bit if i & 1 else 0)

    own_rows = inner // blocks
    head_sum = head.total()
    asks = lax.ppermute(
        head_sum[: 2 * own_rows], "seq", [(i, exchanged(i, top)) for i in range(blocks)]
    ).astype(f32)
    query_grad = asks[:own_rows, :part].T
    out_grad = asks[own_rows:, :part]
    keyval_grad = (
        lax.ppermute(
            head_sum[2 * own_rows :], "seq", [(i, exchanged(i, pair)) for i in range(blocks)]
        )
        .astype(f32)[:, :part]
        .T
    )
    gateup_grad = jnp.concatenate([one.total(f32)[:, :part].T for one in (near, far) if one], 1)
    small = small.reshape(-1)
    return (
        output.T[None],
        input_back.T[None],
        small[:width],
        small[width : 2 * width],
        small[2 * width : taken].reshape(BUCKETS, H),
        query_grad,
        keyval_grad,
        out_grad,
        gateup_grad,
        down_grad,
    )


def solution(mesh):
    placed = (
        P("dp", "seq", None),
        P("dp", "seq", None),
        P("dp", None),
        P(),
        P(),
        P(),
        P(),
        P(),
        P(),
        P(),
        P(),
    )
    return jax.shard_map(
        on_device,
        mesh=mesh,
        in_specs=placed,
        out_specs=(
            P("dp", "seq", None),
            P("dp", "seq", None),
            P(),
            P(),
            P(),
            P("dp", "seq"),
            P("dp", "seq"),
            P("seq", "dp"),
            P("dp", "seq"),
            P("seq", "dp"),
        ),
        check_vma=False,
    )
```

```python
import functools

import jax
import jax.numpy as jnp
from jax import lax
from jax.experimental import pallas as pl
from jax.experimental.pallas import tpu as pltpu
from jax.sharding import PartitionSpec as P

H = 6
DH = 64
BUCKETS = 32
ITEM_MOST = 4
REACH = ITEM_MOST - 1
PAIR = 2 * DH
UNITS = 896

bucket_edges = (12, 16, 23, 32, 46, 64, 91)
negative_fill = -1e30
f32 = jnp.float32
bf16 = jnp.bfloat16
VMEM_MOST = 56 * 1024 * 1024
FLOPS_PER_US = 5_000_000_000


def bucket_of(relative):
    ahead = jnp.where(relative > 0, 16, 0).astype(jnp.int32)
    distance = jnp.abs(relative)
    beyond = 8 + sum(((distance >= edge).astype(jnp.int32) for edge in bucket_edges))
    return ahead + jnp.where(distance < 8, distance, beyond)


def dot_nn(left, right):
    return lax.dot_general(left, right, (((1,), (0,)), ((), ())), preferred_element_type=f32)


def dot_nt(left, right):
    return lax.dot_general(left, right, (((1,), (1,)), ((), ())), preferred_element_type=f32)


def dot_tn(left, right):
    return lax.dot_general(left, right, (((0,), (0,)), ((), ())), preferred_element_type=f32)


def rms_scale(values):
    return lax.rsqrt(jnp.mean(values * values, axis=-1, keepdims=True) + 1e-06)


def lasting(microseconds):
    return pl.CostEstimate(
        flops=int(microseconds * FLOPS_PER_US), bytes_accessed=0, transcendentals=0
    )


def whole(shape):
    return pl.BlockSpec(shape, lambda *_: (0,) * len(shape))


def params():
    return pltpu.CompilerParams(vmem_limit_bytes=VMEM_MOST)


def up_to(count, step):
    return -(-count // step) * step


def spread_width(width):
    return 2 * up_to(width // 2, 128)


def spread_rows(out, value, gain=None):
    half = value.shape[0] // 2
    each = out.shape[1] // 2
    nothing = jnp.zeros((out.shape[0], each - half), out.dtype)
    for index in range(2):
        part = value[index * half : (index + 1) * half].T
        if gain is not None:
            part = part * gain[:, index * half : (index + 1) * half]
        out[:, index * each : index * each + half] = part.astype(out.dtype)
        out[:, index * each + half : (index + 1) * each] = nothing


def spread_depth(value, wide):
    half = value.shape[0] // 2
    nothing = jnp.zeros((wide // 2 - half, value.shape[1]), value.dtype)
    return jnp.concatenate([value[:half], nothing, value[half:], nothing], 0)


def as_column(row):
    return jnp.broadcast_to(row, (128, row.shape[1])).T[:, :1]


def as_row(column):
    return jnp.broadcast_to(column, (column.shape[0], 128)).T[:1]


def shift_by_head(value):
    return pltpu.roll(value, DH, 1)


def columns(value, index):
    return value[:, index * PAIR : (index + 1) * PAIR]


def low_lanes(shape):
    return lax.broadcasted_iota(jnp.int32, shape, len(shape) - 1) % PAIR < DH


def packed_heads(query, keyval, half):
    low = low_lanes((query.shape[0], PAIR))
    key = [columns(keyval, i) for i in range(3)]
    value = [columns(keyval, i + 3) for i in range(3)]
    ask = [columns(query, i) for i in range(3)]
    if half == 0:
        parts = [
            key[0],
            jnp.where(low, key[1], shift_by_head(value[1])),
            value[0],
            ask[0],
            jnp.where(low, ask[1], 0.0),
        ]
    else:
        parts = [
            key[2],
            jnp.where(low, shift_by_head(key[1]), value[1]),
            value[2],
            ask[2],
            jnp.where(low, shift_by_head(ask[1]), 0.0),
        ]
    return jnp.concatenate(parts, 1).astype(bf16)


def open_kernel(
    spot_ref, inputs_ref, gain_ref, w_query_ref, w_keyval_ref, hidden_ref, mine_ref, other_ref
):
    inputs = inputs_ref[...].astype(f32)
    scale = lax.rsqrt(jnp.mean(inputs * inputs, axis=0, keepdims=True) + 1e-06)
    spread_rows(hidden_ref, inputs * scale, gain_ref[...])
    hidden = hidden_ref[...]
    wide = hidden.shape[1]
    keyval = dot_nn(hidden, spread_depth(w_keyval_ref[...], wide))
    query = dot_nn(hidden, spread_depth(w_query_ref[...], wide))
    first = packed_heads(query, keyval, 0)
    second = packed_heads(query, keyval, 1)

    @pl.when(spot_ref[0] == 0)
    def _():
        mine_ref[...] = first
        other_ref[...] = second

    @pl.when(spot_ref[0] != 0)
    def _():
        mine_ref[...] = second
        other_ref[...] = first


def opened(spot, inputs, gain, w_query, w_keyval):
    width, rows = inputs.shape
    inner = w_query.shape[1]
    pack = jax.ShapeDtypeStruct((rows, 5 * PAIR), bf16)
    return pl.pallas_call(
        open_kernel,
        grid_spec=pltpu.PrefetchScalarGridSpec(
            num_scalar_prefetch=1,
            grid=(1,),
            in_specs=[
                whole((width, rows)),
                whole((1, width)),
                whole((width, inner)),
                whole((width, 2 * inner)),
            ],
            out_specs=[
                whole((rows, spread_width(width))),
                whole(pack.shape),
                whole(pack.shape),
            ],
        ),
        out_shape=[jax.ShapeDtypeStruct((rows, spread_width(width)), bf16), pack, pack],
        compiler_params=params(),
        cost_estimate=lasting(5),
    )(spot, inputs, gain, w_query, w_keyval)


def turn_kernel(in_ref, out_ref):
    spread_rows(out_ref, in_ref[...])


def turned_rows(value):
    width, rows = value.shape
    return pl.pallas_call(
        turn_kernel,
        out_shape=jax.ShapeDtypeStruct((rows, spread_width(width)), value.dtype),
        compiler_params=params(),
        cost_estimate=lasting(2),
    )(value)


def bias_kernel(place_ref, by_shift_ref, out_ref):
    rows, keys = out_ref.shape[2:]
    wide = by_shift_ref.shape[-1]
    spread = jnp.broadcast_to(by_shift_ref[0, 0], (rows, wide))
    turned = pltpu.roll(spread, 0, 1, stride=1, stride_axis=0)[:, :keys]
    key = lax.broadcasted_iota(jnp.int32, (rows, keys), 1)
    length = place_ref[2 + pl.program_id(0)]
    out_ref[0, 0] = jnp.where(key < length * rows, turned, negative_fill)


def window_bias(place, by_shift, rows):
    keys = ITEM_MOST * rows
    both, heads, wide = by_shift.shape
    return pl.pallas_call(
        bias_kernel,
        grid_spec=pltpu.PrefetchScalarGridSpec(
            num_scalar_prefetch=1,
            grid=(both, heads),
            in_specs=[pl.BlockSpec((1, 1, 1, wide), lambda b, h, _: (b, h, 0, 0))],
            out_specs=pl.BlockSpec((1, 1, rows, keys), lambda b, h, _: (b, h, 0, 0)),
        ),
        out_shape=jax.ShapeDtypeStruct((both, heads, rows, keys), f32),
        compiler_params=params(),
        cost_estimate=lasting(6),
    )(place, by_shift.reshape(both, heads, 1, wide))


SLOTS = 2 * REACH + 2


def pair_kernel(spot_ref, mine_ref, got_ref, both_ref, first_ref, second_ref):
    rows = mine_ref.shape[0]
    wide = first_ref.shape[1]
    mine, got = mine_ref[:, :wide], got_ref[:, :wide]

    def put(first, second):
        first_ref[...] = first
        second_ref[...] = second
        both_ref[:rows, :] = first
        both_ref[rows:, :] = second

    @pl.when(spot_ref[0] == 0)
    def _():
        put(mine, got)

    @pl.when(spot_ref[0] != 0)
    def _():
        put(got, mine)


def paired(spot, mine, got):
    rows = mine.shape[0]
    shapes = [(2 * rows, 3 * PAIR), (rows, 3 * PAIR), (rows, 3 * PAIR)]
    return pl.pallas_call(
        pair_kernel,
        grid_spec=pltpu.PrefetchScalarGridSpec(
            num_scalar_prefetch=1,
            grid=(1,),
            in_specs=[whole(mine.shape)] * 2,
            out_specs=[whole(shape) for shape in shapes],
        ),
        out_shape=[jax.ShapeDtypeStruct(shape, bf16) for shape in shapes],
        compiler_params=params(),
        cost_estimate=lasting(1),
    )(spot, mine, got)


GROUPS = ((0, 2), (0, 2), (1, 1))


def spread_heads(own, mine, got):
    value = jnp.where(own, mine, got)
    first = columns(value, 0)
    low = low_lanes(first.shape)
    nothing = jnp.zeros_like(first)
    return jnp.where(low, first, nothing), jnp.where(low, nothing, first), columns(value, 1)


def attend_kernel(
    place_ref, mine_ref, got_ref, behind_far, behind, pair_ref, ahead, ahead_far, bias_ref,
    attended_mine, attended_other, prob_ref, window_ref
):
    rows = mine_ref.shape[0]
    wide = window_ref.shape[1]
    block = pl.program_id(0)
    own = block == place_ref[4]

    @pl.when(block == 0)
    def _():
        at = 0
        for piece in (behind_far, behind, pair_ref, ahead, ahead_far):
            window_ref[at : at + piece.shape[0], :] = piece[...]
            at += piece.shape[0]

    asks = spread_heads(own, mine_ref[:, wide:], got_ref[:, wide:])
    start = pl.multiple_of((REACH + block - place_ref[block]) * rows, rows)
    window = window_ref[pl.ds(start, ITEM_MOST * rows), :]
    parts = []
    for head, (key, value) in enumerate(GROUPS):
        scores = dot_nt(asks[head], columns(window, key)) + bias_ref[0, head]
        exponent = jnp.exp(scores - jnp.max(scores, axis=-1, keepdims=True))
        prob = exponent / jnp.sum(exponent, axis=-1, keepdims=True)
        prob_ref[0, head] = prob
        parts.append(dot_nn(prob.astype(bf16), columns(window, value)))

    def put(out):
        low = low_lanes((rows, PAIR))
        out[:PAIR, :] = jnp.where(low, parts[0], parts[1]).T.astype(bf16)
        out[PAIR:, :] = parts[2].T[DH:].astype(bf16)

    @pl.when(own)
    def _():
        put(attended_mine)

    @pl.when(jnp.logical_not(own))
    def _():
        put(attended_other)


def attend(place, mine, got, pieces, bias):
    rows = mine.shape[0]
    keys = ITEM_MOST * rows
    wide = pieces[0].shape[1]
    heads = bias.shape[1]
    tall = pl.BlockSpec((1, heads, rows, keys), lambda b, _: (b, 0, 0, 0))
    return pl.pallas_call(
        attend_kernel,
        grid_spec=pltpu.PrefetchScalarGridSpec(
            num_scalar_prefetch=1,
            grid=(2,),
            in_specs=[whole(mine.shape)] * 2 + [whole(piece.shape) for piece in pieces] + [tall],
            out_specs=[
                whole((heads * DH, rows)),
                whole((heads * DH, rows)),
                tall,
                whole((SLOTS * rows, wide)),
            ],
        ),
        out_shape=[
            jax.ShapeDtypeStruct((heads * DH, rows), bf16),
            jax.ShapeDtypeStruct((heads * DH, rows), bf16),
            jax.ShapeDtypeStruct((2, heads, rows, keys), f32),
            jax.ShapeDtypeStruct((SLOTS * rows, wide), bf16),
        ],
        compiler_params=params(),
        cost_estimate=lasting(9),
    )(place, mine, got, *pieces, bias)


def natural_heads(half, mine, other, out):
    each = mine.shape[0]

    def put(first, second):
        out[:each, :] = first[...]
        out[each : each + DH, :] = second[PAIR:, :]
        out[each + DH :, :] = second[:PAIR, :]

    @pl.when(half == 0)
    def _():
        put(mine, other)

    @pl.when(half != 0)
    def _():
        put(other, mine)


def middle_kernel(
    spot_ref, mine_ref, other_ref, inputs_ref, w_out_ref, gain_ref, middle_ref, hidden_ref, attended
):
    natural_heads(spot_ref[0], mine_ref, other_ref, attended)
    middle = inputs_ref[...].astype(f32) + dot_nn(w_out_ref[...], attended[...])
    middle_ref[...] = middle
    scale = lax.rsqrt(jnp.mean(middle * middle, axis=0, keepdims=True) + 1e-06)
    spread_rows(hidden_ref, middle * scale, gain_ref[...])


def middle_part(spot, mine, other, inputs, w_out, gain):
    width, rows = inputs.shape
    inner = w_out.shape[1]
    return pl.pallas_call(
        middle_kernel,
        grid_spec=pltpu.PrefetchScalarGridSpec(
            num_scalar_prefetch=1,
            grid=(1,),
            in_specs=[
                whole(mine.shape),
                whole(other.shape),
                whole((width, rows)),
                whole((width, inner)),
                whole((1, width)),
            ],
            out_specs=[whole((width, rows)), whole((rows, spread_width(width)))],
            scratch_shapes=[pltpu.VMEM((inner, rows), bf16)],
        ),
        out_shape=[
            jax.ShapeDtypeStruct((width, rows), f32),
            jax.ShapeDtypeStruct((rows, spread_width(width)), bf16),
        ],
        compiler_params=params(),
        cost_estimate=lasting(4),
    )(spot, mine, other, inputs, w_out, gain)


GELU_A = 0.7978845608028654
GELU_B = 0.044715


def packed_back(back, half):
    low = low_lanes((back.shape[0], PAIR))
    middle = columns(back, 1)
    if half == 0:
        parts = [columns(back, 0), jnp.where(low, 0.0, shift_by_head(middle))]
    else:
        parts = [columns(back, 2), jnp.where(low, 0.0, middle)]
    return jnp.concatenate(parts, 1).astype(bf16)


def ffn_kernel(last, spot_ref, hidden_ref, upstream_ref, gate_w_ref, up_w_ref, down_w_ref, *refs):
    if last:
        out_in, back_in, middle_ref, gain_ref, w_out_ref, cotangent_ref = refs[:6]
        (mixed_ref, both_ref, output_ref, gain_grad_ref, middle_back_ref,
         branch_ref, back_mine_ref, back_other_ref, out_ref, back_ref) = refs[6:]
    else:
        mixed_ref, both_ref, out_ref, back_ref = refs
    step = pl.program_id(0)
    units = gate_w_ref.shape[1]
    hidden = hidden_ref[...]
    wide = hidden.shape[1]
    upstream = upstream_ref[...]
    gateup_w = jnp.concatenate([gate_w_ref[...], up_w_ref[...]], 1)
    gateup = dot_nn(hidden, spread_depth(gateup_w, wide))
    gate, up = gateup[:, :units], gateup[:, units:]
    mixed_back = dot_nn(upstream, spread_depth(down_w_ref[...], wide))
    squared = gate * gate
    bent = jnp.tanh(GELU_A * (gate + GELU_B * (squared * gate)))
    share = 0.5 * (1.0 + bent)
    gelu = gate * share
    slope = share + 0.5 * gate * (1.0 - bent * bent) * (GELU_A * (1.0 + 3.0 * GELU_B * squared))
    mixed = (gelu * up).astype(bf16).T
    gate_back = (mixed_back * up * slope).astype(bf16).T
    up_back = (mixed_back * gelu).astype(bf16).T
    mixed_ref[...] = mixed
    both_ref[0] = gate_back
    both_ref[1] = up_back
    forward = dot_nn(down_w_ref[...], mixed)
    backward = dot_nn(gateup_w, jnp.concatenate([gate_back, up_back], 0))

    @pl.when(step == 0)
    def _():
        if last:
            out_ref[...] = out_in[...] + forward
            back_ref[...] = back_in[...] + backward
        else:
            out_ref[...] = forward
            back_ref[...] = backward

    @pl.when(step > 0)
    def _():
        out_ref[...] += forward
        back_ref[...] += backward

    if not last:
        return

    @pl.when(step == pl.num_programs(0) - 1)
    def _():
        middle = middle_ref[...]
        output_ref[...] = (middle + out_ref[...]).astype(bf16)
        scale = lax.rsqrt(jnp.mean(middle * middle, axis=0, keepdims=True) + 1e-06)
        normed = middle * scale
        back = back_ref[...]
        gain_grad_ref[...] = as_row(jnp.sum(back * normed, axis=1, keepdims=True))
        normed_back = back * as_column(gain_ref[...])
        mean = jnp.mean(normed_back * normed, axis=0, keepdims=True)
        middle_back = cotangent_ref[...].astype(f32) + scale * (normed_back - normed * mean)
        middle_back_ref[...] = middle_back
        spread_rows(branch_ref, middle_back)
        attended_back = dot_nn(branch_ref[...], spread_depth(w_out_ref[...], wide))
        first = packed_back(attended_back, 0)
        second = packed_back(attended_back, 1)

        @pl.when(spot_ref[0] == 0)
        def _():
            back_mine_ref[...] = first
            back_other_ref[...] = second

        @pl.when(spot_ref[0] != 0)
        def _():
            back_mine_ref[...] = second
            back_other_ref[...] = first


def ffn_half(last, spot, hidden, upstream, w_gateup, w_down, more=()):
    rows, wide = hidden.shape
    width, units = w_down.shape
    steps = units // 2 // UNITS
    both = units // UNITS
    in_specs = [
        whole((rows, wide)),
        whole((rows, wide)),
        pl.BlockSpec((width, UNITS), lambda j, s: (0, s[1] * steps + j)),
        pl.BlockSpec((width, UNITS), lambda j, s: (0, both + s[1] * steps + j)),
        pl.BlockSpec((width, UNITS), lambda j, s: (0, s[1] * steps + j)),
    ] + [whole(value.shape) for value in more]
    sums = [jax.ShapeDtypeStruct((width, rows), f32)] * 2
    out_specs = [
        pl.BlockSpec((UNITS, rows), lambda j, s: (j, 0)),
        pl.BlockSpec((2, UNITS, rows), lambda j, s: (0, j, 0)),
    ]
    out_shape = [
        jax.ShapeDtypeStruct((units // 2, rows), bf16),
        jax.ShapeDtypeStruct((2, units // 2, rows), bf16),
    ]
    if last:
        rest = [
            jax.ShapeDtypeStruct((width, rows), bf16),
            jax.ShapeDtypeStruct((1, width), f32),
            jax.ShapeDtypeStruct((width, rows), f32),
            jax.ShapeDtypeStruct((rows, wide), bf16),
            jax.ShapeDtypeStruct((rows, 2 * PAIR), bf16),
            jax.ShapeDtypeStruct((rows, 2 * PAIR), bf16),
        ]
    else:
        rest = sums
    return pl.pallas_call(
        functools.partial(ffn_kernel, last),
        grid_spec=pltpu.PrefetchScalarGridSpec(
            num_scalar_prefetch=1,
            grid=(steps,),
            in_specs=in_specs,
            out_specs=out_specs + [whole(value.shape) for value in rest],
            scratch_shapes=[pltpu.VMEM((width, rows), f32)] * 2 if last else [],
        ),
        out_shape=out_shape + rest,
        compiler_params=params(),
        cost_estimate=lasting(20),
    )(spot, hidden, upstream, w_gateup, w_gateup, w_down, *more)


def half_of(ref, index):
    each = ref.shape[1] // 2
    return ref[:, pl.ds(pl.multiple_of(index * each, 128), each)]


def pair_grad_kernel(
    parts, spot_ref, left_own, left_other, left_far, right_own, right_far, *refs
):
    outs, halves = refs[:-1], refs[-1]
    rows = left_far.shape[-1]
    mine = spot_ref[0]

    @pl.when(pl.program_id(0) == 0)
    def _():
        for index, right in enumerate((right_own, right_far)):
            at = slice(index * rows, (index + 1) * rows)
            halves[0, at, :] = half_of(right, mine)
            halves[1, at, :] = half_of(right, 1 - mine)

    own = left_own[0] if left_other is None else jnp.where(spot_ref[1] != 0, left_own[0], left_other[0])
    left = jnp.concatenate([own, left_far[0]], 1)
    each = left.shape[0] // parts
    for half in range(2):
        product = dot_nn(left, halves[half]).astype(bf16)
        for part in range(parts):
            outs[2 * part + half][...] = product[part * each : (part + 1) * each]


def pair_grad(spot, tiles, tile, parts, left_own, left_far, right_own, right_far):
    count, place = tiles
    rows = left_far.shape[-1]
    wide = right_own.shape[1] // 2
    each = tile // parts
    out = jax.ShapeDtypeStruct((count * each, wide), bf16)
    left = pl.BlockSpec((1, tile, rows), lambda j, _: (*place(j), 0))

    def kernel(spot_ref, *refs):
        if len(left_own) == 1:
            pair_grad_kernel(parts, spot_ref, refs[0], None, *refs[1:])
        else:
            pair_grad_kernel(parts, spot_ref, *refs)

    return pl.pallas_call(
        kernel,
        grid_spec=pltpu.PrefetchScalarGridSpec(
            num_scalar_prefetch=1,
            grid=(count,),
            in_specs=[left] * (len(left_own) + 1) + [whole(right_own.shape), whole(right_far.shape)],
            out_specs=[pl.BlockSpec((each, wide), lambda j, _: (j, 0))] * (2 * parts),
            scratch_shapes=[pltpu.VMEM((2, 2 * rows, wide), bf16)],
        ),
        out_shape=[out] * (2 * parts),
        compiler_params=params(),
        cost_estimate=lasting(24),
    )(spot, *left_own, left_far, right_own, right_far)


def quad_grad_kernel(
    parts, spot_ref, left_own, left_far, left_own_got, left_far_got, *refs
):
    rights, outs, halves = refs[:4], refs[4:-1], refs[-1]
    rows = left_own.shape[-1]
    mine = spot_ref[0]

    @pl.when((pl.program_id(0) == 0) & (pl.program_id(1) == 0))
    def _():
        for index, right in enumerate(rights):
            at = slice(index * rows, (index + 1) * rows)
            halves[0, at, :] = half_of(right, mine)
            halves[1, at, :] = half_of(right, 1 - mine)

    left = jnp.concatenate([left_own[0], left_far[0], left_own_got[0], left_far_got[0]], 1)
    each = left.shape[0] // parts
    for half in range(2):
        product = dot_nn(left, halves[half]).astype(bf16)
        for part in range(parts):
            outs[2 * part + half][...] = product[part * each : (part + 1) * each]


def quad_grad(spot, owned, parts, lefts, lefts_got, rights):
    groups, units, rows = lefts_got[0].shape
    wide = rights[0].shape[1] // 2
    runs = units // owned
    each = owned // parts
    out = jax.ShapeDtypeStruct((groups * runs * each, wide), bf16)
    return pl.pallas_call(
        functools.partial(quad_grad_kernel, parts),
        grid_spec=pltpu.PrefetchScalarGridSpec(
            num_scalar_prefetch=1,
            grid=(groups, runs),
            in_specs=[pl.BlockSpec((1, owned, rows), lambda g, j, s: (g, 2 * j + s[1], 0))] * 2
            + [pl.BlockSpec((1, owned, rows), lambda g, j, s: (g, j, 0))] * 2
            + [whole(right.shape) for right in rights],
            out_specs=[pl.BlockSpec((each, wide), lambda g, j, s: (g * runs + j, 0))] * (2 * parts),
            scratch_shapes=[pltpu.VMEM((2, 4 * rows, wide), bf16)],
        ),
        out_shape=[out] * (2 * parts),
        compiler_params=params(),
        cost_estimate=lasting(12),
    )(spot, *lefts, *lefts_got, *rights)


def heads_grad_kernel(
    spot_ref, keyval_ref, query_ref, attended_own, attended_far, hidden_own, hidden_far, branch_own,
    branch_far, kept_ref, sent_ref, low, high, left
):
    rows = hidden_own.shape[0]
    mine, half = spot_ref[0], spot_ref[1]
    each = query_ref.shape[1]

    def ordered(source, at, first, second):
        @pl.when(half == 0)
        def _():
            for start, stop, to in first:
                left[at + to : at + to + stop - start, :] = source(start, stop)

        @pl.when(half != 0)
        def _():
            for start, stop, to in second:
                left[at + to : at + to + stop - start, :] = source(start, stop)

    same = ((0, 3 * DH, 0),)
    turned = ((PAIR, 3 * DH, 0), (0, PAIR, DH))
    value_first = ((4 * DH, 6 * DH, 0), (3 * DH, 4 * DH, PAIR))
    value_second = ((3 * DH, 6 * DH, 0),)

    def joined(ref):
        return lambda start, stop: jnp.concatenate(
            [ref[0, start:stop, :], ref[1, start:stop, :]], 1
        )

    def plain(start, stop):
        return keyval_ref[start:stop, :]

    ordered(joined(query_ref), 0, same, turned)
    ordered(plain, each, same, turned)
    ordered(plain, 2 * each, value_first, value_second)

    def by_side(start, stop):
        own, far = attended_own[start:stop, :], attended_far[start:stop, :]
        first = jnp.where(half == 0, own, far)
        second = jnp.where(half == 0, far, own)
        return jnp.concatenate([first, second], 1)

    ordered(by_side, 3 * each, same, turned)
    for own, far, at, stop in (
        (hidden_own, hidden_far, 0, 3 * each),
        (branch_own, branch_far, 3 * each, 4 * each),
    ):
        for index, source in ((0, own), (1, far)):

            @pl.when(half == index)
            def _():
                low[:rows, :] = half_of(source, mine)
                high[:rows, :] = half_of(source, 1 - mine)

            @pl.when(half != index)
            def _():
                low[rows:, :] = half_of(source, mine)
                high[rows:, :] = half_of(source, 1 - mine)

        kept_ref[at:stop, :] = dot_nn(left[at:stop, :], low[...]).astype(bf16)
        sent_ref[at:stop, :] = dot_nn(left[at:stop, :], high[...]).astype(bf16)


def heads_grad(spot, keyval, query, attended, hiddens, branches):
    wide = hiddens[0].shape[1] // 2
    rows = hiddens[0].shape[0]
    each = query.shape[1]
    out = jax.ShapeDtypeStruct((4 * each, wide), bf16)
    operands = (keyval, query, *attended, *hiddens, *branches)
    return pl.pallas_call(
        heads_grad_kernel,
        grid_spec=pltpu.PrefetchScalarGridSpec(
            num_scalar_prefetch=1,
            grid=(1,),
            in_specs=[whole(value.shape) for value in operands],
            out_specs=[whole(out.shape)] * 2,
            scratch_shapes=[pltpu.VMEM((2 * rows, wide), bf16)] * 2
            + [pltpu.VMEM((4 * each, 2 * rows), bf16)],
        ),
        out_shape=[out, out],
        compiler_params=params(),
        cost_estimate=lasting(2.1),
    )(spot, *operands)


def attend_back_kernel(
    place_ref, mine_ref, got_ref, window_ref, prob_ref, back_mine, back_got, query_back_ref,
    by_shift_ref, behind_far, behind, pair_ref, ahead, ahead_far, total
):
    rows = mine_ref.shape[0]
    wide = window_ref.shape[1]
    keys = ITEM_MOST * rows
    block = pl.program_id(0)
    own = block == place_ref[4]
    asks = spread_heads(own, mine_ref[:, wide:], got_ref[:, wide:])
    backs = spread_heads(own, back_mine[...], back_got[...])

    @pl.when(block == 0)
    def _():
        total[...] = jnp.zeros_like(total)

    start = pl.multiple_of((REACH + block - place_ref[block]) * rows, rows)
    window = window_ref[pl.ds(start, keys), :]
    row = lax.broadcasted_iota(jnp.int32, (rows, rows), 0)
    column = lax.broadcasted_iota(jnp.int32, (rows, rows), 1)
    flip = jnp.where(row + column == rows - 1, 1.0, 0.0).astype(bf16)
    parts, sums = [], [None] * 3
    for head, (key, value) in enumerate(GROUPS):
        prob = prob_ref[0, head]
        prob_back = dot_nt(backs[head], columns(window, value))
        delta = jnp.sum(prob * prob_back, axis=-1, keepdims=True)
        score_back = (prob * (prob_back - delta)).astype(bf16)
        parts.append(dot_nn(score_back, columns(window, key)))
        key_part = dot_tn(asks[head], score_back)
        value_part = dot_tn(backs[head], prob.astype(bf16))
        for group, add in ((key, key_part), (value, value_part)):
            sums[group] = add if sums[group] is None else sums[group] + add
        flipped = jnp.concatenate([dot_nn(flip, score_back), jnp.zeros((rows, rows), f32)], 1)
        turned = pltpu.roll(flipped, keys + 1, 1, stride=1, stride_axis=0)
        by_shift_ref[0, head] = jnp.sum(turned, axis=0, keepdims=True)
    low = low_lanes((rows, PAIR))
    query_back_ref[0, :PAIR, :] = jnp.where(low, parts[0], parts[1]).T.astype(bf16)
    query_back_ref[0, PAIR:, :] = parts[2].T[:DH].astype(bf16)
    for group in range(3):
        total[group * PAIR : (group + 1) * PAIR, pl.ds(start, keys)] += sums[group]

    @pl.when(block == 1)
    def _():
        at = 0
        for out in (behind_far, behind, pair_ref, ahead, ahead_far):
            out[...] = total[:, at : at + out.shape[1]].astype(out.dtype)
            at += out.shape[1]


def attend_back(place, mine, got, window, prob, back_mine, back_got):
    rows = mine.shape[0]
    _, heads, _, keys = prob.shape
    wide = window.shape[1]
    pieces = [(rows, bf16), (2 * rows, bf16), (2 * rows, f32), (2 * rows, bf16), (rows, bf16)]
    return pl.pallas_call(
        attend_back_kernel,
        grid_spec=pltpu.PrefetchScalarGridSpec(
            num_scalar_prefetch=1,
            grid=(2,),
            in_specs=[
                whole(mine.shape),
                whole(got.shape),
                whole(window.shape),
                pl.BlockSpec((1, heads, rows, keys), lambda b, _: (b, 0, 0, 0)),
                whole(back_mine.shape),
                whole(back_got.shape),
            ],
            out_specs=[
                pl.BlockSpec((1, heads * DH, rows), lambda b, _: (b, 0, 0)),
                pl.BlockSpec((1, heads, 1, keys + rows), lambda b, _: (b, 0, 0, 0)),
            ]
            + [whole((wide, count)) for count, _ in pieces],
            scratch_shapes=[
                pltpu.VMEM((wide, SLOTS * rows), f32),
            ],
        ),
        out_shape=[
            jax.ShapeDtypeStruct((2, heads * DH, rows), bf16),
            jax.ShapeDtypeStruct((2, heads, 1, keys + rows), f32),
        ]
        + [jax.ShapeDtypeStruct((wide, count), dtype) for count, dtype in pieces],
        compiler_params=params(),
        cost_estimate=lasting(3.6),
    )(place, mine, got, window, prob, back_mine, back_got)


def gather_kernel(
    spot_ref, pair_ref, behind, ahead, behind_far, ahead_far, query_ref, both_ref, mine_ref,
    other_ref
):
    rows = behind_far.shape[1]
    wide = pair_ref.shape[0]
    total = pair_ref[...] + behind[...].astype(f32) + ahead[...].astype(f32)
    first = (total[:, :rows] + behind_far[...].astype(f32)).astype(bf16)
    second = (total[:, rows:] + ahead_far[...].astype(f32)).astype(bf16)
    both_ref[:, :rows] = first
    both_ref[:, rows:] = second

    @pl.when(spot_ref[0] == 0)
    def _():
        mine_ref[:wide, :] = first
        other_ref[:wide, :] = second
        mine_ref[wide:, :] = query_ref[0]
        other_ref[wide:, :] = query_ref[1]

    @pl.when(spot_ref[0] != 0)
    def _():
        mine_ref[:wide, :] = second
        other_ref[:wide, :] = first
        mine_ref[wide:, :] = query_ref[1]
        other_ref[wide:, :] = query_ref[0]


def gathered(spot, pair, behind, ahead, behind_far, ahead_far, query):
    wide, rows = behind_far.shape
    operands = (pair, behind, ahead, behind_far, ahead_far, query)
    pack = jax.ShapeDtypeStruct((wide + query.shape[1], rows), bf16)
    both = jax.ShapeDtypeStruct((wide, 2 * rows), bf16)
    return pl.pallas_call(
        gather_kernel,
        grid_spec=pltpu.PrefetchScalarGridSpec(
            num_scalar_prefetch=1,
            grid=(1,),
            in_specs=[whole(value.shape) for value in operands],
            out_specs=[whole(both.shape), whole(pack.shape), whole(pack.shape)],
        ),
        out_shape=[both, pack, pack],
        compiler_params=params(),
        cost_estimate=lasting(3),
    )(spot, *operands)


def close_kernel(
    spot_ref, mine_ref, other_ref, inputs_ref, middle_back_ref, w_query_ref, w_keyval_ref,
    gain_ref, input_back_ref, gain_grad_ref, query_back, keyval_back
):
    inner = query_back.shape[0]
    each = inner // 2

    def put(first, second):
        keyval_back[:each, :] = first[:each, :]
        keyval_back[each : each + DH, :] = second[PAIR : PAIR + DH, :]
        keyval_back[each + DH : inner, :] = second[:PAIR, :]
        keyval_back[inner : inner + PAIR, :] = first[4 * DH : 6 * DH, :]
        keyval_back[inner + PAIR : inner + each, :] = first[3 * DH : 4 * DH, :]
        keyval_back[inner + each :, :] = second[3 * DH : 6 * DH, :]
        query_back[:each, :] = first[inner:, :]
        query_back[each : each + DH, :] = second[inner + PAIR :, :]
        query_back[each + DH :, :] = second[inner : inner + PAIR, :]

    @pl.when(spot_ref[0] == 0)
    def _():
        put(mine_ref, other_ref)

    @pl.when(spot_ref[0] != 0)
    def _():
        put(other_ref, mine_ref)

    inputs = inputs_ref[...].astype(f32)
    scale = lax.rsqrt(jnp.mean(inputs * inputs, axis=0, keepdims=True) + 1e-06)
    normed = inputs * scale
    back = dot_nn(w_query_ref[...], query_back[...]) + dot_nn(w_keyval_ref[...], keyval_back[...])
    gain_grad_ref[...] = as_row(jnp.sum(back * normed, axis=1, keepdims=True))
    normed_back = back * as_column(gain_ref[...])
    mean = jnp.mean(normed_back * normed, axis=0, keepdims=True)
    input_back_ref[...] = (
        middle_back_ref[...] + scale * (normed_back - normed * mean)
    ).astype(bf16)


def closed(spot, mine, other, inputs, middle_back, w_query, w_keyval, gain):
    width, rows = inputs.shape
    inner = w_query.shape[1]
    operands = (mine, other, inputs, middle_back, w_query, w_keyval, gain)
    return pl.pallas_call(
        close_kernel,
        grid_spec=pltpu.PrefetchScalarGridSpec(
            num_scalar_prefetch=1,
            grid=(1,),
            in_specs=[whole(value.shape) for value in operands],
            out_specs=[whole((width, rows)), whole((1, width))],
            scratch_shapes=[
                pltpu.VMEM((inner, rows), bf16),
                pltpu.VMEM((2 * inner, rows), bf16),
            ],
        ),
        out_shape=[
            jax.ShapeDtypeStruct((width, rows), bf16),
            jax.ShapeDtypeStruct((1, width), f32),
        ],
        compiler_params=params(),
        cost_estimate=lasting(18),
    )(spot, *operands)


def swapped(value, axis, bit):
    size = lax.axis_size(axis)
    return lax.ppermute(value, axis, [(i, i ^ bit) for i in range(size)])


def passed_along(value, axis, by):
    size = lax.axis_size(axis)
    pairs = [(i, i + by) for i in range(size) if 0 <= i + by < size]
    return lax.ppermute(value, axis, pairs)


def of_both(value, bit):
    size = lax.axis_size("seq")
    groups = [[i, i | bit] for i in range(size) if not i & bit]
    return lax.all_gather(value, "seq", axis=0, tiled=True, axis_index_groups=groups)


def chosen(value, dim, index):
    return lax.dynamic_index_in_dim(value, index, dim, keepdims=False)


def added(left, right):
    return (left.astype(f32) + right.astype(f32)).astype(bf16)


def parted(state, dims, bit):
    left, right = state
    dim = dims.index(bit)
    mine = (lax.axis_index("seq") // bit) % 2
    kept = added(chosen(left, dim, mine), chosen(right, dim, mine))
    sent = added(chosen(left, dim, 1 - mine), chosen(right, dim, 1 - mine))
    return kept, sent, dims[:dim] + dims[dim + 1 :]


def after(value, *others):
    return lax.optimization_barrier((value, *others))[0]


class Halving:
    def __init__(self, state, dims, order):
        self.kept, self.got = state
        self.dims, self.order = dims, list(order)

    def step(self, earlier):
        bit = self.order.pop(0)
        got = after(self.got, earlier)
        self.kept, sent, self.dims = parted((self.kept, got), self.dims, bit)
        self.got = swapped(sent, "seq", bit)
        return sent

    def total(self, dtype=bf16):
        return (self.kept.astype(f32) + self.got.astype(f32)).astype(dtype)


def on_device(
    tokens,
    cotangent,
    item_lengths,
    gain_attn,
    gain_ffn,
    rel_table,
    w_query,
    w_keyval,
    w_out,
    w_gateup,
    w_down,
):
    rows = tokens.shape[1]
    width = tokens.shape[2]
    part = width // 2
    inner = w_query.shape[1]
    blocks = lax.axis_size("seq")
    me = lax.axis_index("seq")
    core = lax.axis_index("dp").astype(jnp.int32)
    top, pair, third = blocks // 2, blocks // 4, blocks // 8
    low = [1 << i for i in range(blocks.bit_length() - 1)][:-2]

    inputs = tokens[0].T
    cotangent = cotangent[0].T
    w_out = w_out.T
    w_down = w_down.T
    gain_attn = gain_attn[None]
    gain_ffn = gain_ffn[None]

    def bit_of(bit):
        return ((me // bit) % 2).astype(jnp.int32)

    side = bit_of(1)
    half = bit_of(pair)
    down_half = bit_of(third)

    hidden_one, mine, other = opened(side[None], inputs, gain_attn, w_query, w_keyval)
    got = swapped(other, "seq", 1)
    blocks_here = me - side + jnp.arange(2, dtype=jnp.int32)
    ends = jnp.cumsum(item_lengths[0])
    own = jnp.sum((ends[None, :] <= blocks_here[:, None]).astype(jnp.int32), 1)
    labels = jnp.arange(item_lengths.shape[1], dtype=jnp.int32)
    mark = labels[None, :] == own[:, None]
    length = jnp.sum(jnp.where(mark, item_lengths[0][None, :], 0), 1)
    end = jnp.sum(jnp.where(mark, ends[None, :], 0), 1)
    place = jnp.concatenate([blocks_here - (end - length), length, side[None]]).astype(jnp.int32)
    keys = ITEM_MOST * rows
    turns = keys + rows
    shift = jnp.arange(turns, dtype=jnp.int32)
    relative = jnp.where(shift < keys, shift, shift - turns)[None, :] - place[:2, None] * rows
    onehot = (
        bucket_of(relative)[:, :, None] == jnp.arange(BUCKETS, dtype=jnp.int32)[None, None, :]
    ).astype(f32)
    table = jnp.where(
        side == 0,
        rel_table[:, :3],
        jnp.concatenate([rel_table[:, 4:6], rel_table[:, 3:4]], 1),
    )
    by_shift = jnp.sum(onehot[:, None] * table.T[None, :, None, :], -1)
    bias = window_bias(place, by_shift, rows)

    got = after(got, bias)
    keyvals, first, second = paired(side[None], mine, got)
    pieces = [
        passed_along(second, "seq", 4),
        passed_along(keyvals, "seq", 2),
        keyvals,
        passed_along(keyvals, "seq", -2),
        passed_along(first, "seq", -4),
    ]

    attended, attended_other, prob, window = attend(place, mine, got, pieces, bias)
    attended_got = swapped(attended_other, "seq", 1)
    upstream = turned_rows(after(cotangent, hidden_one))
    middle, hidden_two = middle_part(
        side[None], attended, attended_got, inputs, w_out, gain_ffn
    )
    hidden_far = swapped(hidden_two, "seq", pair)
    hidden_got = swapped(hidden_two, "seq", 1)
    hidden_far_got = swapped(hidden_far, "seq", 1)
    upstream_far = swapped(upstream, "seq", third)
    hidden_one_far = swapped(hidden_one, "seq", 1)

    mixed_first, back_first, *sums = ffn_half(
        False, jnp.stack([side, 1 - half]), hidden_two, upstream, w_gateup, w_down
    )
    back_far = swapped(back_first, "seq", pair)
    sums = after(tuple(sums), hidden_far, upstream_far, hidden_got)
    mixed_second, back, output, gain_ffn_grad, middle_back, branch, back_mine, back_other = ffn_half(
        True,
        jnp.stack([side, half]),
        hidden_two,
        upstream,
        w_gateup,
        w_down,
        (*sums, middle, gain_ffn, w_out, cotangent),
    )
    same = half == down_half
    mixed_far = swapped(jnp.where(same, mixed_first, mixed_second), "seq", third)
    back_got = swapped(back_other, "seq", 1)
    branch_far = swapped(after(branch, back_got), "seq", 1)
    back_mine = after(back_mine, hidden_one_far, hidden_far_got)

    backs = attend_back(place, mine, got, window, prob, back_mine, back_got)
    query_back, shift_sums = backs[:2]
    sends = backs[2:]

    def over_dp(kept, sent, dims):
        got = swapped(sent, "dp", 1)
        return tuple(
            value.reshape((2,) * dims + (value.shape[0] >> dims, value.shape[1]))
            for value in (kept, got)
        )

    spot = jnp.stack([core, side])
    units = mixed_first.shape[0]
    owned = units * 4 // blocks
    parts = 2 if owned % 32 == 0 else 1

    def other_owners(value):
        value = value.reshape(2, units // owned // 2, 2, owned, rows)
        return chosen(value, 2, 1 - side).reshape(2, units // 2, rows)

    back_got = swapped(other_owners(back), "seq", 1)
    back_far_sent = other_owners(back_far)
    back_far_got = swapped(back_far_sent, "seq", 1)
    down_kept, down_sent = pair_grad(
        jnp.stack([core, same.astype(jnp.int32)]),
        (2, lambda j: (0, j)),
        units // 2,
        1,
        (after(mixed_second, query_back, back_got, back_far_sent)[None], mixed_first[None]),
        mixed_far[None],
        upstream,
        upstream_far,
    )
    down = Halving(
        over_dp(down_kept, down_sent, len(low) + 1),
        [pair, top] + low[-2::-1],
        [pair] + low[-2::-1] + [top],
    )
    sent = down.step(down_kept)
    near_kept, near_sent, *far_grads = quad_grad(
        spot,
        owned,
        parts,
        (after(back, sent), back_far),
        (back_got, back_far_got),
        (hidden_two, hidden_far, hidden_got, hidden_far_got),
    )
    keyval_back, to_close, to_swap = gathered(
        side[None],
        after(sends[2], near_kept),
        passed_along(sends[3], "seq", 2),
        passed_along(sends[1], "seq", -2),
        passed_along(sends[4], "seq", 4),
        passed_along(sends[0], "seq", -4),
        query_back,
    )
    closed_with = swapped(to_swap, "seq", 1)
    gate_dims = [top] + low[:0:-1]
    gate_order = low[:0:-1] + [top]
    near = Halving(over_dp(near_kept, near_sent, len(low)), gate_dims, gate_order)
    far = None
    if parts == 2:
        far = Halving(over_dp(*far_grads, len(low)), gate_dims, gate_order)
    sent = keyval_back
    sent = near.step(sent)
    head_kept, head_sent = heads_grad(
        jnp.stack([core, side]),
        after(keyval_back, sent),
        query_back,
        (attended, attended_other),
        (hidden_one, hidden_one_far),
        (branch, branch_far),
    )
    others = [top, pair] + low[:0:-1]
    count = len(others)
    each = inner // 2

    def by_owner(value):
        def cut(array, bits):
            array = array.reshape((2,) * count + (-1, array.shape[-1]))
            return array.transpose([bits.index(bit) for bit in others] + [count, count + 1])

        asks = [pair] + low[:0:-1] + [top]
        keyvals = [top] + low[:0:-1] + [pair]
        return jnp.concatenate(
            [
                cut(value[:each], asks),
                cut(value[3 * each :], asks),
                cut(value[each : 3 * each], keyvals),
            ],
            -2,
        )

    head = Halving(
        (by_owner(head_kept), by_owner(swapped(head_sent, "dp", 1))),
        others,
        low[1:] + [pair, top],
    )
    sent = head_kept
    sent = far.step(sent) if far else sent
    input_back, gain_attn_grad = closed(
        side[None],
        after(to_close, sent),
        closed_with,
        inputs,
        middle_back,
        w_query,
        w_keyval,
        gain_attn,
    )

    sums = jnp.einsum(
        "pmb,phm->bh", onehot, shift_sums[:, :, 0], precision=lax.Precision.HIGHEST
    )
    nothing = jnp.zeros_like(sums)
    table_local = jnp.where(
        side == 0,
        jnp.concatenate([sums, nothing], 1),
        jnp.concatenate([nothing, sums[:, 2:], sums[:, :2]], 1),
    )
    small = jnp.concatenate(
        [gain_attn_grad.reshape(-1), gain_ffn_grad.reshape(-1), table_local.reshape(-1)]
    )
    taken = small.shape[0]
    small = jnp.pad(small, (0, -taken % 128)).reshape(-1, 128)
    small_got = swapped(small, "dp", 1)
    sent = gain_attn_grad
    small_order = low[::-1] + [pair, top]
    chains = [chain for chain in (near, far, down, head) if chain]
    while any(chain.order for chain in chains) or small_order:
        for chain in chains:
            if chain.order:
                sent = chain.step(sent)
            if small_order and chain in (head, near):
                small = small + after(small_got, sent)
                small_got = swapped(small, "seq", small_order.pop(0))
    small = small + after(small_got, sent)

    turn = [
        (i, (i & ~(top | third)) | (third if i & top else 0) | (top if i & third else 0))
        for i in range(blocks)
    ]
    down_grad = lax.ppermute(down.total(), "seq", turn).astype(f32)[:, :part]
    def exchanged(i, bit):
        return (i & ~(1 | bit)) | (1 if i & bit else 0) | (bit if i & 1 else 0)

    own_rows = inner // blocks
    head_sum = head.total()
    asks = lax.ppermute(
        head_sum[: 2 * own_rows], "seq", [(i, exchanged(i, top)) for i in range(blocks)]
    ).astype(f32)
    query_grad = asks[:own_rows, :part].T
    out_grad = asks[own_rows:, :part]
    keyval_grad = (
        lax.ppermute(
            head_sum[2 * own_rows :], "seq", [(i, exchanged(i, pair)) for i in range(blocks)]
        )
        .astype(f32)[:, :part]
        .T
    )
    gateup_grad = jnp.concatenate([one.total(f32)[:, :part].T for one in (near, far) if one], 1)
    small = small.reshape(-1)
    return (
        output.T[None],
        input_back.T[None],
        small[:width],
        small[width : 2 * width],
        small[2 * width : taken].reshape(BUCKETS, H),
        query_grad,
        keyval_grad,
        out_grad,
        gateup_grad,
        down_grad,
    )


def solution(mesh):
    placed = (
        P("dp", "seq", None),
        P("dp", "seq", None),
        P("dp", None),
        P(),
        P(),
        P(),
        P(),
        P(),
        P(),
        P(),
        P(),
    )
    return jax.shard_map(
        on_device,
        mesh=mesh,
        in_specs=placed,
        out_specs=(
            P("dp", "seq", None),
            P("dp", "seq", None),
            P(),
            P(),
            P(),
            P("dp", "seq"),
            P("dp", "seq"),
            P("seq", "dp"),
            P("dp", "seq"),
            P("seq", "dp"),
        ),
        check_vma=False,
    )
```

```python
import functools

import jax
import jax.numpy as jnp
from jax import lax
from jax.experimental import pallas as pl
from jax.experimental.pallas import tpu as pltpu
from jax.sharding import PartitionSpec as P

H = 6
DH = 64
BUCKETS = 32
ITEM_MOST = 4
REACH = ITEM_MOST - 1
PAIR = 2 * DH
UNITS = 896

bucket_edges = (12, 16, 23, 32, 46, 64, 91)
negative_fill = -1e30
f32 = jnp.float32
bf16 = jnp.bfloat16
VMEM_MOST = 56 * 1024 * 1024
FLOPS_PER_US = 5_000_000_000


def bucket_of(relative):
    ahead = jnp.where(relative > 0, 16, 0).astype(jnp.int32)
    distance = jnp.abs(relative)
    beyond = 8 + sum(((distance >= edge).astype(jnp.int32) for edge in bucket_edges))
    return ahead + jnp.where(distance < 8, distance, beyond)


def dot_nn(left, right):
    return lax.dot_general(left, right, (((1,), (0,)), ((), ())), preferred_element_type=f32)


def dot_nt(left, right):
    return lax.dot_general(left, right, (((1,), (1,)), ((), ())), preferred_element_type=f32)


def dot_tn(left, right):
    return lax.dot_general(left, right, (((0,), (0,)), ((), ())), preferred_element_type=f32)


def rms_scale(values):
    return lax.rsqrt(jnp.mean(values * values, axis=-1, keepdims=True) + 1e-06)


def lasting(microseconds):
    return pl.CostEstimate(
        flops=int(microseconds * FLOPS_PER_US), bytes_accessed=0, transcendentals=0
    )


def whole(shape):
    return pl.BlockSpec(shape, lambda *_: (0,) * len(shape))


def params():
    return pltpu.CompilerParams(vmem_limit_bytes=VMEM_MOST)


def up_to(count, step):
    return -(-count // step) * step


def spread_width(width):
    return 2 * up_to(width // 2, 128)


def spread_rows(out, value, gain=None):
    half = value.shape[0] // 2
    each = out.shape[1] // 2
    nothing = jnp.zeros((out.shape[0], each - half), out.dtype)
    for index in range(2):
        part = value[index * half : (index + 1) * half].T
        if gain is not None:
            part = part * gain[:, index * half : (index + 1) * half]
        out[:, index * each : index * each + half] = part.astype(out.dtype)
        out[:, index * each + half : (index + 1) * each] = nothing


def spread_depth(value, wide):
    half = value.shape[0] // 2
    nothing = jnp.zeros((wide // 2 - half, value.shape[1]), value.dtype)
    return jnp.concatenate([value[:half], nothing, value[half:], nothing], 0)


def as_column(row):
    return jnp.broadcast_to(row, (128, row.shape[1])).T[:, :1]


def as_row(column):
    return jnp.broadcast_to(column, (column.shape[0], 128)).T[:1]


def shift_by_head(value):
    return pltpu.roll(value, DH, 1)


def columns(value, index):
    return value[:, index * PAIR : (index + 1) * PAIR]


def low_lanes(shape):
    return lax.broadcasted_iota(jnp.int32, shape, len(shape) - 1) % PAIR < DH


def packed_heads(query, keyval, half):
    low = low_lanes((query.shape[0], PAIR))
    key = [columns(keyval, i) for i in range(3)]
    value = [columns(keyval, i + 3) for i in range(3)]
    ask = [columns(query, i) for i in range(3)]
    if half == 0:
        parts = [
            key[0],
            jnp.where(low, key[1], shift_by_head(value[1])),
            value[0],
            ask[0],
            jnp.where(low, ask[1], 0.0),
        ]
    else:
        parts = [
            key[2],
            jnp.where(low, shift_by_head(key[1]), value[1]),
            value[2],
            ask[2],
            jnp.where(low, shift_by_head(ask[1]), 0.0),
        ]
    return jnp.concatenate(parts, 1).astype(bf16)


def open_kernel(
    spot_ref, inputs_ref, gain_ref, w_query_ref, w_keyval_ref, hidden_ref, mine_ref, other_ref
):
    inputs = inputs_ref[...].astype(f32)
    scale = lax.rsqrt(jnp.mean(inputs * inputs, axis=0, keepdims=True) + 1e-06)
    spread_rows(hidden_ref, inputs * scale, gain_ref[...])
    hidden = hidden_ref[...]
    wide = hidden.shape[1]
    keyval = dot_nn(hidden, spread_depth(w_keyval_ref[...], wide))
    query = dot_nn(hidden, spread_depth(w_query_ref[...], wide))
    first = packed_heads(query, keyval, 0)
    second = packed_heads(query, keyval, 1)

    @pl.when(spot_ref[0] == 0)
    def _():
        mine_ref[...] = first
        other_ref[...] = second

    @pl.when(spot_ref[0] != 0)
    def _():
        mine_ref[...] = second
        other_ref[...] = first


def opened(spot, inputs, gain, w_query, w_keyval):
    width, rows = inputs.shape
    inner = w_query.shape[1]
    pack = jax.ShapeDtypeStruct((rows, 5 * PAIR), bf16)
    return pl.pallas_call(
        open_kernel,
        grid_spec=pltpu.PrefetchScalarGridSpec(
            num_scalar_prefetch=1,
            grid=(1,),
            in_specs=[
                whole((width, rows)),
                whole((1, width)),
                whole((width, inner)),
                whole((width, 2 * inner)),
            ],
            out_specs=[
                whole((rows, spread_width(width))),
                whole(pack.shape),
                whole(pack.shape),
            ],
        ),
        out_shape=[jax.ShapeDtypeStruct((rows, spread_width(width)), bf16), pack, pack],
        compiler_params=params(),
        cost_estimate=lasting(5),
    )(spot, inputs, gain, w_query, w_keyval)


def turn_kernel(in_ref, out_ref):
    spread_rows(out_ref, in_ref[...])


def turned_rows(value):
    width, rows = value.shape
    return pl.pallas_call(
        turn_kernel,
        out_shape=jax.ShapeDtypeStruct((rows, spread_width(width)), value.dtype),
        compiler_params=params(),
        cost_estimate=lasting(2),
    )(value)


def bias_kernel(place_ref, by_shift_ref, out_ref):
    rows, keys = out_ref.shape[2:]
    wide = by_shift_ref.shape[-1]
    spread = jnp.broadcast_to(by_shift_ref[0, 0], (rows, wide))
    turned = pltpu.roll(spread, 0, 1, stride=1, stride_axis=0)[:, :keys]
    key = lax.broadcasted_iota(jnp.int32, (rows, keys), 1)
    length = place_ref[2 + pl.program_id(0)]
    out_ref[0, 0] = jnp.where(key < length * rows, turned, negative_fill)


def window_bias(place, by_shift, rows):
    keys = ITEM_MOST * rows
    both, heads, wide = by_shift.shape
    return pl.pallas_call(
        bias_kernel,
        grid_spec=pltpu.PrefetchScalarGridSpec(
            num_scalar_prefetch=1,
            grid=(both, heads),
            in_specs=[pl.BlockSpec((1, 1, 1, wide), lambda b, h, _: (b, h, 0, 0))],
            out_specs=pl.BlockSpec((1, 1, rows, keys), lambda b, h, _: (b, h, 0, 0)),
        ),
        out_shape=jax.ShapeDtypeStruct((both, heads, rows, keys), f32),
        compiler_params=params(),
        cost_estimate=lasting(6),
    )(place, by_shift.reshape(both, heads, 1, wide))


SLOTS = 2 * REACH + 2


def pair_kernel(spot_ref, mine_ref, got_ref, both_ref, first_ref, second_ref):
    rows = mine_ref.shape[0]
    wide = first_ref.shape[1]
    mine, got = mine_ref[:, :wide], got_ref[:, :wide]

    def put(first, second):
        first_ref[...] = first
        second_ref[...] = second
        both_ref[:rows, :] = first
        both_ref[rows:, :] = second

    @pl.when(spot_ref[0] == 0)
    def _():
        put(mine, got)

    @pl.when(spot_ref[0] != 0)
    def _():
        put(got, mine)


def paired(spot, mine, got):
    rows = mine.shape[0]
    shapes = [(2 * rows, 3 * PAIR), (rows, 3 * PAIR), (rows, 3 * PAIR)]
    return pl.pallas_call(
        pair_kernel,
        grid_spec=pltpu.PrefetchScalarGridSpec(
            num_scalar_prefetch=1,
            grid=(1,),
            in_specs=[whole(mine.shape)] * 2,
            out_specs=[whole(shape) for shape in shapes],
        ),
        out_shape=[jax.ShapeDtypeStruct(shape, bf16) for shape in shapes],
        compiler_params=params(),
        cost_estimate=lasting(1),
    )(spot, mine, got)


GROUPS = ((0, 2), (0, 2), (1, 1))


def spread_heads(own, mine, got):
    value = jnp.where(own, mine, got)
    first = columns(value, 0)
    low = low_lanes(first.shape)
    nothing = jnp.zeros_like(first)
    return jnp.where(low, first, nothing), jnp.where(low, nothing, first), columns(value, 1)


def attend_kernel(
    place_ref, mine_ref, got_ref, behind_far, behind, pair_ref, ahead, ahead_far, bias_ref,
    attended_mine, attended_other, prob_ref, window_ref
):
    rows = mine_ref.shape[0]
    wide = window_ref.shape[1]
    block = pl.program_id(0)
    own = block == place_ref[4]

    @pl.when(block == 0)
    def _():
        at = 0
        for piece in (behind_far, behind, pair_ref, ahead, ahead_far):
            window_ref[at : at + piece.shape[0], :] = piece[...]
            at += piece.shape[0]

    asks = spread_heads(own, mine_ref[:, wide:], got_ref[:, wide:])
    start = pl.multiple_of((REACH + block - place_ref[block]) * rows, rows)
    window = window_ref[pl.ds(start, ITEM_MOST * rows), :]
    parts = []
    for head, (key, value) in enumerate(GROUPS):
        scores = dot_nt(asks[head], columns(window, key)) + bias_ref[0, head]
        exponent = jnp.exp(scores - jnp.max(scores, axis=-1, keepdims=True))
        prob = exponent / jnp.sum(exponent, axis=-1, keepdims=True)
        prob_ref[0, head] = prob
        parts.append(dot_nn(prob.astype(bf16), columns(window, value)))

    def put(out):
        low = low_lanes((rows, PAIR))
        out[:PAIR, :] = jnp.where(low, parts[0], parts[1]).T.astype(bf16)
        out[PAIR:, :] = parts[2].T[DH:].astype(bf16)

    @pl.when(own)
    def _():
        put(attended_mine)

    @pl.when(jnp.logical_not(own))
    def _():
        put(attended_other)


def attend(place, mine, got, pieces, bias):
    rows = mine.shape[0]
    keys = ITEM_MOST * rows
    wide = pieces[0].shape[1]
    heads = bias.shape[1]
    tall = pl.BlockSpec((1, heads, rows, keys), lambda b, _: (b, 0, 0, 0))
    return pl.pallas_call(
        attend_kernel,
        grid_spec=pltpu.PrefetchScalarGridSpec(
            num_scalar_prefetch=1,
            grid=(2,),
            in_specs=[whole(mine.shape)] * 2 + [whole(piece.shape) for piece in pieces] + [tall],
            out_specs=[
                whole((heads * DH, rows)),
                whole((heads * DH, rows)),
                tall,
                whole((SLOTS * rows, wide)),
            ],
        ),
        out_shape=[
            jax.ShapeDtypeStruct((heads * DH, rows), bf16),
            jax.ShapeDtypeStruct((heads * DH, rows), bf16),
            jax.ShapeDtypeStruct((2, heads, rows, keys), f32),
            jax.ShapeDtypeStruct((SLOTS * rows, wide), bf16),
        ],
        compiler_params=params(),
        cost_estimate=lasting(9),
    )(place, mine, got, *pieces, bias)


def natural_heads(half, mine, other, out):
    each = mine.shape[0]

    def put(first, second):
        out[:each, :] = first[...]
        out[each : each + DH, :] = second[PAIR:, :]
        out[each + DH :, :] = second[:PAIR, :]

    @pl.when(half == 0)
    def _():
        put(mine, other)

    @pl.when(half != 0)
    def _():
        put(other, mine)


def middle_kernel(
    spot_ref, mine_ref, other_ref, inputs_ref, w_out_ref, gain_ref, middle_ref, hidden_ref, attended
):
    natural_heads(spot_ref[0], mine_ref, other_ref, attended)
    middle = inputs_ref[...].astype(f32) + dot_nn(w_out_ref[...], attended[...])
    middle_ref[...] = middle
    scale = lax.rsqrt(jnp.mean(middle * middle, axis=0, keepdims=True) + 1e-06)
    spread_rows(hidden_ref, middle * scale, gain_ref[...])


def middle_part(spot, mine, other, inputs, w_out, gain):
    width, rows = inputs.shape
    inner = w_out.shape[1]
    return pl.pallas_call(
        middle_kernel,
        grid_spec=pltpu.PrefetchScalarGridSpec(
            num_scalar_prefetch=1,
            grid=(1,),
            in_specs=[
                whole(mine.shape),
                whole(other.shape),
                whole((width, rows)),
                whole((width, inner)),
                whole((1, width)),
            ],
            out_specs=[whole((width, rows)), whole((rows, spread_width(width)))],
            scratch_shapes=[pltpu.VMEM((inner, rows), bf16)],
        ),
        out_shape=[
            jax.ShapeDtypeStruct((width, rows), f32),
            jax.ShapeDtypeStruct((rows, spread_width(width)), bf16),
        ],
        compiler_params=params(),
        cost_estimate=lasting(4),
    )(spot, mine, other, inputs, w_out, gain)


GELU_A = 0.7978845608028654
GELU_B = 0.044715


def packed_back(back, half):
    low = low_lanes((back.shape[0], PAIR))
    middle = columns(back, 1)
    if half == 0:
        parts = [columns(back, 0), jnp.where(low, 0.0, shift_by_head(middle))]
    else:
        parts = [columns(back, 2), jnp.where(low, 0.0, middle)]
    return jnp.concatenate(parts, 1).astype(bf16)


def ffn_kernel(last, spot_ref, hidden_ref, upstream_ref, gate_w_ref, up_w_ref, down_w_ref, *refs):
    if last:
        out_in, back_in, middle_ref, gain_ref, w_out_ref, cotangent_ref = refs[:6]
        (mixed_ref, both_ref, output_ref, gain_grad_ref, middle_back_ref,
         branch_ref, back_mine_ref, back_other_ref, out_ref, back_ref) = refs[6:]
    else:
        mixed_ref, both_ref, out_ref, back_ref = refs
    step = pl.program_id(0)
    units = gate_w_ref.shape[1]
    hidden = hidden_ref[...]
    wide = hidden.shape[1]
    upstream = upstream_ref[...]
    gateup_w = jnp.concatenate([gate_w_ref[...], up_w_ref[...]], 1)
    gateup = dot_nn(hidden, spread_depth(gateup_w, wide))
    gate, up = gateup[:, :units], gateup[:, units:]
    mixed_back = dot_nn(upstream, spread_depth(down_w_ref[...], wide))
    squared = gate * gate
    bent = jnp.tanh(GELU_A * (gate + GELU_B * (squared * gate)))
    share = 0.5 * (1.0 + bent)
    gelu = gate * share
    slope = share + 0.5 * gate * (1.0 - bent * bent) * (GELU_A * (1.0 + 3.0 * GELU_B * squared))
    mixed = (gelu * up).astype(bf16).T
    gate_back = (mixed_back * up * slope).astype(bf16).T
    up_back = (mixed_back * gelu).astype(bf16).T
    mixed_ref[...] = mixed
    both_ref[0] = gate_back
    both_ref[1] = up_back
    forward = dot_nn(down_w_ref[...], mixed)
    backward = dot_nn(gateup_w, jnp.concatenate([gate_back, up_back], 0))

    @pl.when(step == 0)
    def _():
        if last:
            out_ref[...] = out_in[...] + forward
            back_ref[...] = back_in[...] + backward
        else:
            out_ref[...] = forward
            back_ref[...] = backward

    @pl.when(step > 0)
    def _():
        out_ref[...] += forward
        back_ref[...] += backward

    if not last:
        return

    @pl.when(step == pl.num_programs(0) - 1)
    def _():
        middle = middle_ref[...]
        output_ref[...] = (middle + out_ref[...]).astype(bf16)
        scale = lax.rsqrt(jnp.mean(middle * middle, axis=0, keepdims=True) + 1e-06)
        normed = middle * scale
        back = back_ref[...]
        gain_grad_ref[...] = as_row(jnp.sum(back * normed, axis=1, keepdims=True))
        normed_back = back * as_column(gain_ref[...])
        mean = jnp.mean(normed_back * normed, axis=0, keepdims=True)
        middle_back = cotangent_ref[...].astype(f32) + scale * (normed_back - normed * mean)
        middle_back_ref[...] = middle_back
        spread_rows(branch_ref, middle_back)
        attended_back = dot_nn(branch_ref[...], spread_depth(w_out_ref[...], wide))
        first = packed_back(attended_back, 0)
        second = packed_back(attended_back, 1)

        @pl.when(spot_ref[0] == 0)
        def _():
            back_mine_ref[...] = first
            back_other_ref[...] = second

        @pl.when(spot_ref[0] != 0)
        def _():
            back_mine_ref[...] = second
            back_other_ref[...] = first


def ffn_half(last, spot, hidden, upstream, w_gateup, w_down, more=()):
    rows, wide = hidden.shape
    width, units = w_down.shape
    steps = units // 2 // UNITS
    both = units // UNITS
    in_specs = [
        whole((rows, wide)),
        whole((rows, wide)),
        pl.BlockSpec((width, UNITS), lambda j, s: (0, s[1] * steps + j)),
        pl.BlockSpec((width, UNITS), lambda j, s: (0, both + s[1] * steps + j)),
        pl.BlockSpec((width, UNITS), lambda j, s: (0, s[1] * steps + j)),
    ] + [whole(value.shape) for value in more]
    sums = [jax.ShapeDtypeStruct((width, rows), f32)] * 2
    out_specs = [
        pl.BlockSpec((UNITS, rows), lambda j, s: (j, 0)),
        pl.BlockSpec((2, UNITS, rows), lambda j, s: (0, j, 0)),
    ]
    out_shape = [
        jax.ShapeDtypeStruct((units // 2, rows), bf16),
        jax.ShapeDtypeStruct((2, units // 2, rows), bf16),
    ]
    if last:
        rest = [
            jax.ShapeDtypeStruct((width, rows), bf16),
            jax.ShapeDtypeStruct((1, width), f32),
            jax.ShapeDtypeStruct((width, rows), f32),
            jax.ShapeDtypeStruct((rows, wide), bf16),
            jax.ShapeDtypeStruct((rows, 2 * PAIR), bf16),
            jax.ShapeDtypeStruct((rows, 2 * PAIR), bf16),
        ]
    else:
        rest = sums
    return pl.pallas_call(
        functools.partial(ffn_kernel, last),
        grid_spec=pltpu.PrefetchScalarGridSpec(
            num_scalar_prefetch=1,
            grid=(steps,),
            in_specs=in_specs,
            out_specs=out_specs + [whole(value.shape) for value in rest],
            scratch_shapes=[pltpu.VMEM((width, rows), f32)] * 2 if last else [],
        ),
        out_shape=out_shape + rest,
        compiler_params=params(),
        cost_estimate=lasting(20),
    )(spot, hidden, upstream, w_gateup, w_gateup, w_down, *more)


def half_of(ref, index):
    each = ref.shape[1] // 2
    return ref[:, pl.ds(pl.multiple_of(index * each, 128), each)]


def pair_grad_kernel(
    parts, spot_ref, left_own, left_other, left_far, right_own, right_far, *refs
):
    outs, halves = refs[:-1], refs[-1]
    rows = left_far.shape[-1]
    mine = spot_ref[0]

    @pl.when(pl.program_id(0) == 0)
    def _():
        for index, right in enumerate((right_own, right_far)):
            at = slice(index * rows, (index + 1) * rows)
            halves[0, at, :] = half_of(right, mine)
            halves[1, at, :] = half_of(right, 1 - mine)

    own = left_own[0] if left_other is None else jnp.where(spot_ref[1] != 0, left_own[0], left_other[0])
    left = jnp.concatenate([own, left_far[0]], 1)
    each = left.shape[0] // parts
    for half in range(2):
        product = dot_nn(left, halves[half]).astype(bf16)
        for part in range(parts):
            outs[2 * part + half][...] = product[part * each : (part + 1) * each]


def pair_grad(spot, tiles, tile, parts, left_own, left_far, right_own, right_far):
    count, place = tiles
    rows = left_far.shape[-1]
    wide = right_own.shape[1] // 2
    each = tile // parts
    out = jax.ShapeDtypeStruct((count * each, wide), bf16)
    left = pl.BlockSpec((1, tile, rows), lambda j, _: (*place(j), 0))

    def kernel(spot_ref, *refs):
        if len(left_own) == 1:
            pair_grad_kernel(parts, spot_ref, refs[0], None, *refs[1:])
        else:
            pair_grad_kernel(parts, spot_ref, *refs)

    return pl.pallas_call(
        kernel,
        grid_spec=pltpu.PrefetchScalarGridSpec(
            num_scalar_prefetch=1,
            grid=(count,),
            in_specs=[left] * (len(left_own) + 1) + [whole(right_own.shape), whole(right_far.shape)],
            out_specs=[pl.BlockSpec((each, wide), lambda j, _: (j, 0))] * (2 * parts),
            scratch_shapes=[pltpu.VMEM((2, 2 * rows, wide), bf16)],
        ),
        out_shape=[out] * (2 * parts),
        compiler_params=params(),
        cost_estimate=lasting(24),
    )(spot, *left_own, left_far, right_own, right_far)


def quad_grad_kernel(
    parts, spot_ref, left_own, left_far, left_own_got, left_far_got, *refs
):
    rights, outs, halves = refs[:4], refs[4:-1], refs[-1]
    rows = left_own.shape[-1]
    mine = spot_ref[0]

    @pl.when((pl.program_id(0) == 0) & (pl.program_id(1) == 0))
    def _():
        for index, right in enumerate(rights):
            at = slice(index * rows, (index + 1) * rows)
            halves[0, at, :] = half_of(right, mine)
            halves[1, at, :] = half_of(right, 1 - mine)

    left = jnp.concatenate([left_own[0], left_far[0], left_own_got[0], left_far_got[0]], 1)
    each = left.shape[0] // parts
    for half in range(2):
        product = dot_nn(left, halves[half]).astype(bf16)
        for part in range(parts):
            outs[2 * part + half][...] = product[part * each : (part + 1) * each]


def quad_grad(spot, owned, parts, lefts, lefts_got, rights):
    groups, units, rows = lefts_got[0].shape
    wide = rights[0].shape[1] // 2
    runs = units // owned
    each = owned // parts
    out = jax.ShapeDtypeStruct((groups * runs * each, wide), bf16)
    return pl.pallas_call(
        functools.partial(quad_grad_kernel, parts),
        grid_spec=pltpu.PrefetchScalarGridSpec(
            num_scalar_prefetch=1,
            grid=(groups, runs),
            in_specs=[pl.BlockSpec((1, owned, rows), lambda g, j, s: (g, 2 * j + s[1], 0))] * 2
            + [pl.BlockSpec((1, owned, rows), lambda g, j, s: (g, j, 0))] * 2
            + [whole(right.shape) for right in rights],
            out_specs=[pl.BlockSpec((each, wide), lambda g, j, s: (g * runs + j, 0))] * (2 * parts),
            scratch_shapes=[pltpu.VMEM((2, 4 * rows, wide), bf16)],
        ),
        out_shape=[out] * (2 * parts),
        compiler_params=params(),
        cost_estimate=lasting(12),
    )(spot, *lefts, *lefts_got, *rights)


def heads_grad_kernel(
    spot_ref, keyval_ref, query_ref, attended_own, attended_far, hidden_own, hidden_far, branch_own,
    branch_far, kept_ref, sent_ref, low, high, left
):
    rows = hidden_own.shape[0]
    mine, half = spot_ref[0], spot_ref[1]
    each = query_ref.shape[1]

    def ordered(source, at, first, second):
        @pl.when(half == 0)
        def _():
            for start, stop, to in first:
                left[at + to : at + to + stop - start, :] = source(start, stop)

        @pl.when(half != 0)
        def _():
            for start, stop, to in second:
                left[at + to : at + to + stop - start, :] = source(start, stop)

    same = ((0, 3 * DH, 0),)
    turned = ((PAIR, 3 * DH, 0), (0, PAIR, DH))
    value_first = ((4 * DH, 6 * DH, 0), (3 * DH, 4 * DH, PAIR))
    value_second = ((3 * DH, 6 * DH, 0),)

    def joined(ref):
        return lambda start, stop: jnp.concatenate(
            [ref[0, start:stop, :], ref[1, start:stop, :]], 1
        )

    def plain(start, stop):
        return keyval_ref[start:stop, :]

    ordered(joined(query_ref), 0, same, turned)
    ordered(plain, each, same, turned)
    ordered(plain, 2 * each, value_first, value_second)

    def by_side(start, stop):
        own, far = attended_own[start:stop, :], attended_far[start:stop, :]
        first = jnp.where(half == 0, own, far)
        second = jnp.where(half == 0, far, own)
        return jnp.concatenate([first, second], 1)

    ordered(by_side, 3 * each, same, turned)
    for own, far, at, stop in (
        (hidden_own, hidden_far, 0, 3 * each),
        (branch_own, branch_far, 3 * each, 4 * each),
    ):
        for index, source in ((0, own), (1, far)):

            @pl.when(half == index)
            def _():
                low[:rows, :] = half_of(source, mine)
                high[:rows, :] = half_of(source, 1 - mine)

            @pl.when(half != index)
            def _():
                low[rows:, :] = half_of(source, mine)
                high[rows:, :] = half_of(source, 1 - mine)

        kept_ref[at:stop, :] = dot_nn(left[at:stop, :], low[...]).astype(bf16)
        sent_ref[at:stop, :] = dot_nn(left[at:stop, :], high[...]).astype(bf16)


def heads_grad(spot, keyval, query, attended, hiddens, branches):
    wide = hiddens[0].shape[1] // 2
    rows = hiddens[0].shape[0]
    each = query.shape[1]
    out = jax.ShapeDtypeStruct((4 * each, wide), bf16)
    operands = (keyval, query, *attended, *hiddens, *branches)
    return pl.pallas_call(
        heads_grad_kernel,
        grid_spec=pltpu.PrefetchScalarGridSpec(
            num_scalar_prefetch=1,
            grid=(1,),
            in_specs=[whole(value.shape) for value in operands],
            out_specs=[whole(out.shape)] * 2,
            scratch_shapes=[pltpu.VMEM((2 * rows, wide), bf16)] * 2
            + [pltpu.VMEM((4 * each, 2 * rows), bf16)],
        ),
        out_shape=[out, out],
        compiler_params=params(),
        cost_estimate=lasting(2.1),
    )(spot, *operands)


def attend_back_kernel(
    place_ref, mine_ref, got_ref, window_ref, prob_ref, back_mine, back_got, query_back_ref,
    by_shift_ref, behind_far, behind, pair_ref, ahead, ahead_far, total
):
    rows = mine_ref.shape[0]
    wide = window_ref.shape[1]
    keys = ITEM_MOST * rows
    block = pl.program_id(0)
    own = block == place_ref[4]
    asks = spread_heads(own, mine_ref[:, wide:], got_ref[:, wide:])
    backs = spread_heads(own, back_mine[...], back_got[...])

    @pl.when(block == 0)
    def _():
        total[...] = jnp.zeros_like(total)

    start = pl.multiple_of((REACH + block - place_ref[block]) * rows, rows)
    window = window_ref[pl.ds(start, keys), :]
    row = lax.broadcasted_iota(jnp.int32, (rows, rows), 0)
    column = lax.broadcasted_iota(jnp.int32, (rows, rows), 1)
    flip = jnp.where(row + column == rows - 1, 1.0, 0.0).astype(bf16)
    parts, sums = [], [None] * 3
    for head, (key, value) in enumerate(GROUPS):
        prob = prob_ref[0, head]
        prob_back = dot_nt(backs[head], columns(window, value))
        delta = jnp.sum(prob * prob_back, axis=-1, keepdims=True)
        score_back = (prob * (prob_back - delta)).astype(bf16)
        parts.append(dot_nn(score_back, columns(window, key)))
        key_part = dot_tn(asks[head], score_back)
        value_part = dot_tn(backs[head], prob.astype(bf16))
        for group, add in ((key, key_part), (value, value_part)):
            sums[group] = add if sums[group] is None else sums[group] + add
        flipped = jnp.concatenate([dot_nn(flip, score_back), jnp.zeros((rows, rows), f32)], 1)
        turned = pltpu.roll(flipped, keys + 1, 1, stride=1, stride_axis=0)
        by_shift_ref[0, head] = jnp.sum(turned, axis=0, keepdims=True)
    low = low_lanes((rows, PAIR))
    query_back_ref[0, :PAIR, :] = jnp.where(low, parts[0], parts[1]).T.astype(bf16)
    query_back_ref[0, PAIR:, :] = parts[2].T[:DH].astype(bf16)
    for group in range(3):
        total[group * PAIR : (group + 1) * PAIR, pl.ds(start, keys)] += sums[group]

    @pl.when(block == 1)
    def _():
        at = 0
        for out in (behind_far, behind, pair_ref, ahead, ahead_far):
            out[...] = total[:, at : at + out.shape[1]].astype(out.dtype)
            at += out.shape[1]


def attend_back(place, mine, got, window, prob, back_mine, back_got):
    rows = mine.shape[0]
    _, heads, _, keys = prob.shape
    wide = window.shape[1]
    pieces = [(rows, bf16), (2 * rows, bf16), (2 * rows, f32), (2 * rows, bf16), (rows, bf16)]
    return pl.pallas_call(
        attend_back_kernel,
        grid_spec=pltpu.PrefetchScalarGridSpec(
            num_scalar_prefetch=1,
            grid=(2,),
            in_specs=[
                whole(mine.shape),
                whole(got.shape),
                whole(window.shape),
                pl.BlockSpec((1, heads, rows, keys), lambda b, _: (b, 0, 0, 0)),
                whole(back_mine.shape),
                whole(back_got.shape),
            ],
            out_specs=[
                pl.BlockSpec((1, heads * DH, rows), lambda b, _: (b, 0, 0)),
                pl.BlockSpec((1, heads, 1, keys + rows), lambda b, _: (b, 0, 0, 0)),
            ]
            + [whole((wide, count)) for count, _ in pieces],
            scratch_shapes=[
                pltpu.VMEM((wide, SLOTS * rows), f32),
            ],
        ),
        out_shape=[
            jax.ShapeDtypeStruct((2, heads * DH, rows), bf16),
            jax.ShapeDtypeStruct((2, heads, 1, keys + rows), f32),
        ]
        + [jax.ShapeDtypeStruct((wide, count), dtype) for count, dtype in pieces],
        compiler_params=params(),
        cost_estimate=lasting(3.6),
    )(place, mine, got, window, prob, back_mine, back_got)


def gather_kernel(
    spot_ref, pair_ref, behind, ahead, behind_far, ahead_far, query_ref, both_ref, mine_ref,
    other_ref
):
    rows = behind_far.shape[1]
    wide = pair_ref.shape[0]
    total = pair_ref[...] + behind[...].astype(f32) + ahead[...].astype(f32)
    first = (total[:, :rows] + behind_far[...].astype(f32)).astype(bf16)
    second = (total[:, rows:] + ahead_far[...].astype(f32)).astype(bf16)
    both_ref[:, :rows] = first
    both_ref[:, rows:] = second

    @pl.when(spot_ref[0] == 0)
    def _():
        mine_ref[:wide, :] = first
        other_ref[:wide, :] = second
        mine_ref[wide:, :] = query_ref[0]
        other_ref[wide:, :] = query_ref[1]

    @pl.when(spot_ref[0] != 0)
    def _():
        mine_ref[:wide, :] = second
        other_ref[:wide, :] = first
        mine_ref[wide:, :] = query_ref[1]
        other_ref[wide:, :] = query_ref[0]


def gathered(spot, pair, behind, ahead, behind_far, ahead_far, query):
    wide, rows = behind_far.shape
    operands = (pair, behind, ahead, behind_far, ahead_far, query)
    pack = jax.ShapeDtypeStruct((wide + query.shape[1], rows), bf16)
    both = jax.ShapeDtypeStruct((wide, 2 * rows), bf16)
    return pl.pallas_call(
        gather_kernel,
        grid_spec=pltpu.PrefetchScalarGridSpec(
            num_scalar_prefetch=1,
            grid=(1,),
            in_specs=[whole(value.shape) for value in operands],
            out_specs=[whole(both.shape), whole(pack.shape), whole(pack.shape)],
        ),
        out_shape=[both, pack, pack],
        compiler_params=params(),
        cost_estimate=lasting(3),
    )(spot, *operands)


def close_kernel(
    spot_ref, mine_ref, other_ref, inputs_ref, middle_back_ref, w_query_ref, w_keyval_ref,
    gain_ref, input_back_ref, gain_grad_ref, query_back, keyval_back
):
    inner = query_back.shape[0]
    each = inner // 2

    def put(first, second):
        keyval_back[:each, :] = first[:each, :]
        keyval_back[each : each + DH, :] = second[PAIR : PAIR + DH, :]
        keyval_back[each + DH : inner, :] = second[:PAIR, :]
        keyval_back[inner : inner + PAIR, :] = first[4 * DH : 6 * DH, :]
        keyval_back[inner + PAIR : inner + each, :] = first[3 * DH : 4 * DH, :]
        keyval_back[inner + each :, :] = second[3 * DH : 6 * DH, :]
        query_back[:each, :] = first[inner:, :]
        query_back[each : each + DH, :] = second[inner + PAIR :, :]
        query_back[each + DH :, :] = second[inner : inner + PAIR, :]

    @pl.when(spot_ref[0] == 0)
    def _():
        put(mine_ref, other_ref)

    @pl.when(spot_ref[0] != 0)
    def _():
        put(other_ref, mine_ref)

    inputs = inputs_ref[...].astype(f32)
    scale = lax.rsqrt(jnp.mean(inputs * inputs, axis=0, keepdims=True) + 1e-06)
    normed = inputs * scale
    back = dot_nn(w_query_ref[...], query_back[...]) + dot_nn(w_keyval_ref[...], keyval_back[...])
    gain_grad_ref[...] = as_row(jnp.sum(back * normed, axis=1, keepdims=True))
    normed_back = back * as_column(gain_ref[...])
    mean = jnp.mean(normed_back * normed, axis=0, keepdims=True)
    input_back_ref[...] = (
        middle_back_ref[...] + scale * (normed_back - normed * mean)
    ).astype(bf16)


def closed(spot, mine, other, inputs, middle_back, w_query, w_keyval, gain):
    width, rows = inputs.shape
    inner = w_query.shape[1]
    operands = (mine, other, inputs, middle_back, w_query, w_keyval, gain)
    return pl.pallas_call(
        close_kernel,
        grid_spec=pltpu.PrefetchScalarGridSpec(
            num_scalar_prefetch=1,
            grid=(1,),
            in_specs=[whole(value.shape) for value in operands],
            out_specs=[whole((width, rows)), whole((1, width))],
            scratch_shapes=[
                pltpu.VMEM((inner, rows), bf16),
                pltpu.VMEM((2 * inner, rows), bf16),
            ],
        ),
        out_shape=[
            jax.ShapeDtypeStruct((width, rows), bf16),
            jax.ShapeDtypeStruct((1, width), f32),
        ],
        compiler_params=params(),
        cost_estimate=lasting(18),
    )(spot, *operands)


def swapped(value, axis, bit):
    size = lax.axis_size(axis)
    return lax.ppermute(value, axis, [(i, i ^ bit) for i in range(size)])


def passed_along(value, axis, by):
    size = lax.axis_size(axis)
    pairs = [(i, i + by) for i in range(size) if 0 <= i + by < size]
    return lax.ppermute(value, axis, pairs)


def of_both(value, bit):
    size = lax.axis_size("seq")
    groups = [[i, i | bit] for i in range(size) if not i & bit]
    return lax.all_gather(value, "seq", axis=0, tiled=True, axis_index_groups=groups)


def chosen(value, dim, index):
    return lax.dynamic_index_in_dim(value, index, dim, keepdims=False)


def added(left, right):
    return (left.astype(f32) + right.astype(f32)).astype(bf16)


def parted(state, dims, bit):
    left, right = state
    dim = dims.index(bit)
    mine = (lax.axis_index("seq") // bit) % 2
    kept = added(chosen(left, dim, mine), chosen(right, dim, mine))
    sent = added(chosen(left, dim, 1 - mine), chosen(right, dim, 1 - mine))
    return kept, sent, dims[:dim] + dims[dim + 1 :]


def after(value, *others):
    return lax.optimization_barrier((value, *others))[0]


class Halving:
    def __init__(self, state, dims, order):
        self.kept, self.got = state
        self.dims, self.order = dims, list(order)

    def step(self, earlier):
        bit = self.order.pop(0)
        got = after(self.got, earlier)
        self.kept, sent, self.dims = parted((self.kept, got), self.dims, bit)
        self.got = swapped(sent, "seq", bit)
        return sent

    def total(self, dtype=bf16):
        return (self.kept.astype(f32) + self.got.astype(f32)).astype(dtype)


def on_device(
    tokens,
    cotangent,
    item_lengths,
    gain_attn,
    gain_ffn,
    rel_table,
    w_query,
    w_keyval,
    w_out,
    w_gateup,
    w_down,
):
    rows = tokens.shape[1]
    width = tokens.shape[2]
    part = width // 2
    inner = w_query.shape[1]
    blocks = lax.axis_size("seq")
    me = lax.axis_index("seq")
    core = lax.axis_index("dp").astype(jnp.int32)
    top, pair, third = blocks // 2, blocks // 4, blocks // 8
    low = [1 << i for i in range(blocks.bit_length() - 1)][:-2]

    inputs = tokens[0].T
    cotangent = cotangent[0].T
    w_out = w_out.T
    w_down = w_down.T
    gain_attn = gain_attn[None]
    gain_ffn = gain_ffn[None]

    def bit_of(bit):
        return ((me // bit) % 2).astype(jnp.int32)

    side = bit_of(1)
    half = bit_of(pair)
    down_half = bit_of(third)

    hidden_one, mine, other = opened(side[None], inputs, gain_attn, w_query, w_keyval)
    got = swapped(other, "seq", 1)
    blocks_here = me - side + jnp.arange(2, dtype=jnp.int32)
    ends = jnp.cumsum(item_lengths[0])
    own = jnp.sum((ends[None, :] <= blocks_here[:, None]).astype(jnp.int32), 1)
    labels = jnp.arange(item_lengths.shape[1], dtype=jnp.int32)
    mark = labels[None, :] == own[:, None]
    length = jnp.sum(jnp.where(mark, item_lengths[0][None, :], 0), 1)
    end = jnp.sum(jnp.where(mark, ends[None, :], 0), 1)
    place = jnp.concatenate([blocks_here - (end - length), length, side[None]]).astype(jnp.int32)
    keys = ITEM_MOST * rows
    turns = keys + rows
    shift = jnp.arange(turns, dtype=jnp.int32)
    relative = jnp.where(shift < keys, shift, shift - turns)[None, :] - place[:2, None] * rows
    onehot = (
        bucket_of(relative)[:, :, None] == jnp.arange(BUCKETS, dtype=jnp.int32)[None, None, :]
    ).astype(f32)
    table = jnp.where(
        side == 0,
        rel_table[:, :3],
        jnp.concatenate([rel_table[:, 4:6], rel_table[:, 3:4]], 1),
    )
    by_shift = jnp.sum(onehot[:, None] * table.T[None, :, None, :], -1)
    bias = window_bias(place, by_shift, rows)

    got = after(got, bias)
    keyvals, first, second = paired(side[None], mine, got)
    pieces = [
        passed_along(second, "seq", 4),
        passed_along(keyvals, "seq", 2),
        keyvals,
        passed_along(keyvals, "seq", -2),
        passed_along(first, "seq", -4),
    ]

    attended, attended_other, prob, window = attend(place, mine, got, pieces, bias)
    attended_got = swapped(attended_other, "seq", 1)
    upstream = turned_rows(after(cotangent, attended))
    middle, hidden_two = middle_part(
        side[None], attended, attended_got, inputs, w_out, gain_ffn
    )
    hidden_far = swapped(hidden_two, "seq", pair)
    hidden_got = swapped(hidden_two, "seq", 1)
    hidden_far_got = swapped(hidden_far, "seq", 1)
    upstream_far = swapped(upstream, "seq", third)
    hidden_one_far = swapped(hidden_one, "seq", 1)

    mixed_first, back_first, *sums = ffn_half(
        False, jnp.stack([side, 1 - half]), hidden_two, upstream, w_gateup, w_down
    )
    back_far = swapped(back_first, "seq", pair)
    sums = after(tuple(sums), hidden_far, upstream_far, hidden_got)
    mixed_second, back, output, gain_ffn_grad, middle_back, branch, back_mine, back_other = ffn_half(
        True,
        jnp.stack([side, half]),
        hidden_two,
        upstream,
        w_gateup,
        w_down,
        (*sums, middle, gain_ffn, w_out, cotangent),
    )
    same = half == down_half
    mixed_far = swapped(jnp.where(same, mixed_first, mixed_second), "seq", third)
    back_got = swapped(back_other, "seq", 1)
    branch_far = swapped(after(branch, back_got), "seq", 1)
    back_mine = after(back_mine, hidden_one_far, hidden_far_got)

    backs = attend_back(place, mine, got, window, prob, back_mine, back_got)
    query_back, shift_sums = backs[:2]
    sends = backs[2:]

    def over_dp(kept, sent, dims):
        got = swapped(sent, "dp", 1)
        return tuple(
            value.reshape((2,) * dims + (value.shape[0] >> dims, value.shape[1]))
            for value in (kept, got)
        )

    spot = jnp.stack([core, side])
    units = mixed_first.shape[0]
    owned = units * 4 // blocks
    parts = 2 if owned % 32 == 0 else 1

    def other_owners(value):
        value = value.reshape(2, units // owned // 2, 2, owned, rows)
        return chosen(value, 2, 1 - side).reshape(2, units // 2, rows)

    back_got = swapped(other_owners(back), "seq", 1)
    back_far_sent = other_owners(back_far)
    back_far_got = swapped(back_far_sent, "seq", 1)
    down_kept, down_sent = pair_grad(
        jnp.stack([core, same.astype(jnp.int32)]),
        (2, lambda j: (0, j)),
        units // 2,
        1,
        (after(mixed_second, query_back, back_got, back_far_sent)[None], mixed_first[None]),
        mixed_far[None],
        upstream,
        upstream_far,
    )
    down = Halving(
        over_dp(down_kept, down_sent, len(low) + 1),
        [pair, top] + low[-2::-1],
        [pair] + low[-2::-1] + [top],
    )
    sent = down.step(down_kept)
    near_kept, near_sent, *far_grads = quad_grad(
        spot,
        owned,
        parts,
        (after(back, sent), back_far),
        (back_got, back_far_got),
        (hidden_two, hidden_far, hidden_got, hidden_far_got),
    )
    keyval_back, to_close, to_swap = gathered(
        side[None],
        after(sends[2], near_kept),
        passed_along(sends[3], "seq", 2),
        passed_along(sends[1], "seq", -2),
        passed_along(sends[4], "seq", 4),
        passed_along(sends[0], "seq", -4),
        query_back,
    )
    closed_with = swapped(to_swap, "seq", 1)
    gate_dims = [top] + low[:0:-1]
    gate_order = low[:0:-1] + [top]
    near = Halving(over_dp(near_kept, near_sent, len(low)), gate_dims, gate_order)
    far = None
    if parts == 2:
        far = Halving(over_dp(*far_grads, len(low)), gate_dims, gate_order)
    sent = keyval_back
    sent = near.step(sent)
    head_kept, head_sent = heads_grad(
        jnp.stack([core, side]),
        after(keyval_back, sent),
        query_back,
        (attended, attended_other),
        (hidden_one, hidden_one_far),
        (branch, branch_far),
    )
    others = [top, pair] + low[:0:-1]
    count = len(others)
    each = inner // 2

    def by_owner(value):
        def cut(array, bits):
            array = array.reshape((2,) * count + (-1, array.shape[-1]))
            return array.transpose([bits.index(bit) for bit in others] + [count, count + 1])

        asks = [pair] + low[:0:-1] + [top]
        keyvals = [top] + low[:0:-1] + [pair]
        return jnp.concatenate(
            [
                cut(value[:each], asks),
                cut(value[3 * each :], asks),
                cut(value[each : 3 * each], keyvals),
            ],
            -2,
        )

    head = Halving(
        (by_owner(head_kept), by_owner(swapped(head_sent, "dp", 1))),
        others,
        low[1:] + [pair, top],
    )
    sent = head_kept
    sent = far.step(sent) if far else sent
    input_back, gain_attn_grad = closed(
        side[None],
        after(to_close, sent),
        closed_with,
        inputs,
        middle_back,
        w_query,
        w_keyval,
        gain_attn,
    )

    sums = jnp.einsum(
        "pmb,phm->bh", onehot, shift_sums[:, :, 0], precision=lax.Precision.HIGHEST
    )
    nothing = jnp.zeros_like(sums)
    table_local = jnp.where(
        side == 0,
        jnp.concatenate([sums, nothing], 1),
        jnp.concatenate([nothing, sums[:, 2:], sums[:, :2]], 1),
    )
    small = jnp.concatenate(
        [gain_attn_grad.reshape(-1), gain_ffn_grad.reshape(-1), table_local.reshape(-1)]
    )
    taken = small.shape[0]
    small = jnp.pad(small, (0, -taken % 128)).reshape(-1, 128)
    small_got = swapped(small, "dp", 1)
    sent = gain_attn_grad
    small_order = low[::-1] + [pair, top]
    chains = [chain for chain in (near, far, down, head) if chain]
    while any(chain.order for chain in chains) or small_order:
        for chain in chains:
            if chain.order:
                sent = chain.step(sent)
            if small_order and chain in (head, near):
                small = small + after(small_got, sent)
                small_got = swapped(small, "seq", small_order.pop(0))
    small = small + after(small_got, sent)

    turn = [
        (i, (i & ~(top | third)) | (third if i & top else 0) | (top if i & third else 0))
        for i in range(blocks)
    ]
    down_grad = lax.ppermute(down.total(), "seq", turn).astype(f32)[:, :part]
    def exchanged(i, bit):
        return (i & ~(1 | bit)) | (1 if i & bit else 0) | (bit if i & 1 else 0)

    own_rows = inner // blocks
    head_sum = head.total()
    asks = lax.ppermute(
        head_sum[: 2 * own_rows], "seq", [(i, exchanged(i, top)) for i in range(blocks)]
    ).astype(f32)
    query_grad = asks[:own_rows, :part].T
    out_grad = asks[own_rows:, :part]
    keyval_grad = (
        lax.ppermute(
            head_sum[2 * own_rows :], "seq", [(i, exchanged(i, pair)) for i in range(blocks)]
        )
        .astype(f32)[:, :part]
        .T
    )
    gateup_grad = jnp.concatenate([one.total(f32)[:, :part].T for one in (near, far) if one], 1)
    small = small.reshape(-1)
    return (
        output.T[None],
        input_back.T[None],
        small[:width],
        small[width : 2 * width],
        small[2 * width : taken].reshape(BUCKETS, H),
        query_grad,
        keyval_grad,
        out_grad,
        gateup_grad,
        down_grad,
    )


def solution(mesh):
    placed = (
        P("dp", "seq", None),
        P("dp", "seq", None),
        P("dp", None),
        P(),
        P(),
        P(),
        P(),
        P(),
        P(),
        P(),
        P(),
    )
    return jax.shard_map(
        on_device,
        mesh=mesh,
        in_specs=placed,
        out_specs=(
            P("dp", "seq", None),
            P("dp", "seq", None),
            P(),
            P(),
            P(),
            P("dp", "seq"),
            P("dp", "seq"),
            P("seq", "dp"),
            P("dp", "seq"),
            P("seq", "dp"),
        ),
        check_vma=False,
    )
```
